32 devices in a mesh: grp: 2 (over y), blk: 16 (over z, x, core).
Axes of the slice: x: 2, y: 2, z: 4, core: 2. Of those that a mesh axis runs over, the one named last changes fastest.
Arguments:
- inputs: bfloat16 [8192, 768], P(('grp', 'blk')), may hold values from -6 to 6
- first_values: bfloat16 [8192, 384], P(('grp', 'blk')), may hold values from -6 to 6
- spans: int32 [2, 3], P('grp'), may hold values from 0 to 127, as said below
- ln1_gain: float32 [768], replicated, may hold values from 0.1 to 1.9
- ln1_shift: float32 [768], replicated, may hold values from -3 to 3
- w_query: bfloat16 [768, 768], replicated, may hold values from -0.5 to 0.5
- b_query: float32 [768], replicated, may hold values from -3 to 3
- w_key: bfloat16 [768, 768], replicated, may hold values from -0.21875 to 0.21875
- w_value: bfloat16 [768, 384], replicated, may hold values from -0.21875 to 0.21875
- b_value: float32 [384], replicated, may hold values from -3 to 3
- w_out: bfloat16 [768, 768], replicated, may hold values from -0.4375 to 0.4375
- b_out: float32 [768], replicated, may hold values from -3 to 3
- ln2_gain: float32 [768], replicated, may hold values from 0.1 to 1.9
- ln2_shift: float32 [768], replicated, may hold values from -3 to 3
- w_up: bfloat16 [768, 3072], replicated, may hold values from -0.21875 to 0.21875
- b_up: float32 [3072], replicated, may hold values from -3 to 3
- w_down: bfloat16 [3072, 768], replicated, may hold values from -0.109375 to 0.109375
- b_down: float32 [768], replicated, may hold values from -3 to 3
- out_grad: bfloat16 [8192, 768], P(('grp', 'blk')), may hold values from -6 to 6
Outputs:
- result: float32 [8192, 768], P(('grp', 'blk'))
- grad_inputs: float32 [8192, 768], P(('grp', 'blk'))
- grad_first_values: bfloat16 [8192, 384], P(('grp', 'blk'))
- grad_ln1_gain: float32 [768], replicated
- grad_ln1_shift: float32 [768], replicated
- grad_w_query: float32 [768, 768], P('blk')
- grad_b_query: float32 [768], replicated
- grad_w_key: float32 [768, 768], P('blk')
- grad_w_value: float32 [768, 384], P('blk')
- grad_b_value: float32 [384], replicated
- grad_w_out: float32 [768, 768], P('blk')
- grad_b_out: float32 [768], replicated
- grad_ln2_gain: float32 [768], replicated
- grad_ln2_shift: float32 [768], replicated
- grad_w_up: float32 [768, 3072], P('blk')
- grad_b_up: float32 [3072], replicated
- grad_w_down: float32 [3072, 768], P('blk')
- grad_b_down: float32 [768], replicated
The draws below stay inside these ranges and needn't reach their ends.
Inputs may be any that keep to these rules, and one draw needn't show every extreme that they name: `spans`: each column lies in 0 .. 127, so one long document of each group runs from the first device of blk to the last; documents before and after it lie on the end devices.
All inputs are finite; a program needn't handle non-finite values.
Results may differ from the reference program's by a relative error of at most 0.02.
Values may be sent and summed in bfloat16 or wider, within the bound.
A program may use at most 192 MiB of HBM per device.

```python
import math
import jax
import jax.numpy as jnp
from jax import lax

D = 768
HEADS = 12
FF = 3072
TOK_DEV = 256
TOKENS = 8192
N_GRP = 2


def draw_spans(key, part):
    key = jax.random.fold_in(key, 7)
    half_rows = TOK_DEV // 2
    drawn = jax.random.randint(key, (N_GRP, 3), 0, half_rows, dtype=jnp.int32)
    return drawn.at[0, 0].set(0).at[0, 2].set(half_rows - 1)


def levels(rng, dims, split, low, top_value):
    def one(dim, shards_of):
        draws = jax.random.uniform(jax.random.fold_in(jax.random.fold_in(rng, 6), dim), (shards_of,), jnp.float32, low / len(split), top_value / len(split))
        return jnp.repeat(jnp.exp(draws), dims[dim] // shards_of).reshape((-1,) + (1,) * (len(dims) - dim - 1))

    gain = one(*split[0])
    for cut in split[1:]:
        gain = gain * one(*cut)
    return gain


def scatter_about(key, dims, deviation, limit, cuts=(), held_as=jnp.bfloat16):
    loudness = levels(key, dims, cuts, -0.22, 0.18) if cuts else 1.0
    array = jax.random.normal(key, dims, jnp.float32) * deviation * loudness
    return jnp.minimum(jnp.maximum(array, -limit), limit).astype(held_as)


def setup_inputs(seed: int = 0) -> dict:
    streams_of = jax.random.split(jax.random.key(seed), 20)
    inputs = scatter_about(streams_of[0], (TOKENS, D), 1.0, 6.0, ((0, 32),))
    first_values = scatter_about(streams_of[1], (TOKENS, D // 2), 1.0, 6.0, ((0, 32),))
    spans = draw_spans(jax.random.fold_in(streams_of[19], 71), 0)
    ln1_gain = jnp.clip(1.0 + 0.18 * jax.random.normal(streams_of[3], (D,), jnp.float32), 0.1, 1.9)
    ln1_shift = scatter_about(streams_of[4], (D,), 0.5, 3.0, (), jnp.float32)
    w_query = scatter_about(streams_of[5], (D, D), (D // 6) ** -0.5, 0.5)
    b_query = scatter_about(streams_of[6], (D,), 0.5, 3.0, (), jnp.float32)
    w_key = scatter_about(streams_of[7], (D, D), D ** -0.5, 0.21875)
    w_value = scatter_about(streams_of[8], (D, D // 2), D ** -0.5, 0.21875)
    b_value = scatter_about(streams_of[9], (D // 2,), 0.5, 3.0, (), jnp.float32)
    w_out = scatter_about(streams_of[10], (D, D), (D // 4) ** -0.5, 0.4375)
    b_out = scatter_about(streams_of[11], (D,), 0.5, 3.0, (), jnp.float32)
    ln2_gain = jnp.clip(1.0 + 0.18 * jax.random.normal(streams_of[12], (D,), jnp.float32), 0.1, 1.9)
    ln2_shift = scatter_about(streams_of[13], (D,), 0.5, 3.0, (), jnp.float32)
    w_up = scatter_about(streams_of[14], (D, FF), D ** -0.5, 0.21875)
    b_up = scatter_about(streams_of[15], (FF,), 0.5, 3.0, (), jnp.float32)
    w_down = scatter_about(streams_of[16], (FF, D), FF ** -0.5, 0.109375)
    b_down = scatter_about(streams_of[17], (D,), 0.5, 3.0, (), jnp.float32)
    out_grad = scatter_about(streams_of[18], (TOKENS, D), 1.0, 6.0, ((0, 32),))
    return dict(inputs=inputs, first_values=first_values, spans=spans, ln1_gain=ln1_gain, ln1_shift=ln1_shift, w_query=w_query, b_query=b_query, w_key=w_key, w_value=w_value, b_value=b_value, w_out=w_out, b_out=b_out, ln2_gain=ln2_gain, ln2_shift=ln2_shift, w_up=w_up, b_up=b_up, w_down=w_down, b_down=b_down, out_grad=out_grad)


EPSILON = 1e-05
GELU_COEF = 0.7978845608028654
HIGHEST = lax.Precision.HIGHEST

@jax.custom_vjp
def low(v):
    return lax.optimization_barrier(v.astype(jnp.bfloat16)).astype(jnp.float32)

@jax.custom_vjp
def low_back(v):
    return v

def low_keep(v):
    return (low(v), None)

def low_pass(kept, grad):
    return (grad,)

def back_keep(v):
    return (v, None)

def back_low(kept, grad):
    return (low(grad),)
low.defvjp(low_keep, low_pass)
low_back.defvjp(back_keep, back_low)

def layer_norm(values, gain_vector, shift_vector):
    average = lax.optimization_barrier(jnp.mean(values, axis=-1, keepdims=True))
    centred = values - average
    variance = lax.optimization_barrier(jnp.mean(centred * centred, axis=-1, keepdims=True))
    return centred * lax.rsqrt(variance + EPSILON) * gain_vector + shift_vector

def gelu_tanh(values):
    return 0.5 * values * (1.0 + jnp.tanh(GELU_COEF * (values + 0.044715 * values * values * values)))

def group_bounds(spans_row, length):
    long_end = length - spans_row[1]
    return (spans_row[0], long_end, long_end - spans_row[2])

def key_alive(key_pos, bounds):
    return (key_pos < bounds[2]) | (key_pos >= bounds[1])

def allowed_mask(query_pos, key_pos, bounds):
    query_doc = (query_pos >= bounds[0]).astype(jnp.int32) + (query_pos >= bounds[1]).astype(jnp.int32)
    key_doc = (key_pos >= bounds[0]).astype(jnp.int32) + (key_pos >= bounds[1]).astype(jnp.int32)
    same_doc = query_doc[:, None] == key_doc[None, :]
    causal = key_pos[None, :] <= query_pos[:, None]
    return same_doc & causal & key_alive(key_pos, bounds)[None, :]

def group_forward(inputs, first_values, weights_all, bounds):
    ln1_gain, ln1_shift, w_query, b_query, w_key, w_value, b_value, w_out, b_out, ln2_gain, ln2_shift, w_up, b_up, w_down, b_down = weights_all
    length = inputs.shape[0]
    model_width = inputs.shape[1]
    head_size = model_width // HEADS
    normed = low(layer_norm(inputs, ln1_gain, ln1_shift))
    query_all = low(low_back((jnp.dot(normed, w_query, precision=HIGHEST) + b_query) * 0.125))
    key_all = low(low_back(jnp.dot(normed, w_key, precision=HIGHEST)))
    fresh_values = jnp.dot(normed, w_value, precision=HIGHEST) + b_value
    value_all = low(low_back(jnp.concatenate([fresh_values, first_values], axis=1)))
    positions = jnp.arange(length, dtype=jnp.int32)
    key_heads = key_all.reshape(length, HEADS, head_size)
    value_heads = value_all.reshape(length, HEADS, head_size)
    block_rows = math.gcd(length, 512)
    block_count = length // block_rows

    def attend(block_args):
        query_block, query_pos = block_args
        scores = low_back(jnp.einsum('qhd,khd->hqk', query_block, key_heads, precision=HIGHEST))
        allowed = allowed_mask(query_pos, positions, bounds)[None]
        masked = jnp.where(allowed, scores, -1e+30)
        row_max = lax.optimization_barrier(jnp.max(masked, axis=-1, keepdims=True))
        unscaled = jnp.where(allowed, jnp.exp(masked - row_max), 0.0)
        row_total = lax.optimization_barrier(jnp.sum(unscaled, axis=-1))
        combined = jnp.einsum('hqk,khd->qhd', low(unscaled), value_heads, precision=HIGHEST)
        return (combined / jnp.transpose(row_total)[:, :, None]).reshape(block_rows, model_width)
    query_blocks = query_all.reshape(block_count, block_rows, HEADS, head_size)
    pos_blocks = positions.reshape(block_count, block_rows)
    mixed_all = lax.map(jax.checkpoint(attend), (query_blocks, pos_blocks)).reshape(length, model_width)
    attended = low(low_back(mixed_all))
    branch = low_back(jnp.dot(attended, w_out, precision=HIGHEST) + b_out)
    hidden = inputs + branch
    normed2 = low(layer_norm(hidden, ln2_gain, ln2_shift))
    upper = low_back(jnp.dot(normed2, w_up, precision=HIGHEST) + b_up)
    active = low(gelu_tanh(upper))
    return hidden + jnp.dot(active, w_down, precision=HIGHEST) + b_down

def reference(inputs, first_values, spans, ln1_gain, ln1_shift, w_query, b_query, w_key, w_value, b_value, w_out, b_out, ln2_gain, ln2_shift, w_up, b_up, w_down, b_down, out_grad):
    group_count = spans.shape[0]
    length = inputs.shape[0] // group_count
    weights_all = tuple((item.astype(jnp.float32) for item in (ln1_gain, ln1_shift, w_query, b_query, w_key, w_value, b_value, w_out, b_out, ln2_gain, ln2_shift, w_up, b_up, w_down, b_down)))
    result_parts = []
    input_parts = []
    value_parts = []
    grad_totals = None
    for group_index in range(group_count):
        row_start = group_index * length
        bounds = group_bounds(spans[group_index], length)
        positions = jnp.arange(length, dtype=jnp.int32)
        alive = key_alive(positions, bounds).astype(jnp.float32)

        def forward(inputs_f, first_f, weights_f):
            return group_forward(inputs_f, first_f, weights_f, bounds)
        group_inputs = inputs[row_start:row_start + length].astype(jnp.float32)
        group_first = first_values[row_start:row_start + length].astype(jnp.float32)
        output_rows, pullback = jax.vjp(forward, group_inputs, group_first, weights_all)
        cotangent = out_grad[row_start:row_start + length].astype(jnp.float32) * alive[:, None]
        grad_in, grad_first, grad_weights = pullback(cotangent)
        result_parts.append(output_rows)
        input_parts.append(grad_in)
        value_parts.append(grad_first)
        if grad_totals is None:
            grad_totals = grad_weights
        else:
            grad_totals = jax.tree.map(jnp.add, grad_totals, grad_weights)
    result_all = jnp.concatenate(result_parts, axis=0)
    input_all = jnp.concatenate(input_parts, axis=0)
    value_all = jnp.concatenate(value_parts, axis=0).astype(jnp.bfloat16)
    return (result_all, input_all, value_all, grad_totals[0], grad_totals[1], grad_totals[2], grad_totals[3], grad_totals[4], grad_totals[5], grad_totals[6], grad_totals[7], grad_totals[8], grad_totals[9], grad_totals[10], grad_totals[11], grad_totals[12], grad_totals[13], grad_totals[14])
```

```python
import functools

import jax
import jax.numpy as jnp
from jax import lax
from jax.experimental import pallas as pl
from jax.experimental.pallas import tpu as pltpu
from jax.sharding import PartitionSpec as P

HEADS = 12
PLANES = 4
SLOTS = HEADS // PLANES
EPSILON = 1e-05
GELU_COEF = 0.7978845608028654
NEG_FILL = -1e30
BF16 = jnp.bfloat16
F32 = jnp.float32
MESH = pl.DeviceIdType.MESH
VMEM = pl.BlockSpec(memory_space=pltpu.VMEM)
SMEM = pl.BlockSpec(memory_space=pltpu.SMEM)


def dot(a, b, dims):
    return lax.dot_general(a, b, (dims, ((), ())), preferred_element_type=F32)


NN = ((1,), (0,))
NT = ((1,), (1,))
TN = ((0,), (0,))


def norm_rows(values, gain, shift):
    average = jnp.mean(values, axis=-1, keepdims=True)
    centred = values - average
    variance = jnp.mean(centred * centred, axis=-1, keepdims=True)
    return centred * lax.rsqrt(variance + EPSILON) * gain + shift


def place(plane):
    block = lax.axis_index("blk")
    return block // plane, lax.rem(block, plane)


def at_z(z, c, plane, offset):
    return {"blk": lax.rem(z + offset, PLANES) * plane + c}


def at_x(z, c, plane, offset):
    lines = plane // 2
    column, core = c // 2, lax.rem(c, 2)
    return {"blk": z * plane + lax.rem(column + offset, lines) * 2 + core}


def at_core(z, c, plane):
    return {"blk": z * plane + (c // 2) * 2 + 1 - lax.rem(c, 2)}


def greet(partners):
    barrier = pltpu.get_barrier_semaphore()
    for partner in partners:
        pl.semaphore_signal(barrier, inc=1, device_id=partner, device_id_type=MESH)
    pl.semaphore_wait(barrier, len(partners))


def remote(src, dst, send, recv, partner):
    return pltpu.make_async_remote_copy(
        src_ref=src, dst_ref=dst, send_sem=send, recv_sem=recv,
        device_id=partner, device_id_type=MESH,
    )


def query_rows(pack, first):
    half = pack.shape[1] // 2
    lanes = lax.broadcasted_iota(jnp.int32, pack.shape, 1)
    wide = pack.astype(F32)
    other = pltpu.roll(wide, half, 1)
    keep = lanes < half if first else lanes >= half
    top, bottom = (wide, other) if first else (other, wide)
    return jnp.concatenate(
        [jnp.where(keep, top, 0.0), jnp.where(keep, bottom, 0.0)], axis=0
    ).astype(BF16)


def position_masks(spans_ref, plane, length, c, k, rows):
    first, end = spans_ref[0, 0], length - spans_ref[0, 1]
    dead = end - spans_ref[0, 2]
    width = plane * rows
    key = k * width + lax.broadcasted_iota(jnp.int32, (width, rows), 0)
    query = k * width + c * rows + lax.broadcasted_iota(jnp.int32, (width, rows), 1)
    allowed = key <= query
    if k == 0:
        allowed &= ((key >= first) == (query >= first))
    if k == PLANES - 1:
        allowed &= ((key >= end) == (query >= end)) & ((key < dead) | (key >= end))
    return jnp.where(allowed, 0.0, NEG_FILL)


def forward_kernel(
    plane, x_ref, fv_ref, spans_ref, g_ref, s_ref, wq_ref, bq_ref, wk_ref, wv_ref, bv_ref,
    att_ref, normed_ref, all_ref, o_ref, lse_ref,
    pack, opack, orecv, masks,
    zsend, zrecv, xsend, xrecv, csend, crecv, osend, orecv_sem,
):
    rows, width = x_ref.shape
    size = width // HEADS
    lines = plane // 2
    length = rows * plane * PLANES
    half = rows // 2
    z, c = place(plane)
    core = lax.rem(c, 2)
    greet(
        [at_z(z, c, plane, d) for d in range(1, PLANES)]
        + [at_x(z, c, plane, d) for d in range(1, lines)]
        + [at_core(z, c, plane)]
    )
    normed = norm_rows(x_ref[...].astype(F32), g_ref[...], s_ref[...]).astype(BF16)
    normed_ref[...] = normed
    query = ((dot(normed, wq_ref[...], NN) + bq_ref[...]) * 0.125)
    key = dot(normed, wk_ref[...], NN)
    fresh = dot(normed, wv_ref[...], NN) + bv_ref[...]
    value = jnp.concatenate([fresh, fv_ref[...].astype(F32)], axis=1)
    for head in range(HEADS):
        to, slot = divmod(head, SLOTS)
        cols = slice(head * size, (head + 1) * size)
        pack[to, slot, :rows, :] = jnp.concatenate(
            [key[:, cols], value[:, cols]], axis=1
        ).astype(BF16)
        pack[to, slot, rows:, :] = jnp.concatenate(
            [query[:half, cols], query[half:, cols]], axis=1
        ).astype(BF16)

    zcopies = {}
    for slot in range(SLOTS):
        for d in (2, 1, 3):
            to = lax.rem(z + d, PLANES)
            copy = remote(
                pack.at[to, slot], all_ref.at[slot, z, c],
                zsend.at[slot, d], zrecv.at[slot, d], at_z(z, c, plane, d),
            )
            copy.start()
            zcopies[slot, d] = copy
        all_ref[slot, z, c] = pack[z, slot]

    for k in range(PLANES):
        masks[k] = position_masks(spans_ref, plane, length, c, k, rows)
    first, end = spans_ref[0, 0], length - spans_ref[0, 1]

    started = []

    def spread(slot):
        for d in (0, 1, 3, 2):
            src = lax.rem(z + PLANES - d, PLANES)
            if d:
                zcopies[slot, d].wait_recv()
            block = all_ref.at[slot, src, c, pl.ds(0, rows)]
            for e in range(1, lines):
                copy = remote(
                    block, block, xsend.at[slot, d, e], xrecv.at[slot, d, e], at_x(z, c, plane, e)
                )
                copy.start()
                started.append(copy)
            copy = remote(block, block, csend.at[slot, d, 0], crecv.at[slot, d, 0], at_core(z, c, plane))
            copy.start()
            started.append(copy)

    def pass_on(slot):
        for d in (0, 1, 3, 2):
            src = lax.rem(z + PLANES - d, PLANES)
            for e in range(1, lines):
                column = lax.rem(c // 2 + lines - e, lines) * 2 + core
                block = all_ref.at[slot, src, column, pl.ds(0, rows)]
                remote(
                    block, block, xsend.at[slot, d, e], xrecv.at[slot, d, e], at_x(z, c, plane, e)
                ).wait_recv()
                copy = remote(
                    block, block, csend.at[slot, d, e], crecv.at[slot, d, e], at_core(z, c, plane)
                )
                copy.start()
                started.append(copy)

    def settle(slot):
        for d in range(PLANES):
            for e in range(lines):
                block = all_ref.at[slot, 0, c, pl.ds(0, rows)]
                remote(
                    block, block, csend.at[slot, d, e], crecv.at[slot, d, e], at_core(z, c, plane)
                ).wait_recv()

    def keys_of(slot, k):
        return all_ref[slot, k, :, :rows, :].reshape(plane * rows, 2 * size)

    def attend(slot, k):
        q = query_rows(all_ref[slot, k, c, rows:, :], True)

        def step(state, k2, bias):
            top, total, acc = state
            keys = keys_of(slot, k2)
            scores = bias(dot(keys, q, NT))
            new = jnp.maximum(top, jnp.max(scores, axis=0, keepdims=True))
            prob = jnp.exp(scores - new)
            scale = jnp.exp(top - new)
            return (
                new,
                total * scale + jnp.sum(prob, axis=0, keepdims=True),
                acc * scale + dot(keys, prob.astype(BF16), TN),
            )

        state = (
            jnp.full((1, rows), NEG_FILL, F32),
            jnp.zeros((1, rows), F32),
            jnp.zeros((2 * size, rows), F32),
        )
        state = step(state, k, lambda t: t + masks[k])
        diagonal = state
        for k2 in range(k):
            if k2 == 0:
                index = lax.broadcasted_iota(jnp.int32, (plane * rows, 1), 0)
                shut = jnp.where(index < first, NEG_FILL, 0.0)
                state = step(state, k2, lambda t: t + shut)
            else:
                state = step(state, k2, lambda t: t)
        if k == PLANES - 1:
            position = k * plane * rows + c * rows + lax.broadcasted_iota(jnp.int32, (1, rows), 1)
            after = position >= end
            state = tuple(jnp.where(after, old, new) for old, new in zip(diagonal, state))
        top, total, acc = state
        mixed = acc[size:] / total
        o_ref[slot, k] = mixed
        lse_ref[slot, k] = jnp.broadcast_to(top + jnp.log(total), (8, rows))
        packed = jnp.concatenate([mixed[:, :half], mixed[:, half:]], axis=0)
        opack[slot, k] = jnp.transpose(packed).astype(BF16)

    def give_back(slot):
        orecv[slot, z] = opack[slot, z]
        for d in (2, 1, 3):
            to = lax.rem(z + d, PLANES)
            copy = remote(
                opack.at[slot, to], orecv.at[slot, z],
                osend.at[slot, d], orecv_sem.at[slot, d], at_z(z, c, plane, d),
            )
            copy.start()
            started.append(copy)

    spread(0)
    pass_on(0)
    for slot in range(SLOTS):
        settle(slot)
        for k in range(PLANES):
            attend(slot, k)
            if slot + 1 < SLOTS:
                if k == 1:
                    spread(slot + 1)
                if k == 3:
                    pass_on(slot + 1)
        give_back(slot)
    for slot in range(SLOTS):
        for d in range(1, PLANES):
            remote(
                opack.at[slot, 0], orecv.at[slot, 0],
                osend.at[slot, d], orecv_sem.at[slot, d], at_z(z, c, plane, d),
            ).wait_recv()
    for pair in range(HEADS // 2):
        parts = []
        for head in (2 * pair, 2 * pair + 1):
            src, slot = divmod(head, SLOTS)
            got = orecv[slot, src].astype(F32)
            parts.append(jnp.concatenate([got[:, :size], got[:, size:]], axis=0))
        att_ref[:, pair * 2 * size : (pair + 1) * 2 * size] = jnp.concatenate(parts, axis=1).astype(BF16)
    for copy in list(zcopies.values()) + started:
        copy.wait_send()


def forward_part(inputs, first_values, spans, ln1_gain, ln1_shift, w_query, b_query, w_key, w_value, b_value):
    rows, width = inputs.shape
    plane = lax.axis_size("blk") // PLANES
    lines = plane // 2
    size = width // HEADS
    half = rows // 2
    dma = pltpu.SemaphoreType.DMA
    return pl.pallas_call(
        functools.partial(forward_kernel, plane),
        name="forward",
        out_shape=(
            jax.ShapeDtypeStruct((rows, width), BF16),
            jax.ShapeDtypeStruct((rows, width), BF16),
            jax.ShapeDtypeStruct((SLOTS, PLANES, plane, rows + half, 2 * size), BF16),
            jax.ShapeDtypeStruct((SLOTS, PLANES, size, rows), F32),
            jax.ShapeDtypeStruct((SLOTS, PLANES, 8, rows), F32),
        ),
        in_specs=[VMEM, VMEM, SMEM] + [VMEM] * 7,
        out_specs=(VMEM,) * 5,
        scratch_shapes=[
            pltpu.VMEM((PLANES, SLOTS, rows + half, 2 * size), BF16),
            pltpu.VMEM((SLOTS, PLANES, half, 2 * size), BF16),
            pltpu.VMEM((SLOTS, PLANES, half, 2 * size), BF16),
            pltpu.VMEM((PLANES, plane * rows, rows), F32),
            dma((SLOTS, PLANES)), dma((SLOTS, PLANES)),
            dma((SLOTS, PLANES, lines)), dma((SLOTS, PLANES, lines)),
            dma((SLOTS, PLANES, lines)), dma((SLOTS, PLANES, lines)),
            dma((SLOTS, PLANES)), dma((SLOTS, PLANES)),
        ],
        compiler_params=pltpu.CompilerParams(
            collective_id=1, has_side_effects=True, vmem_limit_bytes=56 << 20
        ),
    )(
        inputs, first_values, spans, ln1_gain.reshape(1, -1), ln1_shift.reshape(1, -1),
        w_query, b_query.reshape(1, -1), w_key, w_value, b_value.reshape(1, -1),
    )


def layer_norm(values, gain_vector, shift_vector):
    average = jnp.mean(values, axis=-1, keepdims=True)
    centred = values - average
    variance = jnp.mean(centred * centred, axis=-1, keepdims=True)
    return centred * lax.rsqrt(variance + EPSILON) * gain_vector + shift_vector


def gelu_tanh(values):
    return (
        0.5 * values * (1.0 + jnp.tanh(GELU_COEF * (values + 0.044715 * values * values * values)))
    )


def key_alive(key_pos, bounds):
    return (key_pos < bounds[2]) | (key_pos >= bounds[1])


def backward_kernel(
    plane, mg_ref, all_ref, o_ref, lse_ref, spans_ref,
    dq_ref, dk_ref, dv_ref,
    dpack, drecv, masks, acc, part, cgot, xpart, xgot, ret, got,
    zsend, zrecv, csend, crecv, xsend, xrecv, rsend, rrecv,
):
    rows, width = mg_ref.shape
    size = width // HEADS
    lines = plane // 2
    length = rows * plane * PLANES
    half = rows // 2
    z, c = place(plane)
    column, core = c // 2, lax.rem(c, 2)
    greet(
        [at_z(z, c, plane, d) for d in range(1, PLANES)]
        + [at_x(z, c, plane, d) for d in range(1, lines)]
        + [at_core(z, c, plane)]
    )
    started = []
    for slot in range(SLOTS):
        for to in range(PLANES):
            cols = slice((to * SLOTS + slot) * size, (to * SLOTS + slot + 1) * size)
            dpack[to, slot] = jnp.concatenate([mg_ref[:half, cols], mg_ref[half:, cols]], axis=1)
        for d in (2, 1, 3):
            to = lax.rem(z + d, PLANES)
            copy = remote(
                dpack.at[to, slot], drecv.at[slot, z],
                zsend.at[slot, d], zrecv.at[slot, d], at_z(z, c, plane, d),
            )
            copy.start()
            started.append(copy)
        drecv[slot, z] = dpack[z, slot]
    for k in range(PLANES):
        masks[k] = position_masks(spans_ref, plane, length, c, k, rows)
    first, end = spans_ref[0, 0], length - spans_ref[0, 1]

    def arrive(slot):
        for d in range(1, PLANES):
            remote(
                dpack.at[0, slot], drecv.at[slot, z],
                zsend.at[slot, d], zrecv.at[slot, d], at_z(z, c, plane, d),
            ).wait_recv()

    def grads(slot, k):
        query = query_rows(all_ref[slot, k, c, rows:, :], True)
        grad = query_rows(drecv[slot, k], False)
        both = jnp.concatenate([query, grad], axis=0)
        turned = jnp.transpose(drecv[slot, k].astype(F32))
        turned = jnp.concatenate([turned[:size], turned[size:]], axis=1)
        delta = jnp.sum(turned * o_ref[slot, k], axis=0, keepdims=True)
        lse = lse_ref[slot, k, 0:1, :]
        query_grad = jnp.zeros((2 * size, rows), F32)
        for k2 in range(k, -1, -1):
            keys = all_ref[slot, k2, :, :rows, :].reshape(plane * rows, 2 * size)
            scores = dot(keys, query, NT)
            prob_grad = dot(keys, grad, NT)
            level = lse
            if k2 == k:
                scores = scores + masks[k]
            else:
                if k2 == 0:
                    index = lax.broadcasted_iota(jnp.int32, (plane * rows, 1), 0)
                    scores = scores + jnp.where(index < first, NEG_FILL, 0.0)
                if k == PLANES - 1:
                    position = k * plane * rows + c * rows + lax.broadcasted_iota(jnp.int32, (1, rows), 1)
                    level = jnp.where(position >= end, -NEG_FILL, lse)
            prob = jnp.exp(scores - level)
            score_grad = (prob * (prob_grad - delta)).astype(BF16)
            update = dot(jnp.concatenate([score_grad, prob.astype(BF16)], axis=1), both, NN)
            if k2 == k:
                acc[slot, k2] = update
            else:
                acc[slot, k2] += update
            query_grad = query_grad + dot(keys, score_grad, TN)
        packed = jnp.concatenate([query_grad[:size, :half], query_grad[:size, half:]], axis=0)
        ret[k, slot, rows:, :] = jnp.transpose(packed).astype(BF16)

    def mine(slot, k, col):
        return acc[slot, k, pl.ds(col * rows, rows), :]

    def reduce_core(slot):
        for line in range(lines):
            for k in range(PLANES):
                part[slot, line, k] = mine(slot, k, 2 * line + 1 - core).astype(BF16)
            copy = remote(
                part.at[slot, line], cgot.at[slot, line],
                csend.at[slot, line], crecv.at[slot, line], at_core(z, c, plane),
            )
            copy.start()
            started.append(copy)

    def reduce_line(slot):
        for line in range(lines):
            remote(
                part.at[slot, line], cgot.at[slot, line],
                csend.at[slot, line], crecv.at[slot, line], at_core(z, c, plane),
            ).wait_recv()
        for e in range(1, lines):
            line = lax.rem(column + e, lines)
            for k in range(PLANES):
                xpart[slot, e, k] = (
                    mine(slot, k, 2 * line + core) + cgot[slot, line, k].astype(F32)
                ).astype(BF16)
            copy = remote(
                xpart.at[slot, e], xgot.at[slot, e],
                xsend.at[slot, e], xrecv.at[slot, e], at_x(z, c, plane, e),
            )
            copy.start()
            started.append(copy)

    def reduce_end(slot):
        for e in range(1, lines):
            remote(
                xpart.at[slot, e], xgot.at[slot, e],
                xsend.at[slot, e], xrecv.at[slot, e], at_x(z, c, plane, e),
            ).wait_recv()
        for k in range(PLANES):
            total = mine(slot, k, c) + cgot[slot, column, k].astype(F32)
            for e in range(1, lines):
                total = total + xgot[slot, e, k].astype(F32)
            ret[k, slot, :rows, :] = total.astype(BF16)
        for d in (2, 1, 3):
            to = lax.rem(z + d, PLANES)
            copy = remote(
                ret.at[to, slot], got.at[slot, z],
                rsend.at[slot, d], rrecv.at[slot, d], at_z(z, c, plane, d),
            )
            copy.start()
            started.append(copy)
        got[slot, z] = ret[z, slot]

    for slot in range(SLOTS):
        arrive(slot)
        for k in range(PLANES):
            grads(slot, k)
            if slot and k == 1:
                reduce_line(slot - 1)
        if slot:
            reduce_end(slot - 1)
        reduce_core(slot)
    reduce_line(SLOTS - 1)
    reduce_end(SLOTS - 1)
    for slot in range(SLOTS):
        for d in range(1, PLANES):
            remote(
                ret.at[0, slot], got.at[slot, z],
                rsend.at[slot, d], rrecv.at[slot, d], at_z(z, c, plane, d),
            ).wait_recv()
    for pair in range(HEADS // 2):
        cols = slice(pair * 2 * size, (pair + 1) * 2 * size)
        keys, values, queries = [], [], []
        for head in (2 * pair, 2 * pair + 1):
            src, slot = divmod(head, SLOTS)
            block = got[slot, src].astype(F32)
            keys.append(block[:rows, :size])
            values.append(block[:rows, size:])
            queries.append(jnp.concatenate([block[rows:, :size], block[rows:, size:]], axis=0))
        dq_ref[:, cols] = jnp.concatenate(queries, axis=1).astype(BF16)
        dk_ref[:, cols] = jnp.concatenate(keys, axis=1).astype(BF16)
        dv_ref[:, cols] = jnp.concatenate(values, axis=1).astype(BF16)
    for copy in started:
        copy.wait_send()


def backward_part(mixed_grad, all_blocks, mixed, lse, spans):
    rows, width = mixed_grad.shape
    plane = lax.axis_size("blk") // PLANES
    lines = plane // 2
    size = width // HEADS
    half = rows // 2
    dma = pltpu.SemaphoreType.DMA
    return pl.pallas_call(
        functools.partial(backward_kernel, plane),
        name="backward",
        out_shape=(jax.ShapeDtypeStruct((rows, width), BF16),) * 3,
        in_specs=[VMEM, VMEM, VMEM, VMEM, SMEM],
        out_specs=(VMEM,) * 3,
        scratch_shapes=[
            pltpu.VMEM((PLANES, SLOTS, half, 2 * size), BF16),
            pltpu.VMEM((SLOTS, PLANES, half, 2 * size), BF16),
            pltpu.VMEM((PLANES, plane * rows, rows), F32),
            pltpu.VMEM((SLOTS, PLANES, plane * rows, 2 * size), F32),
            pltpu.VMEM((SLOTS, lines, PLANES, rows, 2 * size), BF16),
            pltpu.VMEM((SLOTS, lines, PLANES, rows, 2 * size), BF16),
            pltpu.VMEM((SLOTS, lines, PLANES, rows, 2 * size), BF16),
            pltpu.VMEM((SLOTS, lines, PLANES, rows, 2 * size), BF16),
            pltpu.VMEM((PLANES, SLOTS, rows + half, 2 * size), BF16),
            pltpu.VMEM((SLOTS, PLANES, rows + half, 2 * size), BF16),
            dma((SLOTS, PLANES)), dma((SLOTS, PLANES)),
            dma((SLOTS, lines)), dma((SLOTS, lines)),
            dma((SLOTS, lines)), dma((SLOTS, lines)),
            dma((SLOTS, PLANES)), dma((SLOTS, PLANES)),
        ],
        compiler_params=pltpu.CompilerParams(
            collective_id=2, has_side_effects=True, vmem_limit_bytes=56 << 20
        ),
    )(mixed_grad, all_blocks, mixed, lse, spans)


def body(
    inputs,
    first_values,
    spans,
    ln1_gain,
    ln1_shift,
    w_query,
    b_query,
    w_key,
    w_value,
    b_value,
    w_out,
    b_out,
    ln2_gain,
    ln2_shift,
    w_up,
    b_up,
    w_down,
    b_down,
    out_grad,
):
    row_count = inputs.shape[0]
    model_width = inputs.shape[1]
    half_width = model_width // 2
    block_count = lax.axis_size("blk")
    length = row_count * block_count
    my_index = lax.axis_index("blk")
    start_row = my_index * row_count
    positions = start_row + jnp.arange(row_count, dtype=jnp.int32)
    long_end = length - spans[0, 1]
    bounds = (spans[0, 0], long_end, long_end - spans[0, 2])
    source = inputs.astype(jnp.float32)
    attended_low, normed_low, all_blocks, mixed, lse = forward_part(
        inputs, first_values, spans, ln1_gain, ln1_shift, w_query, b_query, w_key, w_value, b_value
    )
    ln1_back = jax.vjp(layer_norm, source, ln1_gain, ln1_shift)[1]
    hidden = source + jnp.dot(attended_low, w_out, preferred_element_type=jnp.float32) + b_out
    normed2, ln2_back = jax.vjp(layer_norm, hidden, ln2_gain, ln2_shift)
    normed2_low = normed2.astype(jnp.bfloat16)
    upper = jnp.dot(normed2_low, w_up, preferred_element_type=jnp.float32) + b_up
    active, gelu_back = jax.vjp(gelu_tanh, upper)
    active_low = active.astype(jnp.bfloat16)
    result = hidden + jnp.dot(active_low, w_down, preferred_element_type=jnp.float32) + b_down
    alive_rows = key_alive(positions, bounds)
    grad_down = out_grad * alive_rows.astype(jnp.bfloat16)[:, None]
    g_w_down = jnp.einsum("tf,td->fd", active_low, grad_down, preferred_element_type=jnp.float32)
    g_b_down = jnp.sum(grad_down.astype(jnp.float32), axis=0)
    active_grad = jnp.einsum("td,fd->tf", grad_down, w_down, preferred_element_type=jnp.float32)
    upper_grad = gelu_back(active_grad)[0].astype(jnp.bfloat16)
    g_w_up = jnp.einsum("tc,tf->cf", normed2_low, upper_grad, preferred_element_type=jnp.float32)
    g_b_up = jnp.sum(upper_grad.astype(jnp.float32), axis=0)
    normed2_grad = jnp.einsum("tf,cf->tc", upper_grad, w_up, preferred_element_type=jnp.float32)
    hidden_norm_grad, g_ln2_gain, g_ln2_shift = ln2_back(normed2_grad)
    hidden_grad = grad_down.astype(jnp.float32) + hidden_norm_grad
    branch_grad = hidden_grad.astype(jnp.bfloat16)
    g_w_out = jnp.einsum("tc,td->cd", attended_low, branch_grad, preferred_element_type=jnp.float32)
    g_b_out = jnp.sum(branch_grad.astype(jnp.float32), axis=0)
    mixed_grad = jnp.einsum(
        "td,cd->tc", branch_grad, w_out, preferred_element_type=jnp.float32
    ).astype(jnp.bfloat16)
    query_grad, key_grad_low, value_grad_low = backward_part(mixed_grad, all_blocks, mixed, lse, spans)
    scaled_grad = query_grad * jnp.bfloat16(0.125)
    fresh_grad = value_grad_low[:, :half_width]
    grad_first_values = value_grad_low[:, half_width:]
    g_w_query = jnp.einsum("tc,td->cd", normed_low, scaled_grad, preferred_element_type=jnp.float32)
    g_b_query = jnp.sum(scaled_grad.astype(jnp.float32), axis=0)
    g_w_key = jnp.einsum("tc,td->cd", normed_low, key_grad_low, preferred_element_type=jnp.float32)
    g_w_value = jnp.einsum("tc,td->cd", normed_low, fresh_grad, preferred_element_type=jnp.float32)
    g_b_value = jnp.sum(fresh_grad.astype(jnp.float32), axis=0)
    normed_grad = (
        jnp.einsum("td,cd->tc", scaled_grad, w_query, preferred_element_type=jnp.float32)
        + jnp.einsum("td,cd->tc", key_grad_low, w_key, preferred_element_type=jnp.float32)
        + jnp.einsum("td,cd->tc", fresh_grad, w_value, preferred_element_type=jnp.float32)
    )
    source_grad, g_ln1_gain, g_ln1_shift = ln1_back(normed_grad)
    grad_inputs = hidden_grad + source_grad
    vector_parts = (
        g_ln1_gain,
        g_ln1_shift,
        g_b_query,
        g_b_value,
        g_b_out,
        g_ln2_gain,
        g_ln2_shift,
        g_b_up,
        g_b_down,
    )
    vector_total = lax.psum(jnp.concatenate(vector_parts, axis=0), ("grp", "blk"))
    offsets = [0]
    for member in vector_parts:
        offsets.append(offsets[-1] + member.shape[0])
    summed_vectors = [
        vector_total[offsets[place] : offsets[place + 1]] for place in range(len(vector_parts))
    ]
    matrices = (g_w_query, g_w_key, g_w_value, g_w_out, g_w_up, g_w_down)
    shard_sums = (
        lax.psum_scatter(
            matrices[0].astype(jnp.bfloat16), "blk", scatter_dimension=0, tiled=True
        ).astype(jnp.float32),
        lax.psum_scatter(
            matrices[1].astype(jnp.bfloat16), "blk", scatter_dimension=0, tiled=True
        ).astype(jnp.float32),
        lax.psum_scatter(
            matrices[2].astype(jnp.bfloat16), "blk", scatter_dimension=0, tiled=True
        ).astype(jnp.float32),
        lax.psum_scatter(
            matrices[3].astype(jnp.bfloat16), "blk", scatter_dimension=0, tiled=True
        ).astype(jnp.float32),
        lax.psum_scatter(
            matrices[4].astype(jnp.bfloat16), "blk", scatter_dimension=0, tiled=True
        ).astype(jnp.float32),
        lax.psum_scatter(
            matrices[5].astype(jnp.bfloat16), "blk", scatter_dimension=0, tiled=True
        ).astype(jnp.float32),
    )
    shard_sums = (
        lax.psum(shard_sums[0].astype(jnp.bfloat16), "grp").astype(jnp.float32),
        lax.psum(shard_sums[1].astype(jnp.bfloat16), "grp").astype(jnp.float32),
        lax.psum(shard_sums[2].astype(jnp.bfloat16), "grp").astype(jnp.float32),
        lax.psum(shard_sums[3].astype(jnp.bfloat16), "grp").astype(jnp.float32),
        lax.psum(shard_sums[4].astype(jnp.bfloat16), "grp").astype(jnp.float32),
        lax.psum(shard_sums[5].astype(jnp.bfloat16), "grp").astype(jnp.float32),
    )
    return (
        result,
        grad_inputs,
        grad_first_values,
        summed_vectors[0],
        summed_vectors[1],
        shard_sums[0],
        summed_vectors[2],
        shard_sums[1],
        shard_sums[2],
        summed_vectors[3],
        shard_sums[3],
        summed_vectors[4],
        summed_vectors[5],
        summed_vectors[6],
        shard_sums[4],
        summed_vectors[7],
        shard_sums[5],
        summed_vectors[8],
    )


def solution(mesh):
    placed = (
        P(("grp", "blk"), None),
        P(("grp", "blk"), None),
        P("grp", None),
        P(),
        P(),
        P(),
        P(),
        P(),
        P(),
        P(),
        P(),
        P(),
        P(),
        P(),
        P(),
        P(),
        P(),
        P(),
        P(("grp", "blk"), None),
    )
    return jax.shard_map(
        body,
        mesh=mesh,
        in_specs=placed,
        out_specs=(
            P(("grp", "blk"), None),
            P(("grp", "blk"), None),
            P(("grp", "blk"), None),
            P(),
            P(),
            P("blk", None),
            P(),
            P("blk", None),
            P("blk", None),
            P(),
            P("blk", None),
            P(),
            P(),
            P(),
            P("blk", None),
            P(),
            P("blk", None),
            P(),
        ),
        check_vma=False,
    )
```

```python
import functools

import jax
import jax.numpy as jnp
from jax import lax
from jax.experimental import pallas as pl
from jax.experimental.pallas import tpu as pltpu
from jax.sharding import PartitionSpec as P

HEADS = 12
PLANES = 4
SLOTS = HEADS // PLANES
EPSILON = 1e-05
GELU_COEF = 0.7978845608028654
NEG_FILL = -1e30
BF16 = jnp.bfloat16
F32 = jnp.float32
MESH = pl.DeviceIdType.MESH
VMEM = pl.BlockSpec(memory_space=pltpu.VMEM)
SMEM = pl.BlockSpec(memory_space=pltpu.SMEM)


def dot(a, b, dims):
    return lax.dot_general(a, b, (dims, ((), ())), preferred_element_type=F32)


NN = ((1,), (0,))
NT = ((1,), (1,))
TN = ((0,), (0,))


def norm_rows(values, gain, shift):
    average = jnp.mean(values, axis=-1, keepdims=True)
    centred = values - average
    variance = jnp.mean(centred * centred, axis=-1, keepdims=True)
    return centred * lax.rsqrt(variance + EPSILON) * gain + shift


def place(plane):
    block = lax.axis_index("blk")
    return block // plane, lax.rem(block, plane)


def at_z(z, c, plane, offset):
    return {"blk": lax.rem(z + offset, PLANES) * plane + c}


def at_x(z, c, plane, offset):
    lines = plane // 2
    column, core = c // 2, lax.rem(c, 2)
    return {"blk": z * plane + lax.rem(column + offset, lines) * 2 + core}


def at_core(z, c, plane):
    return {"blk": z * plane + (c // 2) * 2 + 1 - lax.rem(c, 2)}


def greet(partners):
    barrier = pltpu.get_barrier_semaphore()
    for partner in partners:
        pl.semaphore_signal(barrier, inc=1, device_id=partner, device_id_type=MESH)
    pl.semaphore_wait(barrier, len(partners))


def remote(src, dst, send, recv, partner):
    return pltpu.make_async_remote_copy(
        src_ref=src, dst_ref=dst, send_sem=send, recv_sem=recv,
        device_id=partner, device_id_type=MESH,
    )


def query_rows(pack, first):
    half = pack.shape[1] // 2
    lanes = lax.broadcasted_iota(jnp.int32, pack.shape, 1)
    wide = pack.astype(F32)
    other = pltpu.roll(wide, half, 1)
    keep = lanes < half if first else lanes >= half
    top, bottom = (wide, other) if first else (other, wide)
    return jnp.concatenate(
        [jnp.where(keep, top, 0.0), jnp.where(keep, bottom, 0.0)], axis=0
    ).astype(BF16)


def position_masks(spans_ref, plane, length, c, k, rows):
    first, end = spans_ref[0, 0], length - spans_ref[0, 1]
    dead = end - spans_ref[0, 2]
    width = plane * rows
    key = k * width + lax.broadcasted_iota(jnp.int32, (width, rows), 0)
    query = k * width + c * rows + lax.broadcasted_iota(jnp.int32, (width, rows), 1)
    allowed = key <= query
    if k == 0:
        allowed &= ((key >= first) == (query >= first))
    if k == PLANES - 1:
        allowed &= ((key >= end) == (query >= end)) & ((key < dead) | (key >= end))
    return jnp.where(allowed, 0.0, NEG_FILL)


def forward_kernel(
    plane, x_ref, fv_ref, spans_ref, g_ref, s_ref, wq_ref, bq_ref, wk_ref, wv_ref, bv_ref,
    att_ref, normed_ref, all_ref, o_ref, lse_ref,
    pack, opack, orecv, masks,
    zsend, zrecv, xsend, xrecv, csend, crecv, osend, orecv_sem,
):
    rows, width = x_ref.shape
    size = width // HEADS
    lines = plane // 2
    length = rows * plane * PLANES
    half = rows // 2
    z, c = place(plane)
    core = lax.rem(c, 2)
    greet(
        [at_z(z, c, plane, d) for d in range(1, PLANES)]
        + [at_x(z, c, plane, d) for d in range(1, lines)]
        + [at_core(z, c, plane)]
    )
    normed = norm_rows(
        x_ref[...].astype(F32), g_ref[...].reshape(1, width), s_ref[...].reshape(1, width)
    ).astype(BF16)
    normed_ref[...] = normed
    query = ((dot(normed, wq_ref[...], NN) + bq_ref[...].reshape(1, width)) * 0.125)
    key = dot(normed, wk_ref[...], NN)
    fresh = dot(normed, wv_ref[...], NN) + bv_ref[...].reshape(1, width // 2)
    value = jnp.concatenate([fresh, fv_ref[...].astype(F32)], axis=1)
    for head in range(HEADS):
        to, slot = divmod(head, SLOTS)
        cols = slice(head * size, (head + 1) * size)
        pack[to, slot, :rows, :] = jnp.concatenate(
            [key[:, cols], value[:, cols]], axis=1
        ).astype(BF16)
        pack[to, slot, rows:, :] = jnp.concatenate(
            [query[:half, cols], query[half:, cols]], axis=1
        ).astype(BF16)

    zcopies = {}
    for slot in range(SLOTS):
        for d in (2, 1, 3):
            to = lax.rem(z + d, PLANES)
            copy = remote(
                pack.at[to, slot], all_ref.at[slot, z, c],
                zsend.at[slot, d], zrecv.at[slot, d], at_z(z, c, plane, d),
            )
            copy.start()
            zcopies[slot, d] = copy
        all_ref[slot, z, c] = pack[z, slot]

    for k in range(PLANES):
        masks[k] = position_masks(spans_ref, plane, length, c, k, rows)
    first, end = spans_ref[0, 0], length - spans_ref[0, 1]

    started = []

    def spread(slot):
        for d in (0, 1, 3, 2):
            src = lax.rem(z + PLANES - d, PLANES)
            if d:
                zcopies[slot, d].wait_recv()
            block = all_ref.at[slot, src, c, pl.ds(0, rows)]
            for e in range(1, lines):
                copy = remote(
                    block, block, xsend.at[slot, d, e], xrecv.at[slot, d, e], at_x(z, c, plane, e)
                )
                copy.start()
                started.append(copy)
            copy = remote(block, block, csend.at[slot, d, 0], crecv.at[slot, d, 0], at_core(z, c, plane))
            copy.start()
            started.append(copy)

    def pass_on(slot):
        for d in (0, 1, 3, 2):
            src = lax.rem(z + PLANES - d, PLANES)
            for e in range(1, lines):
                column = lax.rem(c // 2 + lines - e, lines) * 2 + core
                block = all_ref.at[slot, src, column, pl.ds(0, rows)]
                remote(
                    block, block, xsend.at[slot, d, e], xrecv.at[slot, d, e], at_x(z, c, plane, e)
                ).wait_recv()
                copy = remote(
                    block, block, csend.at[slot, d, e], crecv.at[slot, d, e], at_core(z, c, plane)
                )
                copy.start()
                started.append(copy)

    def settle(slot):
        for d in range(PLANES):
            for e in range(lines):
                block = all_ref.at[slot, 0, c, pl.ds(0, rows)]
                remote(
                    block, block, csend.at[slot, d, e], crecv.at[slot, d, e], at_core(z, c, plane)
                ).wait_recv()

    def keys_of(slot, k):
        return all_ref[slot, k, :, :rows, :].reshape(plane * rows, 2 * size)

    def attend(slot, k):
        q = query_rows(all_ref[slot, k, c, rows:, :], True)

        def step(state, k2, bias):
            top, total, acc = state
            keys = keys_of(slot, k2)
            scores = bias(dot(keys, q, NT))
            new = jnp.maximum(top, jnp.max(scores, axis=0, keepdims=True))
            prob = jnp.exp(scores - new)
            scale = jnp.exp(top - new)
            return (
                new,
                total * scale + jnp.sum(prob, axis=0, keepdims=True),
                acc * scale + dot(keys, prob.astype(BF16), TN),
            )

        state = (
            jnp.full((1, rows), NEG_FILL, F32),
            jnp.zeros((1, rows), F32),
            jnp.zeros((2 * size, rows), F32),
        )
        state = step(state, k, lambda t: t + masks[k])
        diagonal = state
        for k2 in range(k):
            if k2 == 0:
                index = lax.broadcasted_iota(jnp.int32, (plane * rows, 1), 0)
                shut = jnp.where(index < first, NEG_FILL, 0.0)
                state = step(state, k2, lambda t: t + shut)
            else:
                state = step(state, k2, lambda t: t)
        if k == PLANES - 1:
            position = k * plane * rows + c * rows + lax.broadcasted_iota(jnp.int32, (1, rows), 1)
            after = position >= end
            state = tuple(jnp.where(after, old, new) for old, new in zip(diagonal, state))
        top, total, acc = state
        mixed = acc[size:] / total
        o_ref[slot, k] = mixed
        lse_ref[slot, k] = jnp.broadcast_to(top + jnp.log(total), (8, rows))
        packed = jnp.concatenate([mixed[:, :half], mixed[:, half:]], axis=0)
        opack[slot, k] = jnp.transpose(packed).astype(BF16)

    def give_back(slot):
        orecv[slot, z] = opack[slot, z]
        for d in (2, 1, 3):
            to = lax.rem(z + d, PLANES)
            copy = remote(
                opack.at[slot, to], orecv.at[slot, z],
                osend.at[slot, d], orecv_sem.at[slot, d], at_z(z, c, plane, d),
            )
            copy.start()
            started.append(copy)

    spread(0)
    pass_on(0)
    for slot in range(SLOTS):
        settle(slot)
        for k in range(PLANES):
            attend(slot, k)
            if slot + 1 < SLOTS:
                if k == 1:
                    spread(slot + 1)
                if k == 3:
                    pass_on(slot + 1)
        give_back(slot)
    for slot in range(SLOTS):
        for d in range(1, PLANES):
            remote(
                opack.at[slot, 0], orecv.at[slot, 0],
                osend.at[slot, d], orecv_sem.at[slot, d], at_z(z, c, plane, d),
            ).wait_recv()
    for pair in range(HEADS // 2):
        parts = []
        for head in (2 * pair, 2 * pair + 1):
            src, slot = divmod(head, SLOTS)
            got = orecv[slot, src].astype(F32)
            parts.append(jnp.concatenate([got[:, :size], got[:, size:]], axis=0))
        att_ref[:, pair * 2 * size : (pair + 1) * 2 * size] = jnp.concatenate(parts, axis=1).astype(BF16)
    for copy in list(zcopies.values()) + started:
        copy.wait_send()


def forward_part(inputs, first_values, spans, ln1_gain, ln1_shift, w_query, b_query, w_key, w_value, b_value):
    rows, width = inputs.shape
    plane = lax.axis_size("blk") // PLANES
    lines = plane // 2
    size = width // HEADS
    half = rows // 2
    dma = pltpu.SemaphoreType.DMA
    return pl.pallas_call(
        functools.partial(forward_kernel, plane),
        name="forward",
        out_shape=(
            jax.ShapeDtypeStruct((rows, width), BF16),
            jax.ShapeDtypeStruct((rows, width), BF16),
            jax.ShapeDtypeStruct((SLOTS, PLANES, plane, rows + half, 2 * size), BF16),
            jax.ShapeDtypeStruct((SLOTS, PLANES, size, rows), F32),
            jax.ShapeDtypeStruct((SLOTS, PLANES, 8, rows), F32),
        ),
        in_specs=[VMEM, VMEM, SMEM] + [VMEM] * 7,
        out_specs=(VMEM,) * 5,
        scratch_shapes=[
            pltpu.VMEM((PLANES, SLOTS, rows + half, 2 * size), BF16),
            pltpu.VMEM((SLOTS, PLANES, half, 2 * size), BF16),
            pltpu.VMEM((SLOTS, PLANES, half, 2 * size), BF16),
            pltpu.VMEM((PLANES, plane * rows, rows), F32),
            dma((SLOTS, PLANES)), dma((SLOTS, PLANES)),
            dma((SLOTS, PLANES, lines)), dma((SLOTS, PLANES, lines)),
            dma((SLOTS, PLANES, lines)), dma((SLOTS, PLANES, lines)),
            dma((SLOTS, PLANES)), dma((SLOTS, PLANES)),
        ],
        compiler_params=pltpu.CompilerParams(
            collective_id=1, has_side_effects=True, vmem_limit_bytes=56 << 20
        ),
    )(
        inputs, first_values, spans, ln1_gain, ln1_shift, w_query, b_query, w_key, w_value, b_value,
    )


def middle_kernel(
    x_ref, att_ref, normed_ref, spans_ref, og_ref, bo_ref, g_ref, s_ref, bu_ref, bd_ref,
    wo_hbm, wu_hbm, wd_hbm,
    result_ref, mg_ref, hg_ref, branch_ref, ug_ref, dout_ref, vec_ref, lt_a, lt_n2, lt_act, lt_n,
    wo_ref, wu_ref, wd_ref, sem,
):
    rows, width = x_ref.shape
    tall = bu_ref.shape[0] // width
    shard = lt_a.shape[4]
    copies = [
        pltpu.make_async_copy(src, dst, sem.at[i])
        for i, (src, dst) in enumerate(((wo_hbm, wo_ref), (wu_hbm, wu_ref), (wd_hbm, wd_ref)))
    ]
    for copy in copies:
        copy.start()

    def turn(value, dst, piece):
        turned = jnp.transpose(value.astype(F32)).astype(BF16)
        at = 0
        span = width // (dst.shape[0] * dst.shape[1] * 2)
        if dst.shape[3] == 1:
            for zz in range(dst.shape[0]):
                for xx in range(dst.shape[1]):
                    for cc in range(2):
                        dst[zz, xx, cc, 0] = turned[at : at + span]
                        at += span
            return
        per = dst.shape[3]
        for unit in range(width // span):
            index = piece * (width // span) + unit
            owner, part = divmod(index, per)
            chip, cc = divmod(owner, 2)
            zz, xx = divmod(chip, dst.shape[1])
            dst[zz, xx, cc, part] = turned[unit * span : (unit + 1) * span]

    def sums(value):
        return jnp.sum(value.astype(F32), axis=0, keepdims=True)

    block = lax.axis_index("blk")
    length = rows * lax.axis_size("blk")
    end = length - spans_ref[0, 1]
    position = block * rows + lax.broadcasted_iota(jnp.int32, (rows, 1), 0)
    alive = (position < end - spans_ref[0, 2]) | (position >= end)
    dout = jnp.where(alive, og_ref[...].astype(F32), 0.0)
    dout_low = dout.astype(BF16)
    dout_ref[...] = dout_low
    vec_ref[3 + tall : 4 + tall, :] = sums(dout)
    attended = att_ref[...]
    turn(normed_ref[...], lt_n, 0)
    turn(attended, lt_a, 0)
    copies[0].wait()
    hidden = x_ref[...].astype(F32) + dot(attended, wo_ref[...], NN) + bo_ref[...].reshape(1, width)
    average = jnp.mean(hidden, axis=-1, keepdims=True)
    centred = hidden - average
    scale = lax.rsqrt(jnp.mean(centred * centred, axis=-1, keepdims=True) + EPSILON)
    unit = centred * scale
    gain = g_ref[...].reshape(1, width)
    normed2 = (unit * gain + s_ref[...].reshape(1, width)).astype(BF16)
    turn(normed2, lt_n2, 0)
    copies[1].wait()
    copies[2].wait()
    result = hidden + bd_ref[...].reshape(1, width)
    normed2_grad = jnp.zeros((rows, width), F32)
    for i in range(tall):
        cols = slice(i * width, (i + 1) * width)
        upper = dot(normed2, wu_ref[:, cols], NN) + bu_ref[cols].reshape(1, width)
        square = upper * upper
        curve = jnp.tanh(GELU_COEF * (upper + 0.044715 * upper * square))
        half = 0.5 * (1.0 + curve)
        active = (upper * half).astype(BF16)
        slope = half + 0.5 * upper * (1.0 - curve * curve) * (GELU_COEF * (1.0 + 3.0 * 0.044715 * square))
        turn(active, lt_act, i)
        result = result + dot(active, wd_ref[cols, :], NN)
        upper_grad = (dot(dout_low, wd_ref[cols, :], NT) * slope).astype(BF16)
        ug_ref[:, cols] = upper_grad
        vec_ref[3 + i : 4 + i, :] = sums(upper_grad)
        normed2_grad = normed2_grad + dot(upper_grad, wu_ref[:, cols], NT)
    result_ref[...] = result
    vec_ref[0:1, :] = sums(normed2_grad * unit)
    vec_ref[1:2, :] = sums(normed2_grad)
    inner = normed2_grad * gain
    back = scale * (
        inner - jnp.mean(inner, axis=-1, keepdims=True) - unit * jnp.mean(inner * unit, axis=-1, keepdims=True)
    )
    hidden_grad = dout + back
    hg_ref[...] = hidden_grad
    branch = hidden_grad.astype(BF16)
    branch_ref[...] = branch
    vec_ref[2:3, :] = sums(branch)
    mg_ref[...] = dot(branch, wo_ref[...], NT).astype(BF16)


def middle_part(plane, inputs, attended, normed, spans, out_grad, b_out, gain, shift, b_up, b_down, w_out, w_up, w_down):
    rows, width = inputs.shape
    hidden = w_up.shape[1]
    tall = hidden // width
    lines = plane // 2
    shard = width // (plane * PLANES)

    def low(*shape):
        return jax.ShapeDtypeStruct(shape, BF16)

    any_space = pl.BlockSpec(memory_space=pl.ANY)
    return pl.pallas_call(
        middle_kernel,
        name="middle",
        out_shape=(
            jax.ShapeDtypeStruct((rows, width), F32), low(rows, width), jax.ShapeDtypeStruct((rows, width), F32),
            low(rows, width), low(rows, hidden), low(rows, width), jax.ShapeDtypeStruct((4 + tall, width), F32),
            low(PLANES, lines, 2, 1, shard, rows), low(PLANES, lines, 2, 1, shard, rows),
            low(PLANES, lines, 2, tall, shard, rows), low(PLANES, lines, 2, 1, shard, rows),
        ),
        in_specs=[VMEM, VMEM, VMEM, SMEM] + [VMEM] * 6 + [any_space] * 3,
        out_specs=(VMEM,) * 11,
        scratch_shapes=[
            pltpu.VMEM((width, width), BF16), pltpu.VMEM((width, hidden), BF16), pltpu.VMEM((hidden, width), BF16),
            pltpu.SemaphoreType.DMA((3,)),
        ],
        compiler_params=pltpu.CompilerParams(vmem_limit_bytes=56 << 20),
    )(inputs, attended, normed, spans, out_grad, b_out, gain, shift, b_up, b_down, w_out, w_up, w_down)


OUT, UP, DOWN, QUERY, KEY, VALUE = 0, 1, 5, 9, 10, 11
PIECES = 12
LINE_FIRST = frozenset((UP + 1, UP + 3, DOWN + 1, DOWN + 3, KEY))


class Refs(dict):
    __getattr__ = dict.get


def backward_kernel(plane, groups, shard, names, attention, weights, *refs):
    r = Refs(zip(names, refs, strict=True))
    mg_ref, all_ref, o_ref, lse_ref, spans_ref, lt_a, lt_n2, lt_act = r.mg_ref, r.all_ref, r.o_ref, r.lse_ref, r.spans_ref, r.lt_a, r.lt_n2, r.lt_act
    lt_n, branch_ref, ug_ref, dout_ref, vec_ref, x_ref, g_ref, hg_ref = r.lt_n, r.branch_ref, r.ug_ref, r.dout_ref, r.vec_ref, r.x_ref, r.g_ref, r.hg_ref
    wq_ref, wk_ref, wv_ref, late_in, gin_ref, gfv_ref, vec1_ref, vec2_ref = r.wq_ref, r.wk_ref, r.wv_ref, r.late_in, r.gin_ref, r.gfv_ref, r.vec1_ref, r.vec2_ref
    late_out, dpack = r.late_out, r.dpack
    drecv, masks, acc, part, cgot, xpart, xgot, ret = r.drecv, r.masks, r.acc, r.part, r.cgot, r.xpart, r.xgot, r.ret
    got, keybuf, keysem, ltp_a, ltp_n2, ltp_act, ltp_n, rp_branch = r.got, r.keybuf, r.keysem, r.ltp_a, r.ltp_n2, r.ltp_act, r.ltp_n, r.rp_branch
    rp_ug, rp_dout, late_own, rp_late, wbuf, gy, gx, sx = r.rp_ug, r.rp_dout, r.late_own, r.rp_late, r.wbuf, r.gy, r.gx, r.sx
    sy, zs, zg, fin, wbuf_v, gy_v, gx_v, sx_v = r.sy, r.zs, r.zg, r.fin, r.wbuf_v, r.gy_v, r.gx_v, r.sx_v
    sy_v, zs_v, zg_v, fin_v, vbuf_c, vbuf_x, vbuf_y, vbuf_z = r.sy_v, r.zs_v, r.zg_v, r.fin_v, r.vbuf_c, r.vbuf_x, r.vbuf_y, r.vbuf_z
    zsend, zrecv, csend, crecv, xsend, xrecv, rsend, rrecv = r.zsend, r.zrecv, r.csend, r.crecv, r.xsend, r.xrecv, r.rsend, r.rrecv
    esend, erecv, s1send, s1recv, s2send, s2recv, wzsend, wzrecv = r.esend, r.erecv, r.s1send, r.s1recv, r.s2send, r.s2recv, r.wzsend, r.wzrecv
    fsend, frecv, vsend, vrecv = r.fsend, r.frecv, r.vsend, r.vrecv
    late_r = late_own if late_own is not None else (late_out if late_out is not None else late_in)
    rows, width = (mg_ref if attention else x_ref).shape
    size = width // HEADS
    lines = plane // 2
    length = rows * plane * PLANES
    half = rows // 2
    z, c = place(plane)
    column, core = c // 2, lax.rem(c, 2)
    group = lax.axis_index("grp")
    lw = width // groups

    def at_group(offset):
        return {"grp": lax.rem(group + offset, groups)}

    to_core = at_core(z, c, plane)
    greet(
        [at_z(z, c, plane, d) for d in range(1, PLANES)]
        + [at_x(z, c, plane, d) for d in range(1, lines)]
        + [to_core]
        + [at_group(d) for d in range(1, groups) if weights]
    )
    sent = []

    def start(copy):
        copy.start()
        sent.append(copy)

    def dcopy(slot, d):
        return remote(
            dpack.at[lax.rem(z + d, PLANES), slot], drecv.at[slot, z],
            zsend.at[slot, d], zrecv.at[slot, d], at_z(z, c, plane, d),
        )

    def key_copy(slot):
        return pltpu.make_async_copy(all_ref.at[slot], keybuf.at[slot % 2], keysem.at[slot % 2])

    for slot in range(SLOTS if attention else 0):
        if slot < 2:
            key_copy(slot).start()
        for to in range(PLANES):
            cols = slice((to * SLOTS + slot) * size, (to * SLOTS + slot + 1) * size)
            dpack[to, slot] = jnp.concatenate([mg_ref[:half, cols], mg_ref[half:, cols]], axis=1)
        for d in (2, 1, 3):
            start(dcopy(slot, d))
        drecv[slot, z] = dpack[z, slot]

    def arrive(slot):
        for d in range(1, PLANES):
            dcopy(slot, d).wait_recv()

    exchange = {}

    def swap(index, src, dst):
        exchange[index] = remote(src, dst, esend.at[index], erecv.at[index], to_core)
        start(exchange[index])

    def arrived(*indices):
        for index in indices:
            copy = exchange.pop(index, None)
            if copy is not None:
                copy.wait_recv()

    if weights:
        swap(0, lt_a.at[:, :, 1 - core], ltp_a)
        swap(1, branch_ref, rp_branch)
        swap(2, lt_n2.at[:, :, 1 - core], ltp_n2)
        swap(3, ug_ref, rp_ug)
        swap(4, lt_act.at[:, :, 1 - core], ltp_act)
        swap(5, dout_ref, rp_dout)
        swap(6, lt_n.at[:, :, 1 - core], ltp_n)

    if attention:
        for k in range(PLANES):
            masks[k] = position_masks(spans_ref, plane, length, c, k, rows).astype(BF16)
        first, end = spans_ref[0, 0], length - spans_ref[0, 1]

    def vectors(batch, value, result):
        stages = [
            (vbuf_c, core, 2, lambda e: to_core, 0),
            (vbuf_x, column, lines, lambda e: at_x(z, c, plane, e), 1),
            (vbuf_y, group, groups, at_group, 2),
            (vbuf_z, z, PLANES, lambda e: at_z(z, c, plane, e), 3),
        ]

        def copies(stage):
            buf, me, count, partner, axis = stages[stage]
            return [
                remote(
                    buf.at[batch, me], buf.at[batch, me],
                    vsend.at[batch, axis, e], vrecv.at[batch, axis, e], partner(e),
                )
                for e in range(1, count)
            ]

        def step(stage):
            if stage == 0:
                total = value()
            else:
                buf, me, count, partner, axis = stages[stage - 1]
                for copy in copies(stage - 1):
                    copy.wait_recv()
                total = buf[batch, 0]
                for i in range(1, count):
                    total = total + buf[batch, i]
            if stage == len(stages):
                result[...] = total
                return
            buf, me = stages[stage][:2]
            buf[batch, me] = total
            for copy in copies(stage):
                start(copy)

        return step

    early_vectors = vectors(0, lambda: vec_ref[...], vec1_ref)

    def bufs(piece):
        if piece == VALUE:
            return 0, wbuf_v, gy_v, gx_v, sx_v, sy_v, zs_v, zg_v, fin_v
        return piece, wbuf, gy, gx, sx, sy, zs, zg, fin

    def make(piece):
        i, buf = bufs(piece)[:2]
        count = PLANES * lines * shard
        if piece == OUT:
            arrived(0, 1)
            mine, theirs = lt_a[:, :, core, 0], ltp_a[:, :, 0]
            right, other = branch_ref[...], rp_branch[...]
        elif piece < DOWN:
            arrived(2, 3)
            cols = slice((piece - UP) * width, (piece - UP + 1) * width)
            mine, theirs = lt_n2[:, :, core, 0], ltp_n2[:, :, 0]
            right, other = ug_ref[:, cols], rp_ug[:, cols]
        elif piece < QUERY:
            arrived(4, 5)
            mine, theirs = lt_act[:, :, core, piece - DOWN], ltp_act[:, :, piece - DOWN]
            right, other = dout_ref[...], rp_dout[...]
        else:
            arrived(6, 7)
            at = (piece - QUERY) * width
            cols = slice(at, at + (width // 2 if piece == VALUE else width))
            mine, theirs = lt_n[:, :, core, 0], ltp_n[:, :, 0]
            right, other = late_r[:, cols], rp_late[:, cols]
        grad = dot(mine.reshape(count, rows), right, NN) + dot(theirs.reshape(count, rows), other, NN)
        lanes = grad.shape[1] // groups
        for h in range(groups):
            for zz in range(PLANES):
                for xx in range(lines):
                    at = (zz * lines + xx) * shard
                    buf[i, h, xx, zz] = grad[at : at + shard, h * lanes : (h + 1) * lanes].astype(BF16)
        for copy in first_copies(piece):
            start(copy)

    def first_copies(piece):
        i, buf, gy_b, gx_b = bufs(piece)[:4]
        n = piece
        if piece in LINE_FIRST:
            return [
                remote(
                    buf.at[i, :, lax.rem(column + e, lines)], gx_b.at[i, e - 1],
                    s1send.at[n, e], s1recv.at[n, e], at_x(z, c, plane, e),
                )
                for e in range(1, lines)
            ]
        return [
            remote(
                buf.at[i, lax.rem(group + e, groups)], gy_b.at[i, e - 1],
                s1send.at[n, e], s1recv.at[n, e], at_group(e),
            )
            for e in range(1, groups)
        ]

    def second_copies(piece):
        i, buf, gy_b, gx_b, sx_b, sy_b = bufs(piece)[:6]
        n = piece
        if piece in LINE_FIRST:
            return [
                remote(
                    sy_b.at[i, e - 1], gy_b.at[i, e - 1, 0],
                    s2send.at[n, e], s2recv.at[n, e], at_group(e),
                )
                for e in range(1, groups)
            ]
        return [
            remote(
                sx_b.at[i, e - 1], gx_b.at[i, e - 1, 0],
                s2send.at[n, e], s2recv.at[n, e], at_x(z, c, plane, e),
            )
            for e in range(1, lines)
        ]

    def first_total(piece, at):
        i, buf, gy_b, gx_b = bufs(piece)[:4]
        if piece in LINE_FIRST:
            value = buf[i, at, column].astype(F32)
            for e in range(1, lines):
                value = value + gx_b[i, e - 1, at].astype(F32)
            return value
        value = buf[i, group, at].astype(F32)
        for e in range(1, groups):
            value = value + gy_b[i, e - 1, at].astype(F32)
        return value

    def second(piece):
        i, buf, gy_b, gx_b, sx_b, sy_b = bufs(piece)[:6]
        for copy in first_copies(piece):
            copy.wait_recv()
        if piece in LINE_FIRST:
            for e in range(1, groups):
                sy_b[i, e - 1] = first_total(piece, lax.rem(group + e, groups)).astype(BF16)
        else:
            for e in range(1, lines):
                sx_b[i, e - 1] = first_total(piece, lax.rem(column + e, lines)).astype(BF16)
        for copy in second_copies(piece):
            start(copy)

    def third_copies(piece):
        i = bufs(piece)[0]
        zs_b, zg_b = bufs(piece)[6:8]
        n = piece
        return [
            remote(
                zs_b.at[i, lax.rem(z + d, PLANES)], zg_b.at[i, d - 1],
                wzsend.at[n, d], wzrecv.at[n, d], at_z(z, c, plane, d),
            )
            for d in (2, 1, 3)
        ]

    def third(piece):
        i, buf, gy_b, gx_b, sx_b, sy_b, zs_b, zg_b, fin_b = bufs(piece)
        for copy in second_copies(piece):
            copy.wait_recv()
        value = first_total(piece, group if piece in LINE_FIRST else column)
        if piece in LINE_FIRST:
            for e in range(1, groups):
                value = value + gy_b[i, e - 1, 0].astype(F32)
        else:
            for e in range(1, lines):
                value = value + gx_b[i, e - 1, 0].astype(F32)
        zs_b[i] = value.astype(BF16)
        for copy in third_copies(piece):
            start(copy)

    def last_copies(piece):
        i = bufs(piece)[0]
        fin_b = bufs(piece)[8]
        n = piece
        return [
            remote(fin_b.at[i, group], fin_b.at[i, group], fsend.at[n, e], frecv.at[n, e], at_group(e))
            for e in range(1, groups)
        ]

    def fourth(piece):
        i, buf, gy_b, gx_b, sx_b, sy_b, zs_b, zg_b, fin_b = bufs(piece)
        for copy in third_copies(piece):
            copy.wait_recv()
        value = zs_b[i, z].astype(F32)
        for d in range(1, PLANES):
            value = value + zg_b[i, d - 1].astype(F32)
        fin_b[i, group] = value.astype(BF16)
        for copy in last_copies(piece):
            start(copy)

    def finish(piece):
        for copy in last_copies(piece):
            copy.wait_recv()

    span = min(plane, 4)

    def grads(slot, k):
        held = keybuf.at[slot % 2]
        query = query_rows(held[k, c, rows:, :], True)
        grad = query_rows(drecv[slot, k], False)
        both = jnp.concatenate([query, grad], axis=0)
        turned = jnp.transpose(drecv[slot, k].astype(F32))
        turned = jnp.concatenate([turned[:size], turned[size:]], axis=1)
        delta = jnp.sum(turned * o_ref[slot, k], axis=0, keepdims=True)
        lse = lse_ref[slot, k, 0:1, :]
        query_grad = jnp.zeros((2 * size, rows), F32)
        for k2 in range(k, -1, -1):
            level = lse
            if k2 < k and k == PLANES - 1:
                position = k * plane * rows + c * rows + lax.broadcasted_iota(jnp.int32, (1, rows), 1)
                level = jnp.where(position >= end, -NEG_FILL, lse)
            for at in range(0, plane, span):
                where = slice(at * rows, (at + span) * rows)
                keys = held[k2, at : at + span, :rows, :].reshape(span * rows, 2 * size)
                scores = dot(keys, query, NT)
                prob_grad = dot(keys, grad, NT)
                if k2 == k:
                    scores = scores + masks[k, where, :].astype(F32)
                elif k2 == 0 and at == 0:
                    index = lax.broadcasted_iota(jnp.int32, (span * rows, 1), 0)
                    scores = scores + jnp.where(index < first, NEG_FILL, 0.0)
                prob = jnp.exp(scores - level)
                score_grad = (prob * (prob_grad - delta)).astype(BF16)
                update = dot(jnp.concatenate([score_grad, prob.astype(BF16)], axis=1), both, NN)
                if k2 == k:
                    acc[slot % 2, k2, where] = update
                else:
                    acc[slot % 2, k2, where] += update
                query_grad = query_grad + dot(keys, score_grad, TN)
        packed = jnp.concatenate([query_grad[:size, :half], query_grad[:size, half:]], axis=0)
        ret[k, slot, rows:, :] = jnp.transpose(packed).astype(BF16)

    def mine(slot, k, col):
        return acc[slot % 2, k, pl.ds(pl.multiple_of(col * rows, rows), rows), :]

    def ccopy(slot, line):
        return remote(
            part.at[slot, line], cgot.at[slot, line],
            csend.at[slot, line], crecv.at[slot, line], to_core,
        )

    def xcopy(slot, e):
        return remote(
            xpart.at[slot, e - 1], xgot.at[slot, e - 1],
            xsend.at[slot, e], xrecv.at[slot, e], at_x(z, c, plane, e),
        )

    def rcopy(slot, d):
        return remote(
            ret.at[lax.rem(z + d, PLANES), slot], got.at[slot, z],
            rsend.at[slot, d], rrecv.at[slot, d], at_z(z, c, plane, d),
        )

    def reduce_core(slot):
        for line in range(lines):
            for k in range(PLANES):
                part[slot, line, k] = mine(slot, k, 2 * line + 1 - core).astype(BF16)
            start(ccopy(slot, line))

    def reduce_line(slot):
        for line in range(lines):
            ccopy(slot, line).wait_recv()
        for e in range(1, lines):
            line = lax.rem(column + e, lines)
            for k in range(PLANES):
                xpart[slot, e - 1, k] = (
                    mine(slot, k, 2 * line + core) + cgot[slot, line, k].astype(F32)
                ).astype(BF16)
            start(xcopy(slot, e))

    def reduce_end(slot):
        for e in range(1, lines):
            xcopy(slot, e).wait_recv()
        for k in range(PLANES):
            total = mine(slot, k, c) + cgot[slot, column, k].astype(F32)
            for e in range(1, lines):
                total = total + xgot[slot, e - 1, k].astype(F32)
            ret[k, slot, :rows, :] = total.astype(BF16)
        for d in (2, 1, 3):
            start(rcopy(slot, d))
        got[slot, z] = ret[z, slot]

    def late_factors():
        for slot in range(SLOTS):
            for d in range(1, PLANES):
                rcopy(slot, d).wait_recv()
        for pair in range(HEADS // 2):
            at = pair * 2 * size
            keys, values, queries = [], [], []
            for head in (2 * pair, 2 * pair + 1):
                src, slot = divmod(head, SLOTS)
                block = got[slot, src].astype(F32)
                keys.append(block[:rows, :size])
                values.append(block[:rows, size:])
                queries.append(jnp.concatenate([block[rows:, :size], block[rows:, size:]], axis=0))
            late_r[:, at : at + 2 * size] = (jnp.concatenate(queries, axis=1) * 0.125).astype(BF16)
            late_r[:, width + at : width + at + 2 * size] = jnp.concatenate(keys, axis=1).astype(BF16)
            if pair < HEADS // 4:
                at = 2 * width + at
                late_r[:, at : at + 2 * size] = jnp.concatenate(values, axis=1).astype(BF16)
            else:
                at = at - width // 2
                gfv_ref[:, at : at + 2 * size] = jnp.concatenate(values, axis=1).astype(BF16)
    def input_grad():
        normed_grad = (
            dot(late_r[:, :width], wq_ref[...], NT)
            + dot(late_r[:, width : 2 * width], wk_ref[...], NT)
            + dot(late_r[:, 2 * width :], wv_ref[...], NT)
        )
        values = x_ref[...].astype(F32)
        centred = values - jnp.mean(values, axis=-1, keepdims=True)
        scale = lax.rsqrt(jnp.mean(centred * centred, axis=-1, keepdims=True) + EPSILON)
        unit = centred * scale
        inner = normed_grad * g_ref[...].reshape(1, width)
        back = scale * (
            inner
            - jnp.mean(inner, axis=-1, keepdims=True)
            - unit * jnp.mean(inner * unit, axis=-1, keepdims=True)
        )
        gin_ref[...] = hg_ref[...] + back

        def sums(v):
            return jnp.sum(v.astype(F32), axis=0, keepdims=True)

        return jnp.concatenate(
            [
                sums(normed_grad * unit),
                sums(normed_grad),
                sums(late_r[:, :width]),
                jnp.concatenate([sums(late_r[:, 2 * width :]), jnp.zeros((1, width // 2), F32)], axis=1),
                jnp.zeros((4, width), F32),
            ],
            axis=0,
        )

    def do(*tasks):
        for stage, what in tasks if weights else ():
            (early_vectors, make, second, third, fourth, finish)[stage](what)

    do((0, 0), (1, OUT), (1, UP + 1), (1, UP))
    if attention:
        for slot in range(SLOTS):
            key_copy(slot).wait()
            arrive(slot)
            for k in range(PLANES):
                grads(slot, k)
                if slot and k == 1:
                    reduce_line(slot - 1)
                do(*AT_POINTS.get((slot, k), ()))
            if slot == 0:
                key_copy(2).start()
            if slot:
                reduce_end(slot - 1)
            reduce_core(slot)
    else:
        for tasks in AT_POINTS.values():
            do(*tasks)
    do(*AFTER[0])
    if attention:
        reduce_line(SLOTS - 1)
    do(*AFTER[1])
    if attention:
        reduce_end(SLOTS - 1)
    do(*AFTER[2])
    if attention:
        late_factors()
    if weights:
        swap(7, late_r, rp_late)
        partial = input_grad()
        late_vectors = vectors(1, lambda: partial, vec2_ref)
        late_vectors(0)
        for stage, tasks in enumerate(AFTER[3:]):
            do(*tasks)
            if stage < 4:
                late_vectors(stage + 1)
    for copy in sent:
        copy.wait_send()


AT_POINTS = {
    (0, 0): ((1, UP + 3), (1, UP + 2)),
    (0, 1): ((1, DOWN + 1), (1, DOWN), (0, 1)),
    (0, 2): ((1, DOWN + 3), (1, DOWN + 2)),
    (0, 3): ((0, 2),),
    (1, 0): ((2, OUT), (2, UP + 1)),
    (1, 1): ((0, 3),),
    (1, 3): ((2, UP), (3, OUT), (0, 4)),
    (2, 0): ((3, UP + 1),),
    (2, 1): ((2, UP + 3),),
    (2, 2): ((2, UP + 2), (4, OUT)),
    (2, 3): ((3, UP), (4, UP + 1)),
}
AFTER = (
    ((2, DOWN), (3, UP + 3)),
    ((2, DOWN + 1), (3, UP + 2), (4, UP)),
    ((2, DOWN + 2), (4, UP + 3), (3, DOWN), (4, UP + 2), (5, OUT)),
    ((1, QUERY), (1, KEY), (1, VALUE), (2, DOWN + 3), (3, DOWN + 1), (4, DOWN)),
    ((3, DOWN + 2), (4, DOWN + 1), (5, UP), (5, UP + 1), (2, KEY), (2, QUERY)),
    ((3, DOWN + 3), (4, DOWN + 2), (2, VALUE), (3, KEY), (5, UP + 2), (5, UP + 3)),
    ((3, QUERY), (4, DOWN + 3), (3, VALUE), (4, KEY)),
    ((4, QUERY), (4, VALUE), (5, DOWN), (5, DOWN + 1), (5, DOWN + 2), (5, DOWN + 3), (5, KEY), (5, QUERY), (5, VALUE)),
)


def backward_call(plane, groups, rows, width, hidden, attention, weights, arrays):
    blocks = plane * PLANES
    lines = plane // 2
    size = width // HEADS
    half = rows // 2
    shard = width // blocks
    tall = hidden // width
    lw = width // groups
    lv = width // 2 // groups
    late = 2 * width + width // 2
    count = PIECES
    dma = pltpu.SemaphoreType.DMA
    most = max(groups, lines)

    def vmem(*shape):
        return pltpu.VMEM(shape, BF16)

    def vmem32(*shape):
        return pltpu.VMEM(shape, F32)

    ins = {}
    outs = {}
    scratch = {}
    if attention:
        ins.update(mg_ref=VMEM, all_ref=pl.BlockSpec(memory_space=pl.ANY), o_ref=VMEM, lse_ref=VMEM, spans_ref=SMEM)
        outs.update(gfv_ref=((rows, width // 2), BF16))
        scratch.update(
            dpack=vmem(PLANES, SLOTS, half, 2 * size),
            drecv=vmem(SLOTS, PLANES, half, 2 * size),
            masks=vmem(PLANES, plane * rows, rows),
            acc=vmem32(2, PLANES, plane * rows, 2 * size),
            part=vmem(SLOTS, lines, PLANES, rows, 2 * size),
            cgot=vmem(SLOTS, lines, PLANES, rows, 2 * size),
            xpart=vmem(SLOTS, lines - 1, PLANES, rows, 2 * size),
            xgot=vmem(SLOTS, lines - 1, PLANES, rows, 2 * size),
            ret=vmem(PLANES, SLOTS, rows + half, 2 * size),
            got=vmem(SLOTS, PLANES, rows + half, 2 * size),
            keybuf=vmem(2, PLANES, plane, rows + half, 2 * size),
            keysem=dma((2,)),
            zsend=dma((SLOTS, PLANES)), zrecv=dma((SLOTS, PLANES)),
            csend=dma((SLOTS, lines)), crecv=dma((SLOTS, lines)),
            xsend=dma((SLOTS, lines)), xrecv=dma((SLOTS, lines)),
            rsend=dma((SLOTS, PLANES)), rrecv=dma((SLOTS, PLANES)),
        )
        if weights:
            scratch.update(late_own=vmem(rows, late))
        else:
            outs.update(late_out=((rows, late), BF16))
    if weights:
        ins.update(
            lt_a=VMEM, lt_n2=VMEM, lt_act=VMEM, lt_n=VMEM, branch_ref=VMEM, ug_ref=VMEM, dout_ref=VMEM, vec_ref=VMEM,
            x_ref=VMEM, g_ref=VMEM, hg_ref=VMEM, wq_ref=VMEM, wk_ref=VMEM, wv_ref=VMEM,
        )
        if not attention:
            ins.update(late_in=VMEM)
        outs.update(
            gin_ref=((rows, width), F32), vec1_ref=((8, width), F32), vec2_ref=((8, width), F32),
            fin=((count - 1, groups, shard, lw), BF16), fin_v=((1, groups, shard, lv), BF16),
        )
        scratch.update(
            ltp_a=vmem(PLANES, lines, 1, shard, rows),
            ltp_n2=vmem(PLANES, lines, 1, shard, rows),
            ltp_act=vmem(PLANES, lines, tall, shard, rows),
            ltp_n=vmem(PLANES, lines, 1, shard, rows),
            rp_branch=vmem(rows, width), rp_ug=vmem(rows, hidden), rp_dout=vmem(rows, width), rp_late=vmem(rows, late),
            vbuf_c=vmem32(2, 2, 8, width), vbuf_x=vmem32(2, lines, 8, width),
            vbuf_y=vmem32(2, groups, 8, width), vbuf_z=vmem32(2, PLANES, 8, width),
            esend=dma((8,)), erecv=dma((8,)),
            s1send=dma((count, most)), s1recv=dma((count, most)),
            s2send=dma((count, most)), s2recv=dma((count, most)),
            wzsend=dma((count, PLANES)), wzrecv=dma((count, PLANES)),
            fsend=dma((count, groups)), frecv=dma((count, groups)),
            vsend=dma((2, 4, max(most, PLANES))), vrecv=dma((2, 4, max(most, PLANES))),
        )
        for tag, n, lanes in (("", count - 1, lw), ("_v", 1, lv)):
            scratch.update({
                "wbuf" + tag: vmem(n, groups, lines, PLANES, shard, lanes),
                "gy" + tag: vmem(n, groups - 1, lines, PLANES, shard, lanes),
                "gx" + tag: vmem(n, lines - 1, groups if LINE_FIRST else 1, PLANES, shard, lanes),
                "sx" + tag: vmem(n, lines - 1, PLANES, shard, lanes),
                "zs" + tag: vmem(n, PLANES, shard, lanes),
                "zg" + tag: vmem(n, PLANES - 1, shard, lanes),
            })
            if LINE_FIRST:
                scratch["sy" + tag] = vmem(n, groups - 1, PLANES, shard, lanes)
    names = tuple(ins) + tuple(outs) + tuple(scratch)
    result = pl.pallas_call(
        functools.partial(backward_kernel, plane, groups, shard, names, attention, weights),
        name="backward",
        out_shape=tuple(jax.ShapeDtypeStruct(*v) for v in outs.values()),
        in_specs=list(ins.values()),
        out_specs=(VMEM,) * len(outs),
        scratch_shapes=list(scratch.values()),
        compiler_params=pltpu.CompilerParams(
            collective_id=2 if attention else 3, has_side_effects=True, vmem_limit_bytes=61 << 20
        ),
    )(*[arrays[name] for name in ins])
    return dict(zip(outs, result))


def tail_kernel(
    gin_ref, gfv_ref, vec1_ref, vec2_ref, fin_ref, finv_ref,
    o_gin, o_gfv, o_g1, o_s1, o_wq, o_bq, o_wk, o_wv, o_bv, o_wo, o_bo, o_g2, o_s2, o_wu, o_bu, o_wd, o_bd,
):
    groups, shard, lanes = fin_ref.shape[1:]
    width = groups * lanes
    tall = o_wd.shape[0] // shard
    o_gin[...] = gin_ref[...]
    o_gfv[...] = gfv_ref[...]

    def put(ref, rows, at, piece):
        for h in range(groups):
            ref[rows, at + h * lanes : at + (h + 1) * lanes] = fin_ref[piece, h].astype(F32)

    everything = slice(0, shard)
    put(o_wo, everything, 0, OUT)
    put(o_wq, everything, 0, QUERY)
    put(o_wk, everything, 0, KEY)
    for i in range(tall):
        put(o_wu, everything, i * width, UP + i)
        put(o_wd, slice(i * shard, (i + 1) * shard), 0, DOWN + i)
    for h in range(groups):
        o_wv[:, h * (lanes // 2) : (h + 1) * (lanes // 2)] = finv_ref[0, h].astype(F32)
    o_g2[...], o_s2[...], o_bo[...], o_bd[...] = vec1_ref[0], vec1_ref[1], vec1_ref[2], vec1_ref[3 + tall]
    for i in range(tall):
        o_bu[i * width : (i + 1) * width] = vec1_ref[3 + i]
    o_g1[...], o_s1[...], o_bq[...] = vec2_ref[0], vec2_ref[1], vec2_ref[2]
    o_bv[...] = vec2_ref[3, : width // 2]


def tail_part(rows, width, hidden, shard, got):
    def out(*shape):
        return jax.ShapeDtypeStruct(shape, F32)

    return pl.pallas_call(
        tail_kernel,
        name="tail",
        out_shape=(
            out(rows, width), jax.ShapeDtypeStruct((rows, width // 2), BF16), out(width), out(width),
            out(shard, width), out(width), out(shard, width), out(shard, width // 2), out(width // 2),
            out(shard, width), out(width), out(width), out(width),
            out(shard, hidden), out(hidden), out(hidden // width * shard, width), out(width),
        ),
        in_specs=[VMEM] * 6,
        out_specs=(VMEM,) * 17,
    )(*got)


def body(
    inputs,
    first_values,
    spans,
    ln1_gain,
    ln1_shift,
    w_query,
    b_query,
    w_key,
    w_value,
    b_value,
    w_out,
    b_out,
    ln2_gain,
    ln2_shift,
    w_up,
    b_up,
    w_down,
    b_down,
    out_grad,
):
    rows, width = inputs.shape
    hidden = w_up.shape[1]
    groups = lax.axis_size("grp")
    plane = lax.axis_size("blk") // PLANES
    attended, normed, all_blocks, mixed, lse = forward_part(
        inputs, first_values, spans, ln1_gain, ln1_shift, w_query, b_query, w_key, w_value, b_value
    )
    result, mixed_grad, hidden_grad, branch_grad, upper_grad, grad_down, vectors, lt_a, lt_n2, lt_act, lt_n = middle_part(
        plane, inputs, attended, normed, spans, out_grad, b_out, ln2_gain, ln2_shift, b_up, b_down, w_out, w_up, w_down
    )
    arrays = dict(
        mg_ref=mixed_grad, all_ref=all_blocks, o_ref=mixed, lse_ref=lse, spans_ref=spans,
        lt_a=lt_a, lt_n2=lt_n2, lt_act=lt_act, lt_n=lt_n,
        branch_ref=branch_grad, ug_ref=upper_grad, dout_ref=grad_down, vec_ref=vectors,
        x_ref=inputs, g_ref=ln1_gain, hg_ref=hidden_grad, wq_ref=w_query, wk_ref=w_key, wv_ref=w_value,
    )
    call = functools.partial(backward_call, plane, groups, rows, width, hidden)
    if plane <= 4:
        got = Refs(call(True, True, arrays))
    else:
        got = Refs(call(True, False, arrays))
        arrays.update(late_in=got.late_out)
        got.update(call(False, True, arrays))
    return (result,) + tuple(
        tail_part(
            rows, width, hidden, width // (plane * PLANES),
            (got.gin_ref, got.gfv_ref, got.vec1_ref, got.vec2_ref, got.fin, got.fin_v),
        )
    )


def solution(mesh):
    placed = (
        P(("grp", "blk"), None),
        P(("grp", "blk"), None),
        P("grp", None),
        P(),
        P(),
        P(),
        P(),
        P(),
        P(),
        P(),
        P(),
        P(),
        P(),
        P(),
        P(),
        P(),
        P(),
        P(),
        P(("grp", "blk"), None),
    )
    return jax.shard_map(
        body,
        mesh=mesh,
        in_specs=placed,
        out_specs=(
            P(("grp", "blk"), None),
            P(("grp", "blk"), None),
            P(("grp", "blk"), None),
            P(),
            P(),
            P("blk", None),
            P(),
            P("blk", None),
            P("blk", None),
            P(),
            P("blk", None),
            P(),
            P(),
            P(),
            P("blk", None),
            P(),
            P("blk", None),
            P(),
        ),
        check_vma=False,
    )
```

```python
import functools

import jax
import jax.numpy as jnp
from jax import lax
from jax.experimental import pallas as pl
from jax.experimental.pallas import tpu as pltpu
from jax.sharding import PartitionSpec as P

HEADS = 12
PLANES = 4
SLOTS = HEADS // PLANES
EPSILON = 1e-05
GELU_COEF = 0.7978845608028654
NEG_FILL = -1e30
BF16 = jnp.bfloat16
F32 = jnp.float32
MESH = pl.DeviceIdType.MESH
VMEM = pl.BlockSpec(memory_space=pltpu.VMEM)
SMEM = pl.BlockSpec(memory_space=pltpu.SMEM)


def dot(a, b, dims):
    return lax.dot_general(a, b, (dims, ((), ())), preferred_element_type=F32)


NN = ((1,), (0,))
NT = ((1,), (1,))
TN = ((0,), (0,))


def norm_rows(values, gain, shift):
    average = jnp.mean(values, axis=-1, keepdims=True)
    centred = values - average
    variance = jnp.mean(centred * centred, axis=-1, keepdims=True)
    return centred * lax.rsqrt(variance + EPSILON) * gain + shift


def place(plane):
    block = lax.axis_index("blk")
    return block // plane, lax.rem(block, plane)


def at_z(z, c, plane, offset):
    return {"blk": lax.rem(z + offset, PLANES) * plane + c}


def at_x(z, c, plane, offset):
    lines = plane // 2
    column, core = c // 2, lax.rem(c, 2)
    return {"blk": z * plane + lax.rem(column + offset, lines) * 2 + core}


def at_core(z, c, plane):
    return {"blk": z * plane + (c // 2) * 2 + 1 - lax.rem(c, 2)}


def greet(partners):
    barrier = pltpu.get_barrier_semaphore()
    for partner in partners:
        pl.semaphore_signal(barrier, inc=1, device_id=partner, device_id_type=MESH)
    pl.semaphore_wait(barrier, len(partners))


def remote(src, dst, send, recv, partner):
    return pltpu.make_async_remote_copy(
        src_ref=src, dst_ref=dst, send_sem=send, recv_sem=recv,
        device_id=partner, device_id_type=MESH,
    )


def query_rows(pack, first):
    half = pack.shape[1] // 2
    lanes = lax.broadcasted_iota(jnp.int32, pack.shape, 1)
    wide = pack.astype(F32)
    other = pltpu.roll(wide, half, 1)
    keep = lanes < half if first else lanes >= half
    top, bottom = (wide, other) if first else (other, wide)
    return jnp.concatenate(
        [jnp.where(keep, top, 0.0), jnp.where(keep, bottom, 0.0)], axis=0
    ).astype(BF16)


def position_masks(spans_ref, plane, length, c, k, rows):
    first, end = spans_ref[0, 0], length - spans_ref[0, 1]
    dead = end - spans_ref[0, 2]
    width = plane * rows
    key = k * width + lax.broadcasted_iota(jnp.int32, (width, rows), 0)
    query = k * width + c * rows + lax.broadcasted_iota(jnp.int32, (width, rows), 1)
    allowed = key <= query
    if k == 0:
        allowed &= ((key >= first) == (query >= first))
    if k == PLANES - 1:
        allowed &= ((key >= end) == (query >= end)) & ((key < dead) | (key >= end))
    return jnp.where(allowed, 0.0, NEG_FILL)


def forward_kernel(
    plane, x_ref, fv_ref, spans_ref, g_ref, s_ref, wq_ref, bq_ref, wk_ref, wv_ref, bv_ref,
    att_ref, normed_ref, all_ref, o_ref, lse_ref,
    pack, opack, orecv, masks,
    zsend, zrecv, xsend, xrecv, csend, crecv, osend, orecv_sem,
):
    rows, width = x_ref.shape
    size = width // HEADS
    lines = plane // 2
    length = rows * plane * PLANES
    half = rows // 2
    z, c = place(plane)
    core = lax.rem(c, 2)
    greet(
        [at_z(z, c, plane, d) for d in range(1, PLANES)]
        + [at_x(z, c, plane, d) for d in range(1, lines)]
        + [at_core(z, c, plane)]
    )
    normed = norm_rows(
        x_ref[...].astype(F32), g_ref[...].reshape(1, width), s_ref[...].reshape(1, width)
    ).astype(BF16)
    normed_ref[...] = normed
    query = ((dot(normed, wq_ref[...], NN) + bq_ref[...].reshape(1, width)) * 0.125)
    key = dot(normed, wk_ref[...], NN)
    fresh = dot(normed, wv_ref[...], NN) + bv_ref[...].reshape(1, width // 2)
    value = jnp.concatenate([fresh, fv_ref[...].astype(F32)], axis=1)
    for head in range(HEADS):
        to, slot = divmod(head, SLOTS)
        cols = slice(head * size, (head + 1) * size)
        pack[to, slot, :rows, :] = jnp.concatenate(
            [key[:, cols], value[:, cols]], axis=1
        ).astype(BF16)
        pack[to, slot, rows:, :] = jnp.concatenate(
            [query[:half, cols], query[half:, cols]], axis=1
        ).astype(BF16)

    zcopies = {}
    for slot in range(SLOTS):
        for d in (2, 1, 3):
            to = lax.rem(z + d, PLANES)
            copy = remote(
                pack.at[to, slot], all_ref.at[slot, z, c],
                zsend.at[slot, d], zrecv.at[slot, d], at_z(z, c, plane, d),
            )
            copy.start()
            zcopies[slot, d] = copy
        all_ref[slot, z, c] = pack[z, slot]

    for k in range(PLANES):
        masks[k] = position_masks(spans_ref, plane, length, c, k, rows)
    first, end = spans_ref[0, 0], length - spans_ref[0, 1]

    started = []

    def spread(slot):
        for d in (0, 1, 3, 2):
            src = lax.rem(z + PLANES - d, PLANES)
            if d:
                zcopies[slot, d].wait_recv()
            block = all_ref.at[slot, src, c, pl.ds(0, rows)]
            for e in range(1, lines):
                copy = remote(
                    block, block, xsend.at[slot, d, e], xrecv.at[slot, d, e], at_x(z, c, plane, e)
                )
                copy.start()
                started.append(copy)
            copy = remote(block, block, csend.at[slot, d, 0], crecv.at[slot, d, 0], at_core(z, c, plane))
            copy.start()
            started.append(copy)

    def pass_on(slot):
        for d in (0, 1, 3, 2):
            src = lax.rem(z + PLANES - d, PLANES)
            for e in range(1, lines):
                column = lax.rem(c // 2 + lines - e, lines) * 2 + core
                block = all_ref.at[slot, src, column, pl.ds(0, rows)]
                remote(
                    block, block, xsend.at[slot, d, e], xrecv.at[slot, d, e], at_x(z, c, plane, e)
                ).wait_recv()
                copy = remote(
                    block, block, csend.at[slot, d, e], crecv.at[slot, d, e], at_core(z, c, plane)
                )
                copy.start()
                started.append(copy)

    def settle(slot):
        for d in range(PLANES):
            for e in range(lines):
                block = all_ref.at[slot, 0, c, pl.ds(0, rows)]
                remote(
                    block, block, csend.at[slot, d, e], crecv.at[slot, d, e], at_core(z, c, plane)
                ).wait_recv()

    def keys_of(slot, k):
        return all_ref[slot, k, :, :rows, :].reshape(plane * rows, 2 * size)

    def attend(slot, k):
        q = query_rows(all_ref[slot, k, c, rows:, :], True)

        def step(state, k2, bias):
            top, total, acc = state
            keys = keys_of(slot, k2)
            scores = bias(dot(keys, q, NT))
            new = jnp.maximum(top, jnp.max(scores, axis=0, keepdims=True))
            prob = jnp.exp(scores - new)
            scale = jnp.exp(top - new)
            return (
                new,
                total * scale + jnp.sum(prob, axis=0, keepdims=True),
                acc * scale + dot(keys, prob.astype(BF16), TN),
            )

        state = (
            jnp.full((1, rows), NEG_FILL, F32),
            jnp.zeros((1, rows), F32),
            jnp.zeros((2 * size, rows), F32),
        )
        state = step(state, k, lambda t: t + masks[k])
        diagonal = state
        for k2 in range(k):
            if k2 == 0:
                index = lax.broadcasted_iota(jnp.int32, (plane * rows, 1), 0)
                shut = jnp.where(index < first, NEG_FILL, 0.0)
                state = step(state, k2, lambda t: t + shut)
            else:
                state = step(state, k2, lambda t: t)
        if k == PLANES - 1:
            position = k * plane * rows + c * rows + lax.broadcasted_iota(jnp.int32, (1, rows), 1)
            after = position >= end
            state = tuple(jnp.where(after, old, new) for old, new in zip(diagonal, state))
        top, total, acc = state
        mixed = acc[size:] / total
        o_ref[slot, k] = mixed
        lse_ref[slot, k] = jnp.broadcast_to(top + jnp.log(total), (8, rows))
        packed = jnp.concatenate([mixed[:, :half], mixed[:, half:]], axis=0)
        opack[slot, k] = jnp.transpose(packed).astype(BF16)

    def give_back(slot):
        orecv[slot, z] = opack[slot, z]
        for d in (2, 1, 3):
            to = lax.rem(z + d, PLANES)
            copy = remote(
                opack.at[slot, to], orecv.at[slot, z],
                osend.at[slot, d], orecv_sem.at[slot, d], at_z(z, c, plane, d),
            )
            copy.start()
            started.append(copy)

    spread(0)
    pass_on(0)
    for slot in range(SLOTS):
        settle(slot)
        for k in range(PLANES):
            attend(slot, k)
            if slot + 1 < SLOTS:
                if k == 1:
                    spread(slot + 1)
                if k == 3:
                    pass_on(slot + 1)
        give_back(slot)
    for slot in range(SLOTS):
        for d in range(1, PLANES):
            remote(
                opack.at[slot, 0], orecv.at[slot, 0],
                osend.at[slot, d], orecv_sem.at[slot, d], at_z(z, c, plane, d),
            ).wait_recv()
    for pair in range(HEADS // 2):
        parts = []
        for head in (2 * pair, 2 * pair + 1):
            src, slot = divmod(head, SLOTS)
            got = orecv[slot, src].astype(F32)
            parts.append(jnp.concatenate([got[:, :size], got[:, size:]], axis=0))
        att_ref[:, pair * 2 * size : (pair + 1) * 2 * size] = jnp.concatenate(parts, axis=1).astype(BF16)
    for copy in list(zcopies.values()) + started:
        copy.wait_send()


def forward_part(inputs, first_values, spans, ln1_gain, ln1_shift, w_query, b_query, w_key, w_value, b_value):
    rows, width = inputs.shape
    plane = lax.axis_size("blk") // PLANES
    lines = plane // 2
    size = width // HEADS
    half = rows // 2
    dma = pltpu.SemaphoreType.DMA
    return pl.pallas_call(
        functools.partial(forward_kernel, plane),
        name="forward",
        out_shape=(
            jax.ShapeDtypeStruct((rows, width), BF16),
            jax.ShapeDtypeStruct((rows, width), BF16),
            jax.ShapeDtypeStruct((SLOTS, PLANES, plane, rows + half, 2 * size), BF16),
            jax.ShapeDtypeStruct((SLOTS, PLANES, size, rows), F32),
            jax.ShapeDtypeStruct((SLOTS, PLANES, 8, rows), F32),
        ),
        in_specs=[VMEM, VMEM, SMEM] + [VMEM] * 7,
        out_specs=(VMEM,) * 5,
        scratch_shapes=[
            pltpu.VMEM((PLANES, SLOTS, rows + half, 2 * size), BF16),
            pltpu.VMEM((SLOTS, PLANES, half, 2 * size), BF16),
            pltpu.VMEM((SLOTS, PLANES, half, 2 * size), BF16),
            pltpu.VMEM((PLANES, plane * rows, rows), F32),
            dma((SLOTS, PLANES)), dma((SLOTS, PLANES)),
            dma((SLOTS, PLANES, lines)), dma((SLOTS, PLANES, lines)),
            dma((SLOTS, PLANES, lines)), dma((SLOTS, PLANES, lines)),
            dma((SLOTS, PLANES)), dma((SLOTS, PLANES)),
        ],
        compiler_params=pltpu.CompilerParams(
            collective_id=1, has_side_effects=True, vmem_limit_bytes=56 << 20
        ),
    )(
        inputs, first_values, spans, ln1_gain, ln1_shift, w_query, b_query, w_key, w_value, b_value,
    )


def middle_kernel(
    x_ref, att_ref, normed_ref, spans_ref, og_ref, bo_ref, g_ref, s_ref, bu_ref, bd_ref,
    wo_hbm, wu_hbm, wd_hbm,
    result_ref, mg_ref, hg_ref, branch_ref, ug_ref, dout_ref, vec_ref, lt_a, lt_n2, lt_act, lt_n,
    wo_ref, wu_ref, wd_ref, sem,
):
    rows, width = x_ref.shape
    tall = bu_ref.shape[0] // width
    shard = lt_a.shape[4]
    copies = [
        pltpu.make_async_copy(src, dst, sem.at[i])
        for i, (src, dst) in enumerate(((wo_hbm, wo_ref), (wu_hbm, wu_ref), (wd_hbm, wd_ref)))
    ]
    for copy in copies:
        copy.start()

    def turn(value, dst, piece):
        turned = jnp.transpose(value.astype(F32)).astype(BF16)
        at = 0
        span = width // (dst.shape[0] * dst.shape[1] * 2)
        if dst.shape[3] == 1:
            for zz in range(dst.shape[0]):
                for xx in range(dst.shape[1]):
                    for cc in range(2):
                        dst[zz, xx, cc, 0] = turned[at : at + span]
                        at += span
            return
        per = dst.shape[3]
        for unit in range(width // span):
            index = piece * (width // span) + unit
            owner, part = divmod(index, per)
            chip, cc = divmod(owner, 2)
            zz, xx = divmod(chip, dst.shape[1])
            dst[zz, xx, cc, part] = turned[unit * span : (unit + 1) * span]

    def sums(value):
        return jnp.sum(value.astype(F32), axis=0, keepdims=True)

    block = lax.axis_index("blk")
    length = rows * lax.axis_size("blk")
    end = length - spans_ref[0, 1]
    position = block * rows + lax.broadcasted_iota(jnp.int32, (rows, 1), 0)
    alive = (position < end - spans_ref[0, 2]) | (position >= end)
    dout = jnp.where(alive, og_ref[...].astype(F32), 0.0)
    dout_low = dout.astype(BF16)
    dout_ref[...] = dout_low
    vec_ref[3 + tall : 4 + tall, :] = sums(dout)
    attended = att_ref[...]
    turn(normed_ref[...], lt_n, 0)
    turn(attended, lt_a, 0)
    copies[0].wait()
    hidden = x_ref[...].astype(F32) + dot(attended, wo_ref[...], NN) + bo_ref[...].reshape(1, width)
    average = jnp.mean(hidden, axis=-1, keepdims=True)
    centred = hidden - average
    scale = lax.rsqrt(jnp.mean(centred * centred, axis=-1, keepdims=True) + EPSILON)
    unit = centred * scale
    gain = g_ref[...].reshape(1, width)
    normed2 = (unit * gain + s_ref[...].reshape(1, width)).astype(BF16)
    turn(normed2, lt_n2, 0)
    copies[1].wait()
    copies[2].wait()
    result = hidden + bd_ref[...].reshape(1, width)
    normed2_grad = jnp.zeros((rows, width), F32)
    for i in range(tall):
        cols = slice(i * width, (i + 1) * width)
        upper = dot(normed2, wu_ref[:, cols], NN) + bu_ref[cols].reshape(1, width)
        square = upper * upper
        curve = jnp.tanh(GELU_COEF * (upper + 0.044715 * upper * square))
        half = 0.5 * (1.0 + curve)
        active = (upper * half).astype(BF16)
        slope = half + 0.5 * upper * (1.0 - curve * curve) * (GELU_COEF * (1.0 + 3.0 * 0.044715 * square))
        turn(active, lt_act, i)
        result = result + dot(active, wd_ref[cols, :], NN)
        upper_grad = (dot(dout_low, wd_ref[cols, :], NT) * slope).astype(BF16)
        ug_ref[:, cols] = upper_grad
        vec_ref[3 + i : 4 + i, :] = sums(upper_grad)
        normed2_grad = normed2_grad + dot(upper_grad, wu_ref[:, cols], NT)
    result_ref[...] = result
    vec_ref[0:1, :] = sums(normed2_grad * unit)
    vec_ref[1:2, :] = sums(normed2_grad)
    inner = normed2_grad * gain
    back = scale * (
        inner - jnp.mean(inner, axis=-1, keepdims=True) - unit * jnp.mean(inner * unit, axis=-1, keepdims=True)
    )
    hidden_grad = dout + back
    hg_ref[...] = hidden_grad
    branch = hidden_grad.astype(BF16)
    branch_ref[...] = branch
    vec_ref[2:3, :] = sums(branch)
    mg_ref[...] = dot(branch, wo_ref[...], NT).astype(BF16)


def middle_part(plane, inputs, attended, normed, spans, out_grad, b_out, gain, shift, b_up, b_down, w_out, w_up, w_down):
    rows, width = inputs.shape
    hidden = w_up.shape[1]
    tall = hidden // width
    lines = plane // 2
    shard = width // (plane * PLANES)

    def low(*shape):
        return jax.ShapeDtypeStruct(shape, BF16)

    any_space = pl.BlockSpec(memory_space=pl.ANY)
    return pl.pallas_call(
        middle_kernel,
        name="middle",
        out_shape=(
            jax.ShapeDtypeStruct((rows, width), F32), low(rows, width), jax.ShapeDtypeStruct((rows, width), F32),
            low(rows, width), low(rows, hidden), low(rows, width), jax.ShapeDtypeStruct((4 + tall, width), F32),
            low(PLANES, lines, 2, 1, shard, rows), low(PLANES, lines, 2, 1, shard, rows),
            low(PLANES, lines, 2, tall, shard, rows), low(PLANES, lines, 2, 1, shard, rows),
        ),
        in_specs=[VMEM, VMEM, VMEM, SMEM] + [VMEM] * 6 + [any_space] * 3,
        out_specs=(VMEM,) * 11,
        scratch_shapes=[
            pltpu.VMEM((width, width), BF16), pltpu.VMEM((width, hidden), BF16), pltpu.VMEM((hidden, width), BF16),
            pltpu.SemaphoreType.DMA((3,)),
        ],
        compiler_params=pltpu.CompilerParams(vmem_limit_bytes=56 << 20),
    )(inputs, attended, normed, spans, out_grad, b_out, gain, shift, b_up, b_down, w_out, w_up, w_down)


OUT, UP, DOWN, QUERY, KEY, VALUE = 0, 1, 5, 9, 10, 11
PIECES = 12
LINE_FIRST = frozenset((OUT, DOWN, DOWN + 1, VALUE))


class Refs(dict):
    __getattr__ = dict.get


def backward_kernel(plane, groups, shard, names, attention, weights, *refs):
    r = Refs(zip(names, refs, strict=True))
    mg_ref, all_ref, o_ref, lse_ref, spans_ref, lt_a, lt_n2, lt_act = r.mg_ref, r.all_ref, r.o_ref, r.lse_ref, r.spans_ref, r.lt_a, r.lt_n2, r.lt_act
    lt_n, branch_ref, ug_ref, dout_ref, vec_ref, x_ref, g_ref, hg_ref = r.lt_n, r.branch_ref, r.ug_ref, r.dout_ref, r.vec_ref, r.x_ref, r.g_ref, r.hg_ref
    wq_ref, wk_ref, wv_ref, late_in, gin_ref, gfv_ref, vec1_ref = r.wq_ref, r.wk_ref, r.wv_ref, r.late_in, r.gin_ref, r.gfv_ref, r.vec1_ref
    late_out, dpack = r.late_out, r.dpack
    drecv, masks, acc, part, cgot, xpart, xgot, ret = r.drecv, r.masks, r.acc, r.part, r.cgot, r.xpart, r.xgot, r.ret
    got, keybuf, keysem, ltp_a, ltp_n2, ltp_act, ltp_n, rp_branch = r.got, r.keybuf, r.keysem, r.ltp_a, r.ltp_n2, r.ltp_act, r.ltp_n, r.rp_branch
    rp_ug, rp_dout, late_own, rp_late, wbuf, gy, gx, sx = r.rp_ug, r.rp_dout, r.late_own, r.rp_late, r.wbuf, r.gy, r.gx, r.sx
    sy, zs, zg, fin, wbuf_v, gy_v, gx_v, sx_v = r.sy, r.zs, r.zg, r.fin, r.wbuf_v, r.gy_v, r.gx_v, r.sx_v
    sy_v, zs_v, zg_v, fin_v, vbuf_c, vbuf_x, vbuf_y, vbuf_z = r.sy_v, r.zs_v, r.zg_v, r.fin_v, r.vbuf_c, r.vbuf_x, r.vbuf_y, r.vbuf_z
    zsend, zrecv, csend, crecv, xsend, xrecv, rsend, rrecv = r.zsend, r.zrecv, r.csend, r.crecv, r.xsend, r.xrecv, r.rsend, r.rrecv
    esend, erecv, s1send, s1recv, s2send, s2recv, wzsend, wzrecv = r.esend, r.erecv, r.s1send, r.s1recv, r.s2send, r.s2recv, r.wzsend, r.wzrecv
    fsend, frecv, vsend, vrecv = r.fsend, r.frecv, r.vsend, r.vrecv
    late_r = late_own if late_own is not None else (late_out if late_out is not None else late_in)
    rows, width = (mg_ref if attention else x_ref).shape
    size = width // HEADS
    lines = plane // 2
    length = rows * plane * PLANES
    half = rows // 2
    z, c = place(plane)
    column, core = c // 2, lax.rem(c, 2)
    group = lax.axis_index("grp")
    lw = width // groups

    def at_group(offset):
        return {"grp": lax.rem(group + offset, groups)}

    to_core = at_core(z, c, plane)
    greet(
        [at_z(z, c, plane, d) for d in range(1, PLANES)]
        + [at_x(z, c, plane, d) for d in range(1, lines)]
        + [to_core]
        + [at_group(d) for d in range(1, groups) if weights]
    )
    sent = []

    def start(copy):
        copy.start()
        sent.append(copy)

    def dcopy(slot, d):
        return remote(
            dpack.at[lax.rem(z + d, PLANES), slot], drecv.at[slot, z],
            zsend.at[slot, d], zrecv.at[slot, d], at_z(z, c, plane, d),
        )

    def key_copy(slot):
        return pltpu.make_async_copy(all_ref.at[slot], keybuf.at[slot % 2], keysem.at[slot % 2])

    for slot in range(SLOTS if attention else 0):
        if slot < 2:
            key_copy(slot).start()
        for to in range(PLANES):
            cols = slice((to * SLOTS + slot) * size, (to * SLOTS + slot + 1) * size)
            dpack[to, slot] = jnp.concatenate([mg_ref[:half, cols], mg_ref[half:, cols]], axis=1)
        for d in (2, 1, 3):
            start(dcopy(slot, d))
        drecv[slot, z] = dpack[z, slot]

    def arrive(slot):
        for d in range(1, PLANES):
            dcopy(slot, d).wait_recv()

    exchange = {}

    def swap(index, src, dst):
        exchange[index] = remote(src, dst, esend.at[index], erecv.at[index], to_core)
        start(exchange[index])

    def arrived(*indices):
        for index in indices:
            copy = exchange.pop(index, None)
            if copy is not None:
                copy.wait_recv()

    if weights:
        swap(0, lt_a.at[:, :, 1 - core], ltp_a)
        swap(1, branch_ref, rp_branch)
        swap(2, lt_n2.at[:, :, 1 - core], ltp_n2)
        swap(3, ug_ref, rp_ug)
        swap(4, lt_act.at[:, :, 1 - core], ltp_act)
        swap(5, dout_ref, rp_dout)
        swap(6, lt_n.at[:, :, 1 - core], ltp_n)

    if attention:
        for k in range(PLANES):
            masks[k] = position_masks(spans_ref, plane, length, c, k, rows).astype(BF16)
        first, end = spans_ref[0, 0], length - spans_ref[0, 1]

    def vectors(value, result):
        stages = [
            (vbuf_y, group, groups, at_group, 2),
            (vbuf_c, core, 2, lambda e: to_core, 0),
            (vbuf_x, column, lines, lambda e: at_x(z, c, plane, e), 1),
            (vbuf_z, z, PLANES, lambda e: at_z(z, c, plane, e), 3),
        ]

        def copies(stage):
            buf, me, count, partner, axis = stages[stage]
            return [
                remote(
                    buf.at[me], buf.at[me],
                    vsend.at[axis, e], vrecv.at[axis, e], partner(e),
                )
                for e in range(1, count)
            ]

        def step(stage):
            if stage == 0:
                total = value()
            else:
                buf, me, count, partner, axis = stages[stage - 1]
                for copy in copies(stage - 1):
                    copy.wait_recv()
                total = buf[0]
                for i in range(1, count):
                    total = total + buf[i]
            if stage == len(stages):
                result[...] = total
                return
            buf, me = stages[stage][:2]
            buf[me] = total
            for copy in copies(stage):
                start(copy)

        return step

    def bufs(piece):
        if piece == VALUE:
            return 0, wbuf_v, gy_v, gx_v, sx_v, sy_v, zs_v, zg_v, fin_v
        return piece, wbuf, gy, gx, sx, sy, zs, zg, fin

    def make(piece):
        i, buf = bufs(piece)[:2]
        count = PLANES * lines * shard
        if piece == OUT:
            arrived(0, 1)
            mine, theirs = lt_a[:, :, core, 0], ltp_a[:, :, 0]
            right, other = branch_ref[...], rp_branch[...]
        elif piece < DOWN:
            arrived(2, 3)
            cols = slice((piece - UP) * width, (piece - UP + 1) * width)
            mine, theirs = lt_n2[:, :, core, 0], ltp_n2[:, :, 0]
            right, other = ug_ref[:, cols], rp_ug[:, cols]
        elif piece < QUERY:
            arrived(4, 5)
            mine, theirs = lt_act[:, :, core, piece - DOWN], ltp_act[:, :, piece - DOWN]
            right, other = dout_ref[...], rp_dout[...]
        else:
            arrived(6, 7)
            at = (piece - QUERY) * width
            cols = slice(at, at + (width // 2 if piece == VALUE else width))
            mine, theirs = lt_n[:, :, core, 0], ltp_n[:, :, 0]
            right, other = late_r[:, cols], rp_late[:, cols]
        grad = dot(mine.reshape(count, rows), right, NN) + dot(theirs.reshape(count, rows), other, NN)
        lanes = grad.shape[1] // groups
        for h in range(groups):
            for zz in range(PLANES):
                for xx in range(lines):
                    at = (zz * lines + xx) * shard
                    buf[i, h, xx, zz] = grad[at : at + shard, h * lanes : (h + 1) * lanes].astype(BF16)
        for copy in first_copies(piece):
            start(copy)

    def first_copies(piece):
        i, buf, gy_b, gx_b = bufs(piece)[:4]
        n = piece
        if piece in LINE_FIRST:
            return [
                remote(
                    buf.at[i, :, lax.rem(column + e, lines)], gx_b.at[i, e - 1],
                    s1send.at[n, e], s1recv.at[n, e], at_x(z, c, plane, e),
                )
                for e in range(1, lines)
            ]
        return [
            remote(
                buf.at[i, lax.rem(group + e, groups)], gy_b.at[i, e - 1],
                s1send.at[n, e], s1recv.at[n, e], at_group(e),
            )
            for e in range(1, groups)
        ]

    def second_copies(piece):
        i, buf, gy_b, gx_b, sx_b, sy_b = bufs(piece)[:6]
        n = piece
        if piece in LINE_FIRST:
            return [
                remote(
                    sy_b.at[i, e - 1], gy_b.at[i, e - 1, 0],
                    s2send.at[n, e], s2recv.at[n, e], at_group(e),
                )
                for e in range(1, groups)
            ]
        return [
            remote(
                sx_b.at[i, e - 1], gx_b.at[i, e - 1, 0],
                s2send.at[n, e], s2recv.at[n, e], at_x(z, c, plane, e),
            )
            for e in range(1, lines)
        ]

    def first_total(piece, at):
        i, buf, gy_b, gx_b = bufs(piece)[:4]
        if piece in LINE_FIRST:
            value = buf[i, at, column].astype(F32)
            for e in range(1, lines):
                value = value + gx_b[i, e - 1, at].astype(F32)
            return value
        value = buf[i, group, at].astype(F32)
        for e in range(1, groups):
            value = value + gy_b[i, e - 1, at].astype(F32)
        return value

    def second(piece):
        i, buf, gy_b, gx_b, sx_b, sy_b = bufs(piece)[:6]
        for copy in first_copies(piece):
            copy.wait_recv()
        if piece in LINE_FIRST:
            for e in range(1, groups):
                sy_b[i, e - 1] = first_total(piece, lax.rem(group + e, groups)).astype(BF16)
        else:
            for e in range(1, lines):
                sx_b[i, e - 1] = first_total(piece, lax.rem(column + e, lines)).astype(BF16)
        for copy in second_copies(piece):
            start(copy)

    def third_copies(piece):
        i = bufs(piece)[0]
        zs_b, zg_b = bufs(piece)[6:8]
        n = piece
        return [
            remote(
                zs_b.at[i, lax.rem(z + d, PLANES)], zg_b.at[i, d - 1],
                wzsend.at[n, d], wzrecv.at[n, d], at_z(z, c, plane, d),
            )
            for d in (2, 1, 3)
        ]

    def third(piece):
        i, buf, gy_b, gx_b, sx_b, sy_b, zs_b, zg_b, fin_b = bufs(piece)
        for copy in second_copies(piece):
            copy.wait_recv()
        value = first_total(piece, group if piece in LINE_FIRST else column)
        if piece in LINE_FIRST:
            for e in range(1, groups):
                value = value + gy_b[i, e - 1, 0].astype(F32)
        else:
            for e in range(1, lines):
                value = value + gx_b[i, e - 1, 0].astype(F32)
        zs_b[i] = value.astype(BF16)
        for copy in third_copies(piece):
            start(copy)

    def last_copies(piece):
        i = bufs(piece)[0]
        fin_b = bufs(piece)[8]
        n = piece
        return [
            remote(fin_b.at[i, group], fin_b.at[i, group], fsend.at[n, e], frecv.at[n, e], at_group(e))
            for e in range(1, groups)
        ]

    def fourth(piece):
        i, buf, gy_b, gx_b, sx_b, sy_b, zs_b, zg_b, fin_b = bufs(piece)
        for copy in third_copies(piece):
            copy.wait_recv()
        value = zs_b[i, z].astype(F32)
        for d in range(1, PLANES):
            value = value + zg_b[i, d - 1].astype(F32)
        fin_b[i, group] = value.astype(BF16)
        for copy in last_copies(piece):
            start(copy)

    def finish(piece):
        for copy in last_copies(piece):
            copy.wait_recv()

    span = min(plane, 4)

    def grads(slot, k):
        held = keybuf.at[slot % 2]
        query = query_rows(held[k, c, rows:, :], True)
        grad = query_rows(drecv[slot, k], False)
        both = jnp.concatenate([query, grad], axis=0)
        turned = jnp.transpose(drecv[slot, k].astype(F32))
        turned = jnp.concatenate([turned[:size], turned[size:]], axis=1)
        delta = jnp.sum(turned * o_ref[slot, k], axis=0, keepdims=True)
        lse = lse_ref[slot, k, 0:1, :]
        query_grad = jnp.zeros((2 * size, rows), F32)
        for k2 in range(k, -1, -1):
            level = lse
            if k2 < k and k == PLANES - 1:
                position = k * plane * rows + c * rows + lax.broadcasted_iota(jnp.int32, (1, rows), 1)
                level = jnp.where(position >= end, -NEG_FILL, lse)
            for at in range(0, plane, span):
                where = slice(at * rows, (at + span) * rows)
                keys = held[k2, at : at + span, :rows, :].reshape(span * rows, 2 * size)
                scores = dot(keys, query, NT)
                prob_grad = dot(keys, grad, NT)
                if k2 == k:
                    scores = scores + masks[k, where, :].astype(F32)
                elif k2 == 0 and at == 0:
                    index = lax.broadcasted_iota(jnp.int32, (span * rows, 1), 0)
                    scores = scores + jnp.where(index < first, NEG_FILL, 0.0)
                prob = jnp.exp(scores - level)
                score_grad = (prob * (prob_grad - delta)).astype(BF16)
                update = dot(jnp.concatenate([score_grad, prob.astype(BF16)], axis=1), both, NN)
                if k2 == k:
                    acc[slot % 2, k2, where] = update
                else:
                    acc[slot % 2, k2, where] += update
                query_grad = query_grad + dot(keys, score_grad, TN)
        packed = jnp.concatenate([query_grad[:size, :half], query_grad[:size, half:]], axis=0)
        ret[k, slot, rows:, :] = jnp.transpose(packed).astype(BF16)

    def mine(slot, k, col):
        return acc[slot % 2, k, pl.ds(pl.multiple_of(col * rows, rows), rows), :]

    def ccopy(slot, line):
        return remote(
            part.at[slot, line], cgot.at[slot, line],
            csend.at[slot, line], crecv.at[slot, line], to_core,
        )

    def xcopy(slot, e):
        return remote(
            xpart.at[slot, e - 1], xgot.at[slot, e - 1],
            xsend.at[slot, e], xrecv.at[slot, e], at_x(z, c, plane, e),
        )

    def rcopy(slot, d):
        return remote(
            ret.at[lax.rem(z + d, PLANES), slot], got.at[slot, z],
            rsend.at[slot, d], rrecv.at[slot, d], at_z(z, c, plane, d),
        )

    def reduce_core(slot):
        for line in range(lines):
            for k in range(PLANES):
                part[slot, line, k] = mine(slot, k, 2 * line + 1 - core).astype(BF16)
            start(ccopy(slot, line))

    def reduce_line(slot):
        for line in range(lines):
            ccopy(slot, line).wait_recv()
        for e in range(1, lines):
            line = lax.rem(column + e, lines)
            for k in range(PLANES):
                xpart[slot, e - 1, k] = (
                    mine(slot, k, 2 * line + core) + cgot[slot, line, k].astype(F32)
                ).astype(BF16)
            start(xcopy(slot, e))

    def reduce_end(slot):
        for e in range(1, lines):
            xcopy(slot, e).wait_recv()
        for k in range(PLANES):
            total = mine(slot, k, c) + cgot[slot, column, k].astype(F32)
            for e in range(1, lines):
                total = total + xgot[slot, e - 1, k].astype(F32)
            ret[k, slot, :rows, :] = total.astype(BF16)
        for d in (2, 1, 3):
            start(rcopy(slot, d))
        got[slot, z] = ret[z, slot]

    def late_factors():
        for slot in range(SLOTS):
            for d in range(1, PLANES):
                rcopy(slot, d).wait_recv()
        for pair in range(HEADS // 2):
            at = pair * 2 * size
            keys, values, queries = [], [], []
            for head in (2 * pair, 2 * pair + 1):
                src, slot = divmod(head, SLOTS)
                block = got[slot, src].astype(F32)
                keys.append(block[:rows, :size])
                values.append(block[:rows, size:])
                queries.append(jnp.concatenate([block[rows:, :size], block[rows:, size:]], axis=0))
            late_r[:, at : at + 2 * size] = (jnp.concatenate(queries, axis=1) * 0.125).astype(BF16)
            late_r[:, width + at : width + at + 2 * size] = jnp.concatenate(keys, axis=1).astype(BF16)
            if pair < HEADS // 4:
                at = 2 * width + at
                late_r[:, at : at + 2 * size] = jnp.concatenate(values, axis=1).astype(BF16)
            else:
                at = at - width // 2
                gfv_ref[:, at : at + 2 * size] = jnp.concatenate(values, axis=1).astype(BF16)
    def input_grad():
        normed_grad = (
            dot(late_r[:, :width], wq_ref[...], NT)
            + dot(late_r[:, width : 2 * width], wk_ref[...], NT)
            + dot(late_r[:, 2 * width :], wv_ref[...], NT)
        )
        values = x_ref[...].astype(F32)
        centred = values - jnp.mean(values, axis=-1, keepdims=True)
        scale = lax.rsqrt(jnp.mean(centred * centred, axis=-1, keepdims=True) + EPSILON)
        unit = centred * scale
        inner = normed_grad * g_ref[...].reshape(1, width)
        back = scale * (
            inner
            - jnp.mean(inner, axis=-1, keepdims=True)
            - unit * jnp.mean(inner * unit, axis=-1, keepdims=True)
        )
        gin_ref[...] = hg_ref[...] + back

        def sums(v):
            return jnp.sum(v.astype(F32), axis=0, keepdims=True)

        return jnp.concatenate(
            [
                sums(normed_grad * unit),
                sums(normed_grad),
                sums(late_r[:, :width]),
                jnp.concatenate([sums(late_r[:, 2 * width :]), jnp.zeros((1, width // 2), F32)], axis=1),
                jnp.zeros((4, width), F32),
            ],
            axis=0,
        )

    def do(*tasks):
        for stage, what in tasks if weights else ():
            (make, second, third, fourth, finish)[stage - 1](what)

    do(*BEFORE)
    if attention:
        for slot in range(SLOTS):
            key_copy(slot).wait()
            arrive(slot)
            for k in range(PLANES):
                grads(slot, k)
                if slot and k == 1:
                    reduce_line(slot - 1)
                do(*AT_POINTS.get((slot, k), ()))
            if slot == 0:
                key_copy(2).start()
            reduce_core(slot)
            if slot:
                reduce_end(slot - 1)
    else:
        for tasks in AT_POINTS.values():
            do(*tasks)
    do(*AFTER[0])
    if attention:
        reduce_line(SLOTS - 1)
    do(*AFTER[1])
    if attention:
        reduce_end(SLOTS - 1)
    do(*AFTER[2])
    if attention:
        late_factors()
    if weights:
        swap(7, late_r, rp_late)
        partial = input_grad()
        late_vectors = vectors(lambda: jnp.concatenate([vec_ref[...], partial], axis=0), vec1_ref)
        late_vectors(0)
        for stage, tasks in enumerate(AFTER[3:]):
            do(*tasks)
            if stage < 4:
                late_vectors(stage + 1)
    arrived(*range(8))
    for copy in sent:
        copy.wait_send()


BEFORE = ((1, OUT),)
AT_POINTS = {
    (0, 1): ((1, UP + 2), (1, DOWN)),
    (1, 0): ((2, OUT),),
    (1, 1): ((1, DOWN + 3), (2, UP + 2)),
    (1, 2): ((1, UP + 3), (3, OUT), (1, UP)),
    (2, 1): ((2, DOWN + 3), (2, DOWN)),
    (2, 2): ((3, UP + 2),),
}
AFTER = (
    (),
    ((2, UP), (1, UP + 1), (4, OUT), (1, DOWN + 2)),
    ((1, DOWN + 1), (2, UP + 1), (3, DOWN + 3), (2, DOWN + 1), (3, DOWN), (4, UP + 2)),
    ((3, UP + 1), (3, UP), (2, UP + 3), (1, QUERY)),
    ((1, KEY), (3, DOWN + 1)),
    ((4, DOWN), (2, DOWN + 2), (4, UP + 1), (1, VALUE)),
    ((2, QUERY), (3, DOWN + 2), (3, UP + 3)),
    (
        (4, DOWN + 1), (5, UP + 2), (4, DOWN + 3), (2, KEY), (2, VALUE), (3, QUERY), (3, KEY), (3, VALUE), (4, UP),
        (4, UP + 3), (4, DOWN + 2), (4, QUERY), (4, KEY), (4, VALUE), (5, OUT), (5, UP), (5, UP + 1), (5, UP + 3),
        (5, DOWN), (5, DOWN + 1), (5, DOWN + 2), (5, DOWN + 3), (5, QUERY), (5, KEY), (5, VALUE),
    ),
)


def backward_call(plane, groups, rows, width, hidden, attention, weights, arrays):
    blocks = plane * PLANES
    lines = plane // 2
    size = width // HEADS
    half = rows // 2
    shard = width // blocks
    tall = hidden // width
    lw = width // groups
    lv = width // 2 // groups
    late = 2 * width + width // 2
    count = PIECES
    dma = pltpu.SemaphoreType.DMA
    most = max(groups, lines)

    def vmem(*shape):
        return pltpu.VMEM(shape, BF16)

    def vmem32(*shape):
        return pltpu.VMEM(shape, F32)

    ins = {}
    outs = {}
    scratch = {}
    if attention:
        ins.update(mg_ref=VMEM, all_ref=pl.BlockSpec(memory_space=pl.ANY), o_ref=VMEM, lse_ref=VMEM, spans_ref=SMEM)
        outs.update(gfv_ref=((rows, width // 2), BF16))
        scratch.update(
            dpack=vmem(PLANES, SLOTS, half, 2 * size),
            drecv=vmem(SLOTS, PLANES, half, 2 * size),
            masks=vmem(PLANES, plane * rows, rows),
            acc=vmem32(2, PLANES, plane * rows, 2 * size),
            part=vmem(SLOTS, lines, PLANES, rows, 2 * size),
            cgot=vmem(SLOTS, lines, PLANES, rows, 2 * size),
            xpart=vmem(SLOTS, lines - 1, PLANES, rows, 2 * size),
            xgot=vmem(SLOTS, lines - 1, PLANES, rows, 2 * size),
            ret=vmem(PLANES, SLOTS, rows + half, 2 * size),
            got=vmem(SLOTS, PLANES, rows + half, 2 * size),
            keybuf=vmem(2, PLANES, plane, rows + half, 2 * size),
            keysem=dma((2,)),
            zsend=dma((SLOTS, PLANES)), zrecv=dma((SLOTS, PLANES)),
            csend=dma((SLOTS, lines)), crecv=dma((SLOTS, lines)),
            xsend=dma((SLOTS, lines)), xrecv=dma((SLOTS, lines)),
            rsend=dma((SLOTS, PLANES)), rrecv=dma((SLOTS, PLANES)),
        )
        if weights:
            scratch.update(late_own=vmem(rows, late))
        else:
            outs.update(late_out=((rows, late), BF16))
    if weights:
        ins.update(
            lt_a=VMEM, lt_n2=VMEM, lt_act=VMEM, lt_n=VMEM, branch_ref=VMEM, ug_ref=VMEM, dout_ref=VMEM, vec_ref=VMEM,
            x_ref=VMEM, g_ref=VMEM, hg_ref=VMEM, wq_ref=VMEM, wk_ref=VMEM, wv_ref=VMEM,
        )
        if not attention:
            ins.update(late_in=VMEM)
        outs.update(
            gin_ref=((rows, width), F32), vec1_ref=((16, width), F32),
            fin=((count - 1, groups, shard, lw), BF16), fin_v=((1, groups, shard, lv), BF16),
        )
        scratch.update(
            ltp_a=vmem(PLANES, lines, 1, shard, rows),
            ltp_n2=vmem(PLANES, lines, 1, shard, rows),
            ltp_act=vmem(PLANES, lines, tall, shard, rows),
            ltp_n=vmem(PLANES, lines, 1, shard, rows),
            rp_branch=vmem(rows, width), rp_ug=vmem(rows, hidden), rp_dout=vmem(rows, width), rp_late=vmem(rows, late),
            vbuf_c=vmem32(2, 16, width), vbuf_x=vmem32(lines, 16, width),
            vbuf_y=vmem32(groups, 16, width), vbuf_z=vmem32(PLANES, 16, width),
            esend=dma((8,)), erecv=dma((8,)),
            s1send=dma((count, most)), s1recv=dma((count, most)),
            s2send=dma((count, most)), s2recv=dma((count, most)),
            wzsend=dma((count, PLANES)), wzrecv=dma((count, PLANES)),
            fsend=dma((count, groups)), frecv=dma((count, groups)),
            vsend=dma((4, max(most, PLANES))), vrecv=dma((4, max(most, PLANES))),
        )
        for tag, n, lanes in (("", count - 1, lw), ("_v", 1, lv)):
            scratch.update({
                "wbuf" + tag: vmem(n, groups, lines, PLANES, shard, lanes),
                "gy" + tag: vmem(n, groups - 1, lines, PLANES, shard, lanes),
                "gx" + tag: vmem(n, lines - 1, groups if LINE_FIRST else 1, PLANES, shard, lanes),
                "sx" + tag: vmem(n, lines - 1, PLANES, shard, lanes),
                "zs" + tag: vmem(n, PLANES, shard, lanes),
                "zg" + tag: vmem(n, PLANES - 1, shard, lanes),
            })
            if LINE_FIRST:
                scratch["sy" + tag] = vmem(n, groups - 1, PLANES, shard, lanes)
    names = tuple(ins) + tuple(outs) + tuple(scratch)
    result = pl.pallas_call(
        functools.partial(backward_kernel, plane, groups, shard, names, attention, weights),
        name="backward",
        out_shape=tuple(jax.ShapeDtypeStruct(*v) for v in outs.values()),
        in_specs=list(ins.values()),
        out_specs=(VMEM,) * len(outs),
        scratch_shapes=list(scratch.values()),
        compiler_params=pltpu.CompilerParams(
            collective_id=2 if attention else 3, has_side_effects=True, vmem_limit_bytes=61 << 20
        ),
    )(*[arrays[name] for name in ins])
    return dict(zip(outs, result))


def tail_kernel(
    gin_ref, gfv_ref, vec1_ref, fin_ref, finv_ref,
    o_gin, o_gfv, o_g1, o_s1, o_wq, o_bq, o_wk, o_wv, o_bv, o_wo, o_bo, o_g2, o_s2, o_wu, o_bu, o_wd, o_bd,
):
    groups, shard, lanes = fin_ref.shape[1:]
    width = groups * lanes
    tall = o_wd.shape[0] // shard
    o_gin[...] = gin_ref[...]
    o_gfv[...] = gfv_ref[...]

    def put(ref, rows, at, piece):
        for h in range(groups):
            ref[rows, at + h * lanes : at + (h + 1) * lanes] = fin_ref[piece, h].astype(F32)

    everything = slice(0, shard)
    put(o_wo, everything, 0, OUT)
    put(o_wq, everything, 0, QUERY)
    put(o_wk, everything, 0, KEY)
    for i in range(tall):
        put(o_wu, everything, i * width, UP + i)
        put(o_wd, slice(i * shard, (i + 1) * shard), 0, DOWN + i)
    for h in range(groups):
        o_wv[:, h * (lanes // 2) : (h + 1) * (lanes // 2)] = finv_ref[0, h].astype(F32)
    o_g2[...], o_s2[...], o_bo[...], o_bd[...] = vec1_ref[0], vec1_ref[1], vec1_ref[2], vec1_ref[3 + tall]
    for i in range(tall):
        o_bu[i * width : (i + 1) * width] = vec1_ref[3 + i]
    o_g1[...], o_s1[...], o_bq[...] = vec1_ref[8], vec1_ref[9], vec1_ref[10]
    o_bv[...] = vec1_ref[11, : width // 2]


def tail_part(rows, width, hidden, shard, got):
    def out(*shape):
        return jax.ShapeDtypeStruct(shape, F32)

    return pl.pallas_call(
        tail_kernel,
        name="tail",
        out_shape=(
            out(rows, width), jax.ShapeDtypeStruct((rows, width // 2), BF16), out(width), out(width),
            out(shard, width), out(width), out(shard, width), out(shard, width // 2), out(width // 2),
            out(shard, width), out(width), out(width), out(width),
            out(shard, hidden), out(hidden), out(hidden // width * shard, width), out(width),
        ),
        in_specs=[VMEM] * 5,
        out_specs=(VMEM,) * 17,
    )(*got)


def body(
    inputs,
    first_values,
    spans,
    ln1_gain,
    ln1_shift,
    w_query,
    b_query,
    w_key,
    w_value,
    b_value,
    w_out,
    b_out,
    ln2_gain,
    ln2_shift,
    w_up,
    b_up,
    w_down,
    b_down,
    out_grad,
):
    rows, width = inputs.shape
    hidden = w_up.shape[1]
    groups = lax.axis_size("grp")
    plane = lax.axis_size("blk") // PLANES
    attended, normed, all_blocks, mixed, lse = forward_part(
        inputs, first_values, spans, ln1_gain, ln1_shift, w_query, b_query, w_key, w_value, b_value
    )
    result, mixed_grad, hidden_grad, branch_grad, upper_grad, grad_down, vectors, lt_a, lt_n2, lt_act, lt_n = middle_part(
        plane, inputs, attended, normed, spans, out_grad, b_out, ln2_gain, ln2_shift, b_up, b_down, w_out, w_up, w_down
    )
    arrays = dict(
        mg_ref=mixed_grad, all_ref=all_blocks, o_ref=mixed, lse_ref=lse, spans_ref=spans,
        lt_a=lt_a, lt_n2=lt_n2, lt_act=lt_act, lt_n=lt_n,
        branch_ref=branch_grad, ug_ref=upper_grad, dout_ref=grad_down, vec_ref=vectors,
        x_ref=inputs, g_ref=ln1_gain, hg_ref=hidden_grad, wq_ref=w_query, wk_ref=w_key, wv_ref=w_value,
    )
    call = functools.partial(backward_call, plane, groups, rows, width, hidden)
    if plane <= 4:
        got = Refs(call(True, True, arrays))
    else:
        got = Refs(call(True, False, arrays))
        arrays.update(late_in=got.late_out)
        got.update(call(False, True, arrays))
    return (result,) + tuple(
        tail_part(
            rows, width, hidden, width // (plane * PLANES),
            (got.gin_ref, got.gfv_ref, got.vec1_ref, got.fin, got.fin_v),
        )
    )


def solution(mesh):
    placed = (
        P(("grp", "blk"), None),
        P(("grp", "blk"), None),
        P("grp", None),
        P(),
        P(),
        P(),
        P(),
        P(),
        P(),
        P(),
        P(),
        P(),
        P(),
        P(),
        P(),
        P(),
        P(),
        P(),
        P(("grp", "blk"), None),
    )
    return jax.shard_map(
        body,
        mesh=mesh,
        in_specs=placed,
        out_specs=(
            P(("grp", "blk"), None),
            P(("grp", "blk"), None),
            P(("grp", "blk"), None),
            P(),
            P(),
            P("blk", None),
            P(),
            P("blk", None),
            P("blk", None),
            P(),
            P("blk", None),
            P(),
            P(),
            P(),
            P("blk", None),
            P(),
            P("blk", None),
            P(),
        ),
        check_vma=False,
    )
```

```python
import functools

import jax
import jax.numpy as jnp
from jax import lax
from jax.experimental import pallas as pl
from jax.experimental.pallas import tpu as pltpu
from jax.sharding import PartitionSpec as P

HEADS = 12
PLANES = 4
SLOTS = HEADS // PLANES
EPSILON = 1e-05
GELU_COEF = 0.7978845608028654
NEG_FILL = -1e30
BF16 = jnp.bfloat16
F32 = jnp.float32
MESH = pl.DeviceIdType.MESH
VMEM = pl.BlockSpec(memory_space=pltpu.VMEM)
SMEM = pl.BlockSpec(memory_space=pltpu.SMEM)


def dot(a, b, dims):
    return lax.dot_general(a, b, (dims, ((), ())), preferred_element_type=F32)


NN = ((1,), (0,))
NT = ((1,), (1,))
TN = ((0,), (0,))


def norm_rows(values, gain, shift):
    average = jnp.mean(values, axis=-1, keepdims=True)
    centred = values - average
    variance = jnp.mean(centred * centred, axis=-1, keepdims=True)
    return centred * lax.rsqrt(variance + EPSILON) * gain + shift


def place(plane):
    block = lax.axis_index("blk")
    return block // plane, lax.rem(block, plane)


def at_z(z, c, plane, offset):
    return {"blk": lax.rem(z + offset, PLANES) * plane + c}


def at_x(z, c, plane, offset):
    lines = plane // 2
    column, core = c // 2, lax.rem(c, 2)
    return {"blk": z * plane + lax.rem(column + offset, lines) * 2 + core}


def at_core(z, c, plane):
    return {"blk": z * plane + (c // 2) * 2 + 1 - lax.rem(c, 2)}


def greet(partners):
    barrier = pltpu.get_barrier_semaphore()
    for partner in partners:
        pl.semaphore_signal(barrier, inc=1, device_id=partner, device_id_type=MESH)
    pl.semaphore_wait(barrier, len(partners))


def remote(src, dst, send, recv, partner):
    return pltpu.make_async_remote_copy(
        src_ref=src, dst_ref=dst, send_sem=send, recv_sem=recv,
        device_id=partner, device_id_type=MESH,
    )


def query_rows(pack, first):
    half = pack.shape[1] // 2
    lanes = lax.broadcasted_iota(jnp.int32, pack.shape, 1)
    wide = pack.astype(F32)
    other = pltpu.roll(wide, half, 1)
    keep = lanes < half if first else lanes >= half
    top, bottom = (wide, other) if first else (other, wide)
    return jnp.concatenate(
        [jnp.where(keep, top, 0.0), jnp.where(keep, bottom, 0.0)], axis=0
    ).astype(BF16)


def position_masks(spans_ref, plane, length, c, k, rows):
    first, end = spans_ref[0, 0], length - spans_ref[0, 1]
    dead = end - spans_ref[0, 2]
    width = plane * rows
    key = k * width + lax.broadcasted_iota(jnp.int32, (width, rows), 0)
    query = k * width + c * rows + lax.broadcasted_iota(jnp.int32, (width, rows), 1)
    allowed = key <= query
    if k == 0:
        allowed &= ((key >= first) == (query >= first))
    if k == PLANES - 1:
        allowed &= ((key >= end) == (query >= end)) & ((key < dead) | (key >= end))
    return jnp.where(allowed, 0.0, NEG_FILL)


def forward_kernel(
    plane, x_ref, fv_ref, spans_ref, g_ref, s_ref, wq_ref, bq_ref, wk_ref, wv_ref, bv_ref,
    att_ref, normed_ref, all_ref, o_ref, lse_ref,
    pack, opack, orecv, masks,
    zsend, zrecv, xsend, xrecv, csend, crecv, osend, orecv_sem,
):
    rows, width = x_ref.shape
    size = width // HEADS
    lines = plane // 2
    length = rows * plane * PLANES
    half = rows // 2
    z, c = place(plane)
    core = lax.rem(c, 2)
    greet(
        [at_z(z, c, plane, d) for d in range(1, PLANES)]
        + [at_x(z, c, plane, d) for d in range(1, lines)]
        + [at_core(z, c, plane)]
    )
    normed = norm_rows(
        x_ref[...].astype(F32), g_ref[...].reshape(1, width), s_ref[...].reshape(1, width)
    ).astype(BF16)
    normed_ref[...] = normed
    query = ((dot(normed, wq_ref[...], NN) + bq_ref[...].reshape(1, width)) * 0.125)
    key = dot(normed, wk_ref[...], NN)
    fresh = dot(normed, wv_ref[...], NN) + bv_ref[...].reshape(1, width // 2)
    value = jnp.concatenate([fresh, fv_ref[...].astype(F32)], axis=1)
    for head in range(HEADS):
        to, slot = divmod(head, SLOTS)
        cols = slice(head * size, (head + 1) * size)
        pack[to, slot, :rows, :] = jnp.concatenate(
            [key[:, cols], value[:, cols]], axis=1
        ).astype(BF16)
        pack[to, slot, rows:, :] = jnp.concatenate(
            [query[:half, cols], query[half:, cols]], axis=1
        ).astype(BF16)

    zcopies = {}
    for slot in range(SLOTS):
        for d in (2, 1, 3):
            to = lax.rem(z + d, PLANES)
            copy = remote(
                pack.at[to, slot], all_ref.at[slot, z, c],
                zsend.at[slot, d], zrecv.at[slot, d], at_z(z, c, plane, d),
            )
            copy.start()
            zcopies[slot, d] = copy
        all_ref[slot, z, c] = pack[z, slot]

    started = []

    def hand_out(slot, d):
        block = all_ref.at[slot, lax.rem(z + PLANES - d, PLANES), c, pl.ds(0, rows)]
        for e in range(1, lines):
            copy = remote(
                block, block, xsend.at[slot, d, e], xrecv.at[slot, d, e], at_x(z, c, plane, e)
            )
            copy.start()
            started.append(copy)
        copy = remote(block, block, csend.at[slot, d, 0], crecv.at[slot, d, 0], at_core(z, c, plane))
        copy.start()
        started.append(copy)

    for slot in range(SLOTS):
        hand_out(slot, 0)
    for k in range(PLANES):
        masks[k] = position_masks(spans_ref, plane, length, c, k, rows)
    first, end = spans_ref[0, 0], length - spans_ref[0, 1]

    def spread(slot):
        for d in (1, 3, 2):
            zcopies[slot, d].wait_recv()
            hand_out(slot, d)

    def pass_on(slot):
        for d in (0, 1, 3, 2):
            src = lax.rem(z + PLANES - d, PLANES)
            for e in range(1, lines):
                column = lax.rem(c // 2 + lines - e, lines) * 2 + core
                block = all_ref.at[slot, src, column, pl.ds(0, rows)]
                remote(
                    block, block, xsend.at[slot, d, e], xrecv.at[slot, d, e], at_x(z, c, plane, e)
                ).wait_recv()
                copy = remote(
                    block, block, csend.at[slot, d, e], crecv.at[slot, d, e], at_core(z, c, plane)
                )
                copy.start()
                started.append(copy)

    def settle(slot):
        for d in range(PLANES):
            for e in range(lines):
                block = all_ref.at[slot, 0, c, pl.ds(0, rows)]
                remote(
                    block, block, csend.at[slot, d, e], crecv.at[slot, d, e], at_core(z, c, plane)
                ).wait_recv()

    def keys_of(slot, k):
        return all_ref[slot, k, :, :rows, :].reshape(plane * rows, 2 * size)

    def attend(slot, k):
        q = query_rows(all_ref[slot, k, c, rows:, :], True)

        def step(state, k2, bias):
            top, total, acc = state
            count = plane
            blocks = [all_ref[slot, k2, b, :rows, :] for b in range(count)]
            scores = [bias(dot(blocks[b], q, NT), b) for b in range(count)]
            new = top
            for part in scores:
                new = jnp.maximum(new, jnp.max(part, axis=0, keepdims=True))
            scale = jnp.exp(top - new)
            total, acc = total * scale, acc * scale
            for b in range(count):
                prob = jnp.exp(scores[b] - new)
                total = total + jnp.sum(prob, axis=0, keepdims=True)
                acc = acc + dot(blocks[b], prob.astype(BF16), TN)
            return new, total, acc

        state = (
            jnp.full((1, rows), NEG_FILL, F32),
            jnp.zeros((1, rows), F32),
            jnp.zeros((2 * size, rows), F32),
        )
        state = step(state, k, lambda t, b: t + masks[k, b * rows : (b + 1) * rows])
        diagonal = state
        for k2 in range(k):
            if k2 == 0:
                index = lax.broadcasted_iota(jnp.int32, (rows, 1), 0)
                shut = jnp.where(index < first, NEG_FILL, 0.0)
                state = step(state, k2, lambda t, b: t + shut if b == 0 else t)
            else:
                state = step(state, k2, lambda t, b: t)
        if k == PLANES - 1:
            position = k * plane * rows + c * rows + lax.broadcasted_iota(jnp.int32, (1, rows), 1)
            after = position >= end
            state = tuple(jnp.where(after, old, new) for old, new in zip(diagonal, state))
        top, total, acc = state
        mixed = acc[size:] / total
        o_ref[slot, k] = mixed
        lse_ref[slot, k] = jnp.broadcast_to(top + jnp.log(total), (8, rows))
        packed = jnp.concatenate([mixed[:, :half], mixed[:, half:]], axis=0)
        opack[slot, k] = jnp.transpose(packed).astype(BF16)

    def back(slot, k, src):
        return remote(
            opack.at[slot, k], orecv.at[slot, src],
            osend.at[slot, k], orecv_sem.at[slot, src], {"blk": k * plane + c},
        )

    def give_back(slot, k):
        @pl.when(z == k)
        def _():
            orecv[slot, k] = opack[slot, k]

        @pl.when(z != k)
        def _():
            back(slot, k, z).start()

    spread(0)
    pass_on(0)
    settle(0)
    spread(1)
    for slot in range(SLOTS):
        if slot:
            settle(slot)
        for k in range(PLANES - 1, -1, -1):
            attend(slot, k)
            give_back(slot, k)
        if slot + 2 < SLOTS:
            spread(slot + 2)
        if slot + 1 < SLOTS:
            pass_on(slot + 1)
    for slot in range(SLOTS):
        for k in range(PLANES):
            @pl.when(z != k)
            def _(slot=slot, k=k):
                back(slot, 0, k).wait_recv()
    for pair in range(HEADS // 2):
        parts = []
        for head in (2 * pair, 2 * pair + 1):
            src, slot = divmod(head, SLOTS)
            got = orecv[slot, src].astype(F32)
            parts.append(jnp.concatenate([got[:, :size], got[:, size:]], axis=0))
        att_ref[:, pair * 2 * size : (pair + 1) * 2 * size] = jnp.concatenate(parts, axis=1).astype(BF16)
    for slot in range(SLOTS):
        for k in range(PLANES):
            @pl.when(z != k)
            def _(slot=slot, k=k):
                back(slot, k, 0).wait_send()
    for copy in list(zcopies.values()) + started:
        copy.wait_send()


def forward_part(inputs, first_values, spans, ln1_gain, ln1_shift, w_query, b_query, w_key, w_value, b_value):
    rows, width = inputs.shape
    plane = lax.axis_size("blk") // PLANES
    lines = plane // 2
    size = width // HEADS
    half = rows // 2
    dma = pltpu.SemaphoreType.DMA
    return pl.pallas_call(
        functools.partial(forward_kernel, plane),
        name="forward",
        out_shape=(
            jax.ShapeDtypeStruct((rows, width), BF16),
            jax.ShapeDtypeStruct((rows, width), BF16),
            jax.ShapeDtypeStruct((SLOTS, PLANES, plane, rows + half, 2 * size), BF16),
            jax.ShapeDtypeStruct((SLOTS, PLANES, size, rows), F32),
            jax.ShapeDtypeStruct((SLOTS, PLANES, 8, rows), F32),
        ),
        in_specs=[VMEM, VMEM, SMEM] + [VMEM] * 7,
        out_specs=(VMEM,) * 5,
        scratch_shapes=[
            pltpu.VMEM((PLANES, SLOTS, rows + half, 2 * size), BF16),
            pltpu.VMEM((SLOTS, PLANES, half, 2 * size), BF16),
            pltpu.VMEM((SLOTS, PLANES, half, 2 * size), BF16),
            pltpu.VMEM((PLANES, plane * rows, rows), F32),
            dma((SLOTS, PLANES)), dma((SLOTS, PLANES)),
            dma((SLOTS, PLANES, lines)), dma((SLOTS, PLANES, lines)),
            dma((SLOTS, PLANES, lines)), dma((SLOTS, PLANES, lines)),
            dma((SLOTS, PLANES)), dma((SLOTS, PLANES)),
        ],
        compiler_params=pltpu.CompilerParams(
            collective_id=1, has_side_effects=True, vmem_limit_bytes=56 << 20
        ),
    )(
        inputs, first_values, spans, ln1_gain, ln1_shift, w_query, b_query, w_key, w_value, b_value,
    )


def middle_kernel(
    x_ref, att_ref, normed_ref, spans_ref, og_ref, bo_ref, g_ref, s_ref, bu_ref, bd_ref,
    wo_hbm, wu_hbm, wd_hbm,
    result_ref, mg_ref, hg_ref, branch_ref, ug_ref, dout_ref, vec_ref, lt_a, lt_n2, lt_act, lt_n,
    wo_ref, wu_ref, wd_ref, sem,
):
    rows, width = x_ref.shape
    tall = bu_ref.shape[0] // width
    shard = lt_a.shape[4]
    copies = [
        pltpu.make_async_copy(src, dst, sem.at[i])
        for i, (src, dst) in enumerate(((wo_hbm, wo_ref), (wu_hbm, wu_ref), (wd_hbm, wd_ref)))
    ]
    for copy in copies:
        copy.start()

    def turn(value, dst, piece):
        turned = jnp.transpose(value.astype(F32)).astype(BF16)
        at = 0
        span = width // (dst.shape[0] * dst.shape[1] * 2)
        if dst.shape[3] == 1:
            for zz in range(dst.shape[0]):
                for xx in range(dst.shape[1]):
                    for cc in range(2):
                        dst[zz, xx, cc, 0] = turned[at : at + span]
                        at += span
            return
        per = dst.shape[3]
        for unit in range(width // span):
            index = piece * (width // span) + unit
            owner, part = divmod(index, per)
            chip, cc = divmod(owner, 2)
            zz, xx = divmod(chip, dst.shape[1])
            dst[zz, xx, cc, part] = turned[unit * span : (unit + 1) * span]

    def sums(value):
        return jnp.sum(value.astype(F32), axis=0, keepdims=True)

    block = lax.axis_index("blk")
    length = rows * lax.axis_size("blk")
    end = length - spans_ref[0, 1]
    position = block * rows + lax.broadcasted_iota(jnp.int32, (rows, 1), 0)
    alive = (position < end - spans_ref[0, 2]) | (position >= end)
    dout = jnp.where(alive, og_ref[...].astype(F32), 0.0)
    dout_low = dout.astype(BF16)
    dout_ref[...] = dout_low
    vec_ref[3 + tall : 4 + tall, :] = sums(dout)
    attended = att_ref[...]
    turn(normed_ref[...], lt_n, 0)
    turn(attended, lt_a, 0)
    copies[0].wait()
    hidden = x_ref[...].astype(F32) + dot(attended, wo_ref[...], NN) + bo_ref[...].reshape(1, width)
    average = jnp.mean(hidden, axis=-1, keepdims=True)
    centred = hidden - average
    scale = lax.rsqrt(jnp.mean(centred * centred, axis=-1, keepdims=True) + EPSILON)
    unit = centred * scale
    gain = g_ref[...].reshape(1, width)
    normed2 = (unit * gain + s_ref[...].reshape(1, width)).astype(BF16)
    turn(normed2, lt_n2, 0)
    copies[1].wait()
    copies[2].wait()
    result = hidden + bd_ref[...].reshape(1, width)
    normed2_grad = jnp.zeros((rows, width), F32)
    for i in range(tall):
        cols = slice(i * width, (i + 1) * width)
        upper = dot(normed2, wu_ref[:, cols], NN) + bu_ref[cols].reshape(1, width)
        square = upper * upper
        curve = jnp.tanh(GELU_COEF * (upper + 0.044715 * upper * square))
        half = 0.5 * (1.0 + curve)
        active = (upper * half).astype(BF16)
        slope = half + 0.5 * upper * (1.0 - curve * curve) * (GELU_COEF * (1.0 + 3.0 * 0.044715 * square))
        turn(active, lt_act, i)
        result = result + dot(active, wd_ref[cols, :], NN)
        upper_grad = (dot(dout_low, wd_ref[cols, :], NT) * slope).astype(BF16)
        ug_ref[:, cols] = upper_grad
        vec_ref[3 + i : 4 + i, :] = sums(upper_grad)
        normed2_grad = normed2_grad + dot(upper_grad, wu_ref[:, cols], NT)
    result_ref[...] = result
    vec_ref[0:1, :] = sums(normed2_grad * unit)
    vec_ref[1:2, :] = sums(normed2_grad)
    inner = normed2_grad * gain
    back = scale * (
        inner - jnp.mean(inner, axis=-1, keepdims=True) - unit * jnp.mean(inner * unit, axis=-1, keepdims=True)
    )
    hidden_grad = dout + back
    hg_ref[...] = hidden_grad
    branch = hidden_grad.astype(BF16)
    branch_ref[...] = branch
    vec_ref[2:3, :] = sums(branch)
    mg_ref[...] = dot(branch, wo_ref[...], NT).astype(BF16)


def middle_part(plane, inputs, attended, normed, spans, out_grad, b_out, gain, shift, b_up, b_down, w_out, w_up, w_down):
    rows, width = inputs.shape
    hidden = w_up.shape[1]
    tall = hidden // width
    lines = plane // 2
    shard = width // (plane * PLANES)

    def low(*shape):
        return jax.ShapeDtypeStruct(shape, BF16)

    any_space = pl.BlockSpec(memory_space=pl.ANY)
    return pl.pallas_call(
        middle_kernel,
        name="middle",
        out_shape=(
            jax.ShapeDtypeStruct((rows, width), F32), low(rows, width), jax.ShapeDtypeStruct((rows, width), F32),
            low(rows, width), low(rows, hidden), low(rows, width), jax.ShapeDtypeStruct((4 + tall, width), F32),
            low(PLANES, lines, 2, 1, shard, rows), low(PLANES, lines, 2, 1, shard, rows),
            low(PLANES, lines, 2, tall, shard, rows), low(PLANES, lines, 2, 1, shard, rows),
        ),
        in_specs=[VMEM, VMEM, VMEM, SMEM] + [VMEM] * 6 + [any_space] * 3,
        out_specs=(VMEM,) * 11,
        scratch_shapes=[
            pltpu.VMEM((width, width), BF16), pltpu.VMEM((width, hidden), BF16), pltpu.VMEM((hidden, width), BF16),
            pltpu.SemaphoreType.DMA((3,)),
        ],
        compiler_params=pltpu.CompilerParams(vmem_limit_bytes=56 << 20),
    )(inputs, attended, normed, spans, out_grad, b_out, gain, shift, b_up, b_down, w_out, w_up, w_down)


OUT, UP, DOWN, QUERY, KEY, VALUE = 0, 1, 5, 9, 10, 11
PIECES = 12
LINE_FIRST = frozenset((OUT, DOWN, DOWN + 1, VALUE))


class Refs(dict):
    __getattr__ = dict.get


def backward_kernel(plane, groups, shard, names, attention, weights, *refs):
    r = Refs(zip(names, refs, strict=True))
    mg_ref, all_ref, o_ref, lse_ref, spans_ref, lt_a, lt_n2, lt_act = r.mg_ref, r.all_ref, r.o_ref, r.lse_ref, r.spans_ref, r.lt_a, r.lt_n2, r.lt_act
    lt_n, branch_ref, ug_ref, dout_ref, vec_ref, x_ref, g_ref, hg_ref = r.lt_n, r.branch_ref, r.ug_ref, r.dout_ref, r.vec_ref, r.x_ref, r.g_ref, r.hg_ref
    wq_ref, wk_ref, wv_ref, late_in, gin_ref, gfv_ref, vec1_ref = r.wq_ref, r.wk_ref, r.wv_ref, r.late_in, r.gin_ref, r.gfv_ref, r.vec1_ref
    late_out, dpack = r.late_out, r.dpack
    drecv, masks, acc, part, cgot, xpart, xgot, ret = r.drecv, r.masks, r.acc, r.part, r.cgot, r.xpart, r.xgot, r.ret
    got, keybuf, keysem, ltp_a, ltp_n2, ltp_act, ltp_n, rp_branch = r.got, r.keybuf, r.keysem, r.ltp_a, r.ltp_n2, r.ltp_act, r.ltp_n, r.rp_branch
    rp_ug, rp_dout, late_own, rp_late, wbuf, gy, gx, sx = r.rp_ug, r.rp_dout, r.late_own, r.rp_late, r.wbuf, r.gy, r.gx, r.sx
    sy, zs, zg, fin, wbuf_v, gy_v, gx_v, sx_v = r.sy, r.zs, r.zg, r.fin, r.wbuf_v, r.gy_v, r.gx_v, r.sx_v
    sy_v, zs_v, zg_v, fin_v, vbuf_c, vbuf_x, vbuf_y, vbuf_z = r.sy_v, r.zs_v, r.zg_v, r.fin_v, r.vbuf_c, r.vbuf_x, r.vbuf_y, r.vbuf_z
    zsend, zrecv, csend, crecv, xsend, xrecv, rsend, rrecv = r.zsend, r.zrecv, r.csend, r.crecv, r.xsend, r.xrecv, r.rsend, r.rrecv
    esend, erecv, s1send, s1recv, s2send, s2recv, wzsend, wzrecv = r.esend, r.erecv, r.s1send, r.s1recv, r.s2send, r.s2recv, r.wzsend, r.wzrecv
    fsend, frecv, vsend, vrecv = r.fsend, r.frecv, r.vsend, r.vrecv
    late_r = late_own if late_own is not None else (late_out if late_out is not None else late_in)
    rows, width = (mg_ref if attention else x_ref).shape
    size = width // HEADS
    lines = plane // 2
    length = rows * plane * PLANES
    half = rows // 2
    z, c = place(plane)
    column, core = c // 2, lax.rem(c, 2)
    group = lax.axis_index("grp")
    lw = width // groups

    def at_group(offset):
        return {"grp": lax.rem(group + offset, groups)}

    to_core = at_core(z, c, plane)
    greet(
        [at_z(z, c, plane, d) for d in range(1, PLANES)]
        + [at_x(z, c, plane, d) for d in range(1, lines)]
        + [to_core]
        + [at_group(d) for d in range(1, groups) if weights]
    )
    sent = []

    def start(copy):
        copy.start()
        sent.append(copy)

    def dcopy(slot, d):
        return remote(
            dpack.at[lax.rem(z + d, PLANES), slot], drecv.at[slot, z],
            zsend.at[slot, d], zrecv.at[slot, d], at_z(z, c, plane, d),
        )

    def key_copy(slot):
        return pltpu.make_async_copy(all_ref.at[slot], keybuf.at[slot % 2], keysem.at[slot % 2])

    for slot in range(SLOTS if attention else 0):
        if slot < 2:
            key_copy(slot).start()
        for to in range(PLANES):
            cols = slice((to * SLOTS + slot) * size, (to * SLOTS + slot + 1) * size)
            dpack[to, slot] = jnp.concatenate([mg_ref[:half, cols], mg_ref[half:, cols]], axis=1)
        for d in (2, 1, 3):
            start(dcopy(slot, d))
        drecv[slot, z] = dpack[z, slot]

    def arrive(slot):
        for d in range(1, PLANES):
            dcopy(slot, d).wait_recv()

    exchange = {}

    def swap(index, src, dst):
        exchange[index] = remote(src, dst, esend.at[index], erecv.at[index], to_core)
        start(exchange[index])

    def arrived(*indices):
        for index in indices:
            copy = exchange.pop(index, None)
            if copy is not None:
                copy.wait_recv()

    if weights:
        swap(0, lt_a.at[:, :, 1 - core], ltp_a)
        swap(1, branch_ref, rp_branch)
        swap(2, lt_n2.at[:, :, 1 - core], ltp_n2)
        swap(3, ug_ref, rp_ug)
        swap(4, lt_act.at[:, :, 1 - core], ltp_act)
        swap(5, dout_ref, rp_dout)
        swap(6, lt_n.at[:, :, 1 - core], ltp_n)

    if attention:
        for k in range(PLANES):
            masks[k] = position_masks(spans_ref, plane, length, c, k, rows).astype(BF16)
        first, end = spans_ref[0, 0], length - spans_ref[0, 1]

    def vectors(value, result):
        stages = [
            (vbuf_y, group, groups, at_group, 2),
            (vbuf_c, core, 2, lambda e: to_core, 0),
            (vbuf_x, column, lines, lambda e: at_x(z, c, plane, e), 1),
            (vbuf_z, z, PLANES, lambda e: at_z(z, c, plane, e), 3),
        ]

        def copies(stage):
            buf, me, count, partner, axis = stages[stage]
            return [
                remote(
                    buf.at[me], buf.at[me],
                    vsend.at[axis, e], vrecv.at[axis, e], partner(e),
                )
                for e in range(1, count)
            ]

        def step(stage):
            if stage == 0:
                total = value()
            else:
                buf, me, count, partner, axis = stages[stage - 1]
                for copy in copies(stage - 1):
                    copy.wait_recv()
                total = buf[0]
                for i in range(1, count):
                    total = total + buf[i]
            if stage == len(stages):
                result[...] = total
                return
            buf, me = stages[stage][:2]
            buf[me] = total
            for copy in copies(stage):
                start(copy)

        return step

    def bufs(piece):
        if piece == VALUE:
            return 0, wbuf_v, gy_v, gx_v, sx_v, sy_v, zs_v, zg_v, fin_v
        return piece, wbuf, gy, gx, sx, sy, zs, zg, fin

    def make(piece):
        i, buf = bufs(piece)[:2]
        count = PLANES * lines * shard
        if piece == OUT:
            arrived(0, 1)
            mine, theirs = lt_a[:, :, core, 0], ltp_a[:, :, 0]
            right, other = branch_ref[...], rp_branch[...]
        elif piece < DOWN:
            arrived(2, 3)
            cols = slice((piece - UP) * width, (piece - UP + 1) * width)
            mine, theirs = lt_n2[:, :, core, 0], ltp_n2[:, :, 0]
            right, other = ug_ref[:, cols], rp_ug[:, cols]
        elif piece < QUERY:
            arrived(4, 5)
            mine, theirs = lt_act[:, :, core, piece - DOWN], ltp_act[:, :, piece - DOWN]
            right, other = dout_ref[...], rp_dout[...]
        else:
            arrived(6, 7)
            at = (piece - QUERY) * width
            cols = slice(at, at + (width // 2 if piece == VALUE else width))
            mine, theirs = lt_n[:, :, core, 0], ltp_n[:, :, 0]
            right, other = late_r[:, cols], rp_late[:, cols]
        grad = dot(mine.reshape(count, rows), right, NN) + dot(theirs.reshape(count, rows), other, NN)
        lanes = grad.shape[1] // groups
        for h in range(groups):
            for zz in range(PLANES):
                for xx in range(lines):
                    at = (zz * lines + xx) * shard
                    buf[i, h, xx, zz] = grad[at : at + shard, h * lanes : (h + 1) * lanes].astype(BF16)
        for copy in first_copies(piece):
            start(copy)

    def first_copies(piece):
        i, buf, gy_b, gx_b = bufs(piece)[:4]
        n = piece
        if piece in LINE_FIRST:
            return [
                remote(
                    buf.at[i, :, lax.rem(column + e, lines)], gx_b.at[i, e - 1],
                    s1send.at[n, e], s1recv.at[n, e], at_x(z, c, plane, e),
                )
                for e in range(1, lines)
            ]
        return [
            remote(
                buf.at[i, lax.rem(group + e, groups)], gy_b.at[i, e - 1],
                s1send.at[n, e], s1recv.at[n, e], at_group(e),
            )
            for e in range(1, groups)
        ]

    def second_copies(piece):
        i, buf, gy_b, gx_b, sx_b, sy_b = bufs(piece)[:6]
        n = piece
        if piece in LINE_FIRST:
            return [
                remote(
                    sy_b.at[i, e - 1], gy_b.at[i, e - 1, 0],
                    s2send.at[n, e], s2recv.at[n, e], at_group(e),
                )
                for e in range(1, groups)
            ]
        return [
            remote(
                sx_b.at[i, e - 1], gx_b.at[i, e - 1, 0],
                s2send.at[n, e], s2recv.at[n, e], at_x(z, c, plane, e),
            )
            for e in range(1, lines)
        ]

    def first_total(piece, at):
        i, buf, gy_b, gx_b = bufs(piece)[:4]
        if piece in LINE_FIRST:
            value = buf[i, at, column].astype(F32)
            for e in range(1, lines):
                value = value + gx_b[i, e - 1, at].astype(F32)
            return value
        value = buf[i, group, at].astype(F32)
        for e in range(1, groups):
            value = value + gy_b[i, e - 1, at].astype(F32)
        return value

    def second(piece):
        i, buf, gy_b, gx_b, sx_b, sy_b = bufs(piece)[:6]
        for copy in first_copies(piece):
            copy.wait_recv()
        if piece in LINE_FIRST:
            for e in range(1, groups):
                sy_b[i, e - 1] = first_total(piece, lax.rem(group + e, groups)).astype(BF16)
        else:
            for e in range(1, lines):
                sx_b[i, e - 1] = first_total(piece, lax.rem(column + e, lines)).astype(BF16)
        for copy in second_copies(piece):
            start(copy)

    def third_copies(piece):
        i = bufs(piece)[0]
        zs_b, zg_b = bufs(piece)[6:8]
        n = piece
        return [
            remote(
                zs_b.at[i, lax.rem(z + d, PLANES)], zg_b.at[i, d - 1],
                wzsend.at[n, d], wzrecv.at[n, d], at_z(z, c, plane, d),
            )
            for d in (2, 1, 3)
        ]

    def third(piece):
        i, buf, gy_b, gx_b, sx_b, sy_b, zs_b, zg_b, fin_b = bufs(piece)
        for copy in second_copies(piece):
            copy.wait_recv()
        value = first_total(piece, group if piece in LINE_FIRST else column)
        if piece in LINE_FIRST:
            for e in range(1, groups):
                value = value + gy_b[i, e - 1, 0].astype(F32)
        else:
            for e in range(1, lines):
                value = value + gx_b[i, e - 1, 0].astype(F32)
        zs_b[i] = value.astype(BF16)
        for copy in third_copies(piece):
            start(copy)

    def last_copies(piece):
        i = bufs(piece)[0]
        fin_b = bufs(piece)[8]
        n = piece
        return [
            remote(fin_b.at[i, group], fin_b.at[i, group], fsend.at[n, e], frecv.at[n, e], at_group(e))
            for e in range(1, groups)
        ]

    def fourth(piece):
        i, buf, gy_b, gx_b, sx_b, sy_b, zs_b, zg_b, fin_b = bufs(piece)
        for copy in third_copies(piece):
            copy.wait_recv()
        value = zs_b[i, z].astype(F32)
        for d in range(1, PLANES):
            value = value + zg_b[i, d - 1].astype(F32)
        fin_b[i, group] = value.astype(BF16)
        for copy in last_copies(piece):
            start(copy)

    def finish(piece):
        for copy in last_copies(piece):
            copy.wait_recv()

    span = min(plane, 4)

    def grads(slot, k):
        held = keybuf.at[slot % 2]
        query = query_rows(held[k, c, rows:, :], True)
        grad = query_rows(drecv[slot, k], False)
        both = jnp.concatenate([query, grad], axis=0)
        turned = jnp.transpose(drecv[slot, k].astype(F32))
        turned = jnp.concatenate([turned[:size], turned[size:]], axis=1)
        delta = jnp.sum(turned * o_ref[slot, k], axis=0, keepdims=True)
        lse = lse_ref[slot, k, 0:1, :]
        query_grad = jnp.zeros((2 * size, rows), F32)
        for k2 in range(k, -1, -1):
            level = lse
            if k2 < k and k == PLANES - 1:
                position = k * plane * rows + c * rows + lax.broadcasted_iota(jnp.int32, (1, rows), 1)
                level = jnp.where(position >= end, -NEG_FILL, lse)
            for at in range(0, plane, span):
                where = slice(at * rows, (at + span) * rows)
                keys = held[k2, at : at + span, :rows, :].reshape(span * rows, 2 * size)
                scores = dot(keys, query, NT)
                prob_grad = dot(keys, grad, NT)
                if k2 == k:
                    scores = scores + masks[k, where, :].astype(F32)
                elif k2 == 0 and at == 0:
                    index = lax.broadcasted_iota(jnp.int32, (span * rows, 1), 0)
                    scores = scores + jnp.where(index < first, NEG_FILL, 0.0)
                prob = jnp.exp(scores - level)
                score_grad = (prob * (prob_grad - delta)).astype(BF16)
                update = dot(jnp.concatenate([score_grad, prob.astype(BF16)], axis=1), both, NN)
                if k2 == k:
                    acc[slot % 2, k2, where] = update
                else:
                    acc[slot % 2, k2, where] += update
                query_grad = query_grad + dot(keys, score_grad, TN)
        packed = jnp.concatenate([query_grad[:size, :half], query_grad[:size, half:]], axis=0)
        ret[k, slot, rows:, :] = jnp.transpose(packed).astype(BF16)

    def mine(slot, k, col):
        return acc[slot % 2, k, pl.ds(pl.multiple_of(col * rows, rows), rows), :]

    def ccopy(slot, line):
        return remote(
            part.at[slot, line], cgot.at[slot, line],
            csend.at[slot, line], crecv.at[slot, line], to_core,
        )

    def xcopy(slot, e):
        return remote(
            xpart.at[slot, e - 1], xgot.at[slot, e - 1],
            xsend.at[slot, e], xrecv.at[slot, e], at_x(z, c, plane, e),
        )

    def rcopy(slot, d):
        return remote(
            ret.at[lax.rem(z + d, PLANES), slot], got.at[slot, z],
            rsend.at[slot, d], rrecv.at[slot, d], at_z(z, c, plane, d),
        )

    def reduce_core(slot):
        for line in range(lines):
            for k in range(PLANES):
                part[slot, line, k] = mine(slot, k, 2 * line + 1 - core).astype(BF16)
            start(ccopy(slot, line))

    def reduce_line(slot):
        for line in range(lines):
            ccopy(slot, line).wait_recv()
        for e in range(1, lines):
            line = lax.rem(column + e, lines)
            for k in range(PLANES):
                xpart[slot, e - 1, k] = (
                    mine(slot, k, 2 * line + core) + cgot[slot, line, k].astype(F32)
                ).astype(BF16)
            start(xcopy(slot, e))

    def reduce_end(slot):
        for e in range(1, lines):
            xcopy(slot, e).wait_recv()
        for k in range(PLANES):
            total = mine(slot, k, c) + cgot[slot, column, k].astype(F32)
            for e in range(1, lines):
                total = total + xgot[slot, e - 1, k].astype(F32)
            ret[k, slot, :rows, :] = total.astype(BF16)
        for d in (2, 1, 3):
            start(rcopy(slot, d))
        got[slot, z] = ret[z, slot]

    def late_factors():
        for slot in range(SLOTS):
            for d in range(1, PLANES):
                rcopy(slot, d).wait_recv()
        for pair in range(HEADS // 2):
            at = pair * 2 * size
            keys, values, queries = [], [], []
            for head in (2 * pair, 2 * pair + 1):
                src, slot = divmod(head, SLOTS)
                block = got[slot, src].astype(F32)
                keys.append(block[:rows, :size])
                values.append(block[:rows, size:])
                queries.append(jnp.concatenate([block[rows:, :size], block[rows:, size:]], axis=0))
            late_r[:, at : at + 2 * size] = (jnp.concatenate(queries, axis=1) * 0.125).astype(BF16)
            late_r[:, width + at : width + at + 2 * size] = jnp.concatenate(keys, axis=1).astype(BF16)
            if pair < HEADS // 4:
                at = 2 * width + at
                late_r[:, at : at + 2 * size] = jnp.concatenate(values, axis=1).astype(BF16)
            else:
                at = at - width // 2
                gfv_ref[:, at : at + 2 * size] = jnp.concatenate(values, axis=1).astype(BF16)
    def input_grad():
        normed_grad = (
            dot(late_r[:, :width], wq_ref[...], NT)
            + dot(late_r[:, width : 2 * width], wk_ref[...], NT)
            + dot(late_r[:, 2 * width :], wv_ref[...], NT)
        )
        values = x_ref[...].astype(F32)
        centred = values - jnp.mean(values, axis=-1, keepdims=True)
        scale = lax.rsqrt(jnp.mean(centred * centred, axis=-1, keepdims=True) + EPSILON)
        unit = centred * scale
        inner = normed_grad * g_ref[...].reshape(1, width)
        back = scale * (
            inner
            - jnp.mean(inner, axis=-1, keepdims=True)
            - unit * jnp.mean(inner * unit, axis=-1, keepdims=True)
        )
        gin_ref[...] = hg_ref[...] + back

        def sums(v):
            return jnp.sum(v.astype(F32), axis=0, keepdims=True)

        return jnp.concatenate(
            [
                sums(normed_grad * unit),
                sums(normed_grad),
                sums(late_r[:, :width]),
                jnp.concatenate([sums(late_r[:, 2 * width :]), jnp.zeros((1, width // 2), F32)], axis=1),
                jnp.zeros((4, width), F32),
            ],
            axis=0,
        )

    def do(*tasks):
        for stage, what in tasks if weights else ():
            (make, second, third, fourth, finish)[stage - 1](what)

    do(*BEFORE)
    if attention:
        for slot in range(SLOTS):
            key_copy(slot).wait()
            arrive(slot)
            for k in range(PLANES):
                grads(slot, k)
                if slot and k == 1:
                    reduce_line(slot - 1)
                do(*AT_POINTS.get((slot, k), ()))
            if slot == 0:
                key_copy(2).start()
            reduce_core(slot)
            if slot:
                reduce_end(slot - 1)
    else:
        for tasks in AT_POINTS.values():
            do(*tasks)
    do(*AFTER[0])
    if attention:
        reduce_line(SLOTS - 1)
    do(*AFTER[1])
    if attention:
        reduce_end(SLOTS - 1)
    do(*AFTER[2])
    if attention:
        late_factors()
    if weights:
        swap(7, late_r, rp_late)
        partial = input_grad()
        late_vectors = vectors(lambda: jnp.concatenate([vec_ref[...], partial], axis=0), vec1_ref)
        late_vectors(0)
        for stage, tasks in enumerate(AFTER[3:]):
            do(*tasks)
            if stage < 4:
                late_vectors(stage + 1)
    arrived(*range(8))
    for copy in sent:
        copy.wait_send()


BEFORE = ((1, OUT),)
AT_POINTS = {
    (0, 1): ((1, UP + 2), (1, DOWN)),
    (1, 0): ((2, OUT),),
    (1, 1): ((1, DOWN + 3), (2, UP + 2)),
    (1, 2): ((1, UP + 3), (3, OUT), (1, UP)),
    (2, 1): ((2, DOWN + 3), (2, DOWN)),
    (2, 2): ((3, UP + 2),),
}
AFTER = (
    (),
    ((2, UP), (1, UP + 1), (4, OUT), (1, DOWN + 2)),
    ((1, DOWN + 1), (2, UP + 1), (3, DOWN + 3), (2, DOWN + 1), (3, DOWN), (4, UP + 2)),
    ((3, UP + 1), (3, UP), (2, UP + 3), (1, QUERY)),
    ((1, KEY), (3, DOWN + 1)),
    ((4, DOWN), (2, DOWN + 2), (4, UP + 1), (1, VALUE)),
    ((2, QUERY), (3, DOWN + 2), (3, UP + 3)),
    (
        (4, DOWN + 1), (5, UP + 2), (4, DOWN + 3), (2, KEY), (2, VALUE), (3, QUERY), (3, KEY), (3, VALUE), (4, UP),
        (4, UP + 3), (4, DOWN + 2), (4, QUERY), (4, KEY), (4, VALUE), (5, OUT), (5, UP), (5, UP + 1), (5, UP + 3),
        (5, DOWN), (5, DOWN + 1), (5, DOWN + 2), (5, DOWN + 3), (5, QUERY), (5, KEY), (5, VALUE),
    ),
)


def backward_call(plane, groups, rows, width, hidden, attention, weights, arrays):
    blocks = plane * PLANES
    lines = plane // 2
    size = width // HEADS
    half = rows // 2
    shard = width // blocks
    tall = hidden // width
    lw = width // groups
    lv = width // 2 // groups
    late = 2 * width + width // 2
    count = PIECES
    dma = pltpu.SemaphoreType.DMA
    most = max(groups, lines)

    def vmem(*shape):
        return pltpu.VMEM(shape, BF16)

    def vmem32(*shape):
        return pltpu.VMEM(shape, F32)

    ins = {}
    outs = {}
    scratch = {}
    if attention:
        ins.update(mg_ref=VMEM, all_ref=pl.BlockSpec(memory_space=pl.ANY), o_ref=VMEM, lse_ref=VMEM, spans_ref=SMEM)
        outs.update(gfv_ref=((rows, width // 2), BF16))
        scratch.update(
            dpack=vmem(PLANES, SLOTS, half, 2 * size),
            drecv=vmem(SLOTS, PLANES, half, 2 * size),
            masks=vmem(PLANES, plane * rows, rows),
            acc=vmem32(2, PLANES, plane * rows, 2 * size),
            part=vmem(SLOTS, lines, PLANES, rows, 2 * size),
            cgot=vmem(SLOTS, lines, PLANES, rows, 2 * size),
            xpart=vmem(SLOTS, lines - 1, PLANES, rows, 2 * size),
            xgot=vmem(SLOTS, lines - 1, PLANES, rows, 2 * size),
            ret=vmem(PLANES, SLOTS, rows + half, 2 * size),
            got=vmem(SLOTS, PLANES, rows + half, 2 * size),
            keybuf=vmem(2, PLANES, plane, rows + half, 2 * size),
            keysem=dma((2,)),
            zsend=dma((SLOTS, PLANES)), zrecv=dma((SLOTS, PLANES)),
            csend=dma((SLOTS, lines)), crecv=dma((SLOTS, lines)),
            xsend=dma((SLOTS, lines)), xrecv=dma((SLOTS, lines)),
            rsend=dma((SLOTS, PLANES)), rrecv=dma((SLOTS, PLANES)),
        )
        if weights:
            scratch.update(late_own=vmem(rows, late))
        else:
            outs.update(late_out=((rows, late), BF16))
    if weights:
        ins.update(
            lt_a=VMEM, lt_n2=VMEM, lt_act=VMEM, lt_n=VMEM, branch_ref=VMEM, ug_ref=VMEM, dout_ref=VMEM, vec_ref=VMEM,
            x_ref=VMEM, g_ref=VMEM, hg_ref=VMEM, wq_ref=VMEM, wk_ref=VMEM, wv_ref=VMEM,
        )
        if not attention:
            ins.update(late_in=VMEM)
        outs.update(
            gin_ref=((rows, width), F32), vec1_ref=((16, width), F32),
            fin=((count - 1, groups, shard, lw), BF16), fin_v=((1, groups, shard, lv), BF16),
        )
        scratch.update(
            ltp_a=vmem(PLANES, lines, 1, shard, rows),
            ltp_n2=vmem(PLANES, lines, 1, shard, rows),
            ltp_act=vmem(PLANES, lines, tall, shard, rows),
            ltp_n=vmem(PLANES, lines, 1, shard, rows),
            rp_branch=vmem(rows, width), rp_ug=vmem(rows, hidden), rp_dout=vmem(rows, width), rp_late=vmem(rows, late),
            vbuf_c=vmem32(2, 16, width), vbuf_x=vmem32(lines, 16, width),
            vbuf_y=vmem32(groups, 16, width), vbuf_z=vmem32(PLANES, 16, width),
            esend=dma((8,)), erecv=dma((8,)),
            s1send=dma((count, most)), s1recv=dma((count, most)),
            s2send=dma((count, most)), s2recv=dma((count, most)),
            wzsend=dma((count, PLANES)), wzrecv=dma((count, PLANES)),
            fsend=dma((count, groups)), frecv=dma((count, groups)),
            vsend=dma((4, max(most, PLANES))), vrecv=dma((4, max(most, PLANES))),
        )
        for tag, n, lanes in (("", count - 1, lw), ("_v", 1, lv)):
            scratch.update({
                "wbuf" + tag: vmem(n, groups, lines, PLANES, shard, lanes),
                "gy" + tag: vmem(n, groups - 1, lines, PLANES, shard, lanes),
                "gx" + tag: vmem(n, lines - 1, groups if LINE_FIRST else 1, PLANES, shard, lanes),
                "sx" + tag: vmem(n, lines - 1, PLANES, shard, lanes),
                "zs" + tag: vmem(n, PLANES, shard, lanes),
                "zg" + tag: vmem(n, PLANES - 1, shard, lanes),
            })
            if LINE_FIRST:
                scratch["sy" + tag] = vmem(n, groups - 1, PLANES, shard, lanes)
    names = tuple(ins) + tuple(outs) + tuple(scratch)
    result = pl.pallas_call(
        functools.partial(backward_kernel, plane, groups, shard, names, attention, weights),
        name="backward",
        out_shape=tuple(jax.ShapeDtypeStruct(*v) for v in outs.values()),
        in_specs=list(ins.values()),
        out_specs=(VMEM,) * len(outs),
        scratch_shapes=list(scratch.values()),
        compiler_params=pltpu.CompilerParams(
            collective_id=2 if attention else 3, has_side_effects=True, vmem_limit_bytes=61 << 20
        ),
    )(*[arrays[name] for name in ins])
    return dict(zip(outs, result))


def tail_kernel(
    gin_ref, gfv_ref, vec1_ref, fin_ref, finv_ref,
    o_gin, o_gfv, o_g1, o_s1, o_wq, o_bq, o_wk, o_wv, o_bv, o_wo, o_bo, o_g2, o_s2, o_wu, o_bu, o_wd, o_bd,
):
    groups, shard, lanes = fin_ref.shape[1:]
    width = groups * lanes
    tall = o_wd.shape[0] // shard
    o_gin[...] = gin_ref[...]
    o_gfv[...] = gfv_ref[...]

    def put(ref, rows, at, piece):
        for h in range(groups):
            ref[rows, at + h * lanes : at + (h + 1) * lanes] = fin_ref[piece, h].astype(F32)

    everything = slice(0, shard)
    put(o_wo, everything, 0, OUT)
    put(o_wq, everything, 0, QUERY)
    put(o_wk, everything, 0, KEY)
    for i in range(tall):
        put(o_wu, everything, i * width, UP + i)
        put(o_wd, slice(i * shard, (i + 1) * shard), 0, DOWN + i)
    for h in range(groups):
        o_wv[:, h * (lanes // 2) : (h + 1) * (lanes // 2)] = finv_ref[0, h].astype(F32)
    o_g2[...], o_s2[...], o_bo[...], o_bd[...] = vec1_ref[0], vec1_ref[1], vec1_ref[2], vec1_ref[3 + tall]
    for i in range(tall):
        o_bu[i * width : (i + 1) * width] = vec1_ref[3 + i]
    o_g1[...], o_s1[...], o_bq[...] = vec1_ref[8], vec1_ref[9], vec1_ref[10]
    o_bv[...] = vec1_ref[11, : width // 2]


def tail_part(rows, width, hidden, shard, got):
    def out(*shape):
        return jax.ShapeDtypeStruct(shape, F32)

    return pl.pallas_call(
        tail_kernel,
        name="tail",
        out_shape=(
            out(rows, width), jax.ShapeDtypeStruct((rows, width // 2), BF16), out(width), out(width),
            out(shard, width), out(width), out(shard, width), out(shard, width // 2), out(width // 2),
            out(shard, width), out(width), out(width), out(width),
            out(shard, hidden), out(hidden), out(hidden // width * shard, width), out(width),
        ),
        in_specs=[VMEM] * 5,
        out_specs=(VMEM,) * 17,
    )(*got)


def body(
    inputs,
    first_values,
    spans,
    ln1_gain,
    ln1_shift,
    w_query,
    b_query,
    w_key,
    w_value,
    b_value,
    w_out,
    b_out,
    ln2_gain,
    ln2_shift,
    w_up,
    b_up,
    w_down,
    b_down,
    out_grad,
):
    rows, width = inputs.shape
    hidden = w_up.shape[1]
    groups = lax.axis_size("grp")
    plane = lax.axis_size("blk") // PLANES
    attended, normed, all_blocks, mixed, lse = forward_part(
        inputs, first_values, spans, ln1_gain, ln1_shift, w_query, b_query, w_key, w_value, b_value
    )
    result, mixed_grad, hidden_grad, branch_grad, upper_grad, grad_down, vectors, lt_a, lt_n2, lt_act, lt_n = middle_part(
        plane, inputs, attended, normed, spans, out_grad, b_out, ln2_gain, ln2_shift, b_up, b_down, w_out, w_up, w_down
    )
    arrays = dict(
        mg_ref=mixed_grad, all_ref=all_blocks, o_ref=mixed, lse_ref=lse, spans_ref=spans,
        lt_a=lt_a, lt_n2=lt_n2, lt_act=lt_act, lt_n=lt_n,
        branch_ref=branch_grad, ug_ref=upper_grad, dout_ref=grad_down, vec_ref=vectors,
        x_ref=inputs, g_ref=ln1_gain, hg_ref=hidden_grad, wq_ref=w_query, wk_ref=w_key, wv_ref=w_value,
    )
    call = functools.partial(backward_call, plane, groups, rows, width, hidden)
    if plane <= 4:
        got = Refs(call(True, True, arrays))
    else:
        got = Refs(call(True, False, arrays))
        arrays.update(late_in=got.late_out)
        got.update(call(False, True, arrays))
    return (result,) + tuple(
        tail_part(
            rows, width, hidden, width // (plane * PLANES),
            (got.gin_ref, got.gfv_ref, got.vec1_ref, got.fin, got.fin_v),
        )
    )


def solution(mesh):
    placed = (
        P(("grp", "blk"), None),
        P(("grp", "blk"), None),
        P("grp", None),
        P(),
        P(),
        P(),
        P(),
        P(),
        P(),
        P(),
        P(),
        P(),
        P(),
        P(),
        P(),
        P(),
        P(),
        P(),
        P(("grp", "blk"), None),
    )
    return jax.shard_map(
        body,
        mesh=mesh,
        in_specs=placed,
        out_specs=(
            P(("grp", "blk"), None),
            P(("grp", "blk"), None),
            P(("grp", "blk"), None),
            P(),
            P(),
            P("blk", None),
            P(),
            P("blk", None),
            P("blk", None),
            P(),
            P("blk", None),
            P(),
            P(),
            P(),
            P("blk", None),
            P(),
            P("blk", None),
            P(),
        ),
        check_vma=False,
    )
```

```python
import functools

import jax
import jax.numpy as jnp
from jax import lax
from jax.experimental import pallas as pl
from jax.experimental.pallas import tpu as pltpu
from jax.sharding import PartitionSpec as P

HEADS = 12
PLANES = 4
SLOTS = HEADS // PLANES
EPSILON = 1e-05
GELU_COEF = 0.7978845608028654
NEG_FILL = -1e30
BF16 = jnp.bfloat16
F32 = jnp.float32
MESH = pl.DeviceIdType.MESH
VMEM = pl.BlockSpec(memory_space=pltpu.VMEM)
SMEM = pl.BlockSpec(memory_space=pltpu.SMEM)


def dot(a, b, dims):
    return lax.dot_general(a, b, (dims, ((), ())), preferred_element_type=F32)


NN = ((1,), (0,))
NT = ((1,), (1,))
TN = ((0,), (0,))


def norm_rows(values, gain, shift):
    average = jnp.mean(values, axis=-1, keepdims=True)
    centred = values - average
    variance = jnp.mean(centred * centred, axis=-1, keepdims=True)
    return centred * lax.rsqrt(variance + EPSILON) * gain + shift


def place(plane):
    block = lax.axis_index("blk")
    return block // plane, lax.rem(block, plane)


def at_z(z, c, plane, offset):
    return {"blk": lax.rem(z + offset, PLANES) * plane + c}


def at_x(z, c, plane, offset):
    lines = plane // 2
    column, core = c // 2, lax.rem(c, 2)
    return {"blk": z * plane + lax.rem(column + offset, lines) * 2 + core}


def at_core(z, c, plane):
    return {"blk": z * plane + (c // 2) * 2 + 1 - lax.rem(c, 2)}


def greet(partners):
    barrier = pltpu.get_barrier_semaphore()
    for partner in partners:
        pl.semaphore_signal(barrier, inc=1, device_id=partner, device_id_type=MESH)
    pl.semaphore_wait(barrier, len(partners))


def remote(src, dst, send, recv, partner):
    return pltpu.make_async_remote_copy(
        src_ref=src, dst_ref=dst, send_sem=send, recv_sem=recv,
        device_id=partner, device_id_type=MESH,
    )


def query_rows(pack, first):
    half = pack.shape[1] // 2
    lanes = lax.broadcasted_iota(jnp.int32, pack.shape, 1)
    wide = pack.astype(F32)
    other = pltpu.roll(wide, half, 1)
    keep = lanes < half if first else lanes >= half
    top, bottom = (wide, other) if first else (other, wide)
    return jnp.concatenate(
        [jnp.where(keep, top, 0.0), jnp.where(keep, bottom, 0.0)], axis=0
    ).astype(BF16)


def position_masks(spans_ref, plane, length, c, k, rows):
    first, end = spans_ref[0, 0], length - spans_ref[0, 1]
    dead = end - spans_ref[0, 2]
    width = plane * rows
    key = k * width + lax.broadcasted_iota(jnp.int32, (width, rows), 0)
    query = k * width + c * rows + lax.broadcasted_iota(jnp.int32, (width, rows), 1)
    allowed = key <= query
    if k == 0:
        allowed &= ((key >= first) == (query >= first))
    if k == PLANES - 1:
        allowed &= ((key >= end) == (query >= end)) & ((key < dead) | (key >= end))
    return jnp.where(allowed, 0.0, NEG_FILL)


def forward_kernel(
    plane, x_ref, fv_ref, spans_ref, g_ref, s_ref, wq_ref, bq_ref, wk_ref, wv_ref, bv_ref,
    att_ref, normed_ref, all_out, o_ref, lse_ref,
    all_ref, allsem, pack, opack, orecv, masks,
    zsend, zrecv, xsend, xrecv, csend, crecv, osend, orecv_sem,
):
    rows, width = x_ref.shape
    size = width // HEADS
    lines = plane // 2
    length = rows * plane * PLANES
    half = rows // 2
    z, c = place(plane)
    core = lax.rem(c, 2)
    greet(
        [at_z(z, c, plane, d) for d in range(1, PLANES)]
        + [at_x(z, c, plane, d) for d in range(1, lines)]
        + [at_core(z, c, plane)]
    )
    normed = norm_rows(
        x_ref[...].astype(F32), g_ref[...].reshape(1, width), s_ref[...].reshape(1, width)
    ).astype(BF16)
    normed_ref[...] = normed
    query = ((dot(normed, wq_ref[...], NN) + bq_ref[...].reshape(1, width)) * 0.125)
    key = dot(normed, wk_ref[...], NN)
    fresh = dot(normed, wv_ref[...], NN) + bv_ref[...].reshape(1, width // 2)
    value = jnp.concatenate([fresh, fv_ref[...].astype(F32)], axis=1)
    for head in range(HEADS):
        to, slot = divmod(head, SLOTS)
        cols = slice(head * size, (head + 1) * size)
        pack[to, slot, :rows, :] = jnp.concatenate(
            [key[:, cols], value[:, cols]], axis=1
        ).astype(BF16)
        pack[to, slot, rows:, :] = jnp.concatenate(
            [query[:half, cols], query[half:, cols]], axis=1
        ).astype(BF16)

    zcopies = {}
    for slot in range(SLOTS):
        for d in (2, 1, 3):
            to = lax.rem(z + d, PLANES)
            copy = remote(
                pack.at[to, slot], all_ref.at[slot, z, c],
                zsend.at[slot, d], zrecv.at[slot, d], at_z(z, c, plane, d),
            )
            copy.start()
            zcopies[slot, d] = copy
        all_ref[slot, z, c] = pack[z, slot]

    started = []

    def hand_out(slot, d):
        block = all_ref.at[slot, lax.rem(z + PLANES - d, PLANES), c, pl.ds(0, rows)]
        for e in range(1, lines):
            copy = remote(
                block, block, xsend.at[slot, d, e], xrecv.at[slot, d, e], at_x(z, c, plane, e)
            )
            copy.start()
            started.append(copy)
        copy = remote(block, block, csend.at[slot, d, 0], crecv.at[slot, d, 0], at_core(z, c, plane))
        copy.start()
        started.append(copy)

    for slot in range(SLOTS):
        hand_out(slot, 0)
    for k in range(PLANES):
        masks[k] = position_masks(spans_ref, plane, length, c, k, rows)
    first, end = spans_ref[0, 0], length - spans_ref[0, 1]

    def spread(slot):
        for d in (1, 3, 2):
            zcopies[slot, d].wait_recv()
            hand_out(slot, d)

    def pass_on(slot):
        for d in (0, 1, 3, 2):
            src = lax.rem(z + PLANES - d, PLANES)
            for e in range(1, lines):
                column = lax.rem(c // 2 + lines - e, lines) * 2 + core
                block = all_ref.at[slot, src, column, pl.ds(0, rows)]
                remote(
                    block, block, xsend.at[slot, d, e], xrecv.at[slot, d, e], at_x(z, c, plane, e)
                ).wait_recv()
                copy = remote(
                    block, block, csend.at[slot, d, e], crecv.at[slot, d, e], at_core(z, c, plane)
                )
                copy.start()
                started.append(copy)

    def settle(slot):
        for d in range(PLANES):
            for e in range(lines):
                block = all_ref.at[slot, 0, c, pl.ds(0, rows)]
                remote(
                    block, block, csend.at[slot, d, e], crecv.at[slot, d, e], at_core(z, c, plane)
                ).wait_recv()

    def keys_of(slot, k):
        return all_ref[slot, k, :, :rows, :].reshape(plane * rows, 2 * size)

    def attend(slot, k):
        q = query_rows(all_ref[slot, k, c, rows:, :], True)

        def step(state, k2, bias):
            top, total, acc = state
            count = plane
            blocks = [all_ref[slot, k2, b, :rows, :] for b in range(count)]
            scores = [bias(dot(blocks[b], q, NT), b) for b in range(count)]
            new = top
            for part in scores:
                new = jnp.maximum(new, jnp.max(part, axis=0, keepdims=True))
            scale = jnp.exp(top - new)
            total, acc = total * scale, acc * scale
            for b in range(count):
                prob = jnp.exp(scores[b] - new)
                total = total + jnp.sum(prob, axis=0, keepdims=True)
                acc = acc + dot(blocks[b], prob.astype(BF16), TN)
            return new, total, acc

        state = (
            jnp.full((1, rows), NEG_FILL, F32),
            jnp.zeros((1, rows), F32),
            jnp.zeros((2 * size, rows), F32),
        )
        state = step(state, k, lambda t, b: t + masks[k, b * rows : (b + 1) * rows])
        diagonal = state
        for k2 in range(k):
            if k2 == 0:
                index = lax.broadcasted_iota(jnp.int32, (rows, 1), 0)
                shut = jnp.where(index < first, NEG_FILL, 0.0)
                state = step(state, k2, lambda t, b: t + shut if b == 0 else t)
            else:
                state = step(state, k2, lambda t, b: t)
        if k == PLANES - 1:
            position = k * plane * rows + c * rows + lax.broadcasted_iota(jnp.int32, (1, rows), 1)
            after = position >= end
            state = tuple(jnp.where(after, old, new) for old, new in zip(diagonal, state))
        top, total, acc = state
        mixed = acc[size:] / total
        o_ref[slot, k] = mixed
        lse_ref[slot, k] = jnp.broadcast_to(top + jnp.log(total), (8, rows))
        packed = jnp.concatenate([mixed[:, :half], mixed[:, half:]], axis=0)
        opack[slot, k] = jnp.transpose(packed).astype(BF16)

    def back(slot, k, src):
        return remote(
            opack.at[slot, k], orecv.at[slot, src],
            osend.at[slot, k], orecv_sem.at[slot, src], {"blk": k * plane + c},
        )

    def give_back(slot, k):
        @pl.when(z == k)
        def _():
            orecv[slot, k] = opack[slot, k]

        @pl.when(z != k)
        def _():
            back(slot, k, z).start()

    kept = []
    spread(0)
    pass_on(0)
    settle(0)
    spread(1)
    for slot in range(SLOTS):
        if slot:
            settle(slot)
        keep = pltpu.make_async_copy(all_ref.at[slot], all_out.at[slot], allsem.at[slot])
        keep.start()
        kept.append(keep)
        for k in range(PLANES - 1, -1, -1):
            attend(slot, k)
            give_back(slot, k)
        if slot + 2 < SLOTS:
            spread(slot + 2)
        if slot + 1 < SLOTS:
            pass_on(slot + 1)
    for slot in range(SLOTS):
        for k in range(PLANES):
            @pl.when(z != k)
            def _(slot=slot, k=k):
                back(slot, 0, k).wait_recv()
    for pair in range(HEADS // 2):
        parts = []
        for head in (2 * pair, 2 * pair + 1):
            src, slot = divmod(head, SLOTS)
            got = orecv[slot, src].astype(F32)
            parts.append(jnp.concatenate([got[:, :size], got[:, size:]], axis=0))
        att_ref[:, pair * 2 * size : (pair + 1) * 2 * size] = jnp.concatenate(parts, axis=1).astype(BF16)
    for slot in range(SLOTS):
        for k in range(PLANES):
            @pl.when(z != k)
            def _(slot=slot, k=k):
                back(slot, k, 0).wait_send()
    for keep in kept:
        keep.wait()
    for copy in list(zcopies.values()) + started:
        copy.wait_send()


def forward_part(inputs, first_values, spans, ln1_gain, ln1_shift, w_query, b_query, w_key, w_value, b_value):
    rows, width = inputs.shape
    plane = lax.axis_size("blk") // PLANES
    lines = plane // 2
    size = width // HEADS
    half = rows // 2
    dma = pltpu.SemaphoreType.DMA
    return pl.pallas_call(
        functools.partial(forward_kernel, plane),
        name="forward",
        out_shape=(
            jax.ShapeDtypeStruct((rows, width), BF16),
            jax.ShapeDtypeStruct((rows, width), BF16),
            jax.ShapeDtypeStruct((SLOTS, PLANES, plane, rows + half, 2 * size), BF16),
            jax.ShapeDtypeStruct((SLOTS, PLANES, size, rows), F32),
            jax.ShapeDtypeStruct((SLOTS, PLANES, 8, rows), F32),
        ),
        in_specs=[VMEM, VMEM, SMEM] + [VMEM] * 7,
        out_specs=(VMEM, VMEM, pl.BlockSpec(memory_space=pl.ANY), VMEM, VMEM),
        scratch_shapes=[
            pltpu.VMEM((SLOTS, PLANES, plane, rows + half, 2 * size), BF16),
            dma((SLOTS,)),
            pltpu.VMEM((PLANES, SLOTS, rows + half, 2 * size), BF16),
            pltpu.VMEM((SLOTS, PLANES, half, 2 * size), BF16),
            pltpu.VMEM((SLOTS, PLANES, half, 2 * size), BF16),
            pltpu.VMEM((PLANES, plane * rows, rows), F32),
            dma((SLOTS, PLANES)), dma((SLOTS, PLANES)),
            dma((SLOTS, PLANES, lines)), dma((SLOTS, PLANES, lines)),
            dma((SLOTS, PLANES, lines)), dma((SLOTS, PLANES, lines)),
            dma((SLOTS, PLANES)), dma((SLOTS, PLANES)),
        ],
        compiler_params=pltpu.CompilerParams(
            collective_id=1, has_side_effects=True, vmem_limit_bytes=56 << 20
        ),
    )(
        inputs, first_values, spans, ln1_gain, ln1_shift, w_query, b_query, w_key, w_value, b_value,
    )


def middle_kernel(
    x_ref, att_ref, normed_ref, spans_ref, og_ref, bo_ref, g_ref, s_ref, bu_ref, bd_ref,
    wo_hbm, wu_hbm, wd_hbm,
    result_ref, mg_ref, hg_ref, branch_ref, ug_ref, dout_ref, vec_ref, lt_a, lt_n2, lt_act, lt_n,
    wo_ref, wu_ref, wd_ref, sem,
):
    rows, width = x_ref.shape
    tall = bu_ref.shape[0] // width
    shard = lt_a.shape[4]
    copies = [pltpu.make_async_copy(wo_hbm, wo_ref, sem.at[0])]
    for i in range(tall):
        part = pl.ds(i * width, width)
        copies.append(pltpu.make_async_copy(wu_hbm.at[:, part], wu_ref.at[:, part], sem.at[1 + 2 * i]))
        copies.append(pltpu.make_async_copy(wd_hbm.at[part], wd_ref.at[part], sem.at[2 + 2 * i]))
    for copy in copies:
        copy.start()

    def turn(value, dst, piece):
        turned = jnp.transpose(value)
        at = 0
        span = width // (dst.shape[0] * dst.shape[1] * 2)
        if dst.shape[3] == 1:
            for zz in range(dst.shape[0]):
                for xx in range(dst.shape[1]):
                    for cc in range(2):
                        dst[zz, xx, cc, 0] = turned[at : at + span]
                        at += span
            return
        per = dst.shape[3]
        for unit in range(width // span):
            index = piece * (width // span) + unit
            owner, part = divmod(index, per)
            chip, cc = divmod(owner, 2)
            zz, xx = divmod(chip, dst.shape[1])
            dst[zz, xx, cc, part] = turned[unit * span : (unit + 1) * span]

    def sums(value):
        return jnp.sum(value.astype(F32), axis=0, keepdims=True)

    block = lax.axis_index("blk")
    length = rows * lax.axis_size("blk")
    end = length - spans_ref[0, 1]
    position = block * rows + lax.broadcasted_iota(jnp.int32, (rows, 1), 0)
    alive = (position < end - spans_ref[0, 2]) | (position >= end)
    dout = jnp.where(alive, og_ref[...].astype(F32), 0.0)
    dout_low = dout.astype(BF16)
    dout_ref[...] = dout_low
    vec_ref[3 + tall : 4 + tall, :] = sums(dout)
    attended = att_ref[...]
    turn(normed_ref[...], lt_n, 0)
    turn(attended, lt_a, 0)
    copies[0].wait()
    hidden = x_ref[...].astype(F32) + dot(attended, wo_ref[...], NN) + bo_ref[...].reshape(1, width)
    average = jnp.mean(hidden, axis=-1, keepdims=True)
    centred = hidden - average
    scale = lax.rsqrt(jnp.mean(centred * centred, axis=-1, keepdims=True) + EPSILON)
    unit = centred * scale
    gain = g_ref[...].reshape(1, width)
    normed2 = (unit * gain + s_ref[...].reshape(1, width)).astype(BF16)
    turn(normed2, lt_n2, 0)
    result = hidden + bd_ref[...].reshape(1, width)
    normed2_grad = jnp.zeros((rows, width), F32)
    for i in range(tall):
        cols = slice(i * width, (i + 1) * width)
        copies[1 + 2 * i].wait()
        copies[2 + 2 * i].wait()
        upper = dot(normed2, wu_ref[:, cols], NN) + bu_ref[cols].reshape(1, width)
        square = upper * upper
        curve = jnp.tanh(GELU_COEF * (upper + 0.044715 * upper * square))
        half = 0.5 * (1.0 + curve)
        active = (upper * half).astype(BF16)
        slope = half + 0.5 * upper * (1.0 - curve * curve) * (GELU_COEF * (1.0 + 3.0 * 0.044715 * square))
        turn(active, lt_act, i)
        result = result + dot(active, wd_ref[cols, :], NN)
        upper_grad = (dot(dout_low, wd_ref[cols, :], NT) * slope).astype(BF16)
        ug_ref[:, cols] = upper_grad
        vec_ref[3 + i : 4 + i, :] = sums(upper_grad)
        normed2_grad = normed2_grad + dot(upper_grad, wu_ref[:, cols], NT)
    result_ref[...] = result
    vec_ref[0:1, :] = sums(normed2_grad * unit)
    vec_ref[1:2, :] = sums(normed2_grad)
    inner = normed2_grad * gain
    back = scale * (
        inner - jnp.mean(inner, axis=-1, keepdims=True) - unit * jnp.mean(inner * unit, axis=-1, keepdims=True)
    )
    hidden_grad = dout + back
    hg_ref[...] = hidden_grad
    branch = hidden_grad.astype(BF16)
    branch_ref[...] = branch
    vec_ref[2:3, :] = sums(branch)
    mg_ref[...] = dot(branch, wo_ref[...], NT).astype(BF16)


def middle_part(plane, inputs, attended, normed, spans, out_grad, b_out, gain, shift, b_up, b_down, w_out, w_up, w_down):
    rows, width = inputs.shape
    hidden = w_up.shape[1]
    tall = hidden // width
    lines = plane // 2
    shard = width // (plane * PLANES)

    def low(*shape):
        return jax.ShapeDtypeStruct(shape, BF16)

    any_space = pl.BlockSpec(memory_space=pl.ANY)
    return pl.pallas_call(
        middle_kernel,
        name="middle",
        out_shape=(
            jax.ShapeDtypeStruct((rows, width), F32), low(rows, width), jax.ShapeDtypeStruct((rows, width), F32),
            low(rows, width), low(rows, hidden), low(rows, width), jax.ShapeDtypeStruct((4 + tall, width), F32),
            low(PLANES, lines, 2, 1, shard, rows), low(PLANES, lines, 2, 1, shard, rows),
            low(PLANES, lines, 2, tall, shard, rows), low(PLANES, lines, 2, 1, shard, rows),
        ),
        in_specs=[VMEM, VMEM, VMEM, SMEM] + [VMEM] * 6 + [any_space] * 3,
        out_specs=(VMEM,) * 11,
        scratch_shapes=[
            pltpu.VMEM((width, width), BF16), pltpu.VMEM((width, hidden), BF16), pltpu.VMEM((hidden, width), BF16),
            pltpu.SemaphoreType.DMA((1 + 2 * tall,)),
        ],
        compiler_params=pltpu.CompilerParams(vmem_limit_bytes=56 << 20),
    )(inputs, attended, normed, spans, out_grad, b_out, gain, shift, b_up, b_down, w_out, w_up, w_down)


OUT, UP, DOWN, QUERY, KEY, VALUE = 0, 1, 5, 9, 10, 11
PIECES = 12
LINE_FIRST = frozenset((OUT, DOWN, DOWN + 1, VALUE))


class Refs(dict):
    __getattr__ = dict.get


def backward_kernel(plane, groups, shard, names, attention, weights, *refs):
    r = Refs(zip(names, refs, strict=True))
    mg_ref, all_ref, o_ref, lse_ref, spans_ref, lt_a, lt_n2, lt_act = r.mg_ref, r.all_ref, r.o_ref, r.lse_ref, r.spans_ref, r.lt_a, r.lt_n2, r.lt_act
    lt_n, branch_ref, ug_ref, dout_ref, vec_ref, x_ref, g_ref, hg_ref = r.lt_n, r.branch_ref, r.ug_ref, r.dout_ref, r.vec_ref, r.x_ref, r.g_ref, r.hg_ref
    wq_ref, wk_ref, wv_ref, late_in, gin_ref, gfv_ref, vec1_ref = r.wq_ref, r.wk_ref, r.wv_ref, r.late_in, r.gin_ref, r.gfv_ref, r.vec1_ref
    late_out, dpack = r.late_out, r.dpack
    drecv, masks, acc, part, cgot, xpart, xgot, ret = r.drecv, r.masks, r.acc, r.part, r.cgot, r.xpart, r.xgot, r.ret
    got, keybuf, keysem, ltp_a, ltp_n2, ltp_act, ltp_n, rp_branch = r.got, r.keybuf, r.keysem, r.ltp_a, r.ltp_n2, r.ltp_act, r.ltp_n, r.rp_branch
    rp_ug, rp_dout, late_own, rp_late, wbuf, gy, gx, sx = r.rp_ug, r.rp_dout, r.late_own, r.rp_late, r.wbuf, r.gy, r.gx, r.sx
    sy, zs, zg, fin, wbuf_v, gy_v, gx_v, sx_v = r.sy, r.zs, r.zg, r.fin, r.wbuf_v, r.gy_v, r.gx_v, r.sx_v
    sy_v, zs_v, zg_v, fin_v, vbuf_c, vbuf_x, vbuf_y, vbuf_z = r.sy_v, r.zs_v, r.zg_v, r.fin_v, r.vbuf_c, r.vbuf_x, r.vbuf_y, r.vbuf_z
    zsend, zrecv, csend, crecv, xsend, xrecv, rsend, rrecv = r.zsend, r.zrecv, r.csend, r.crecv, r.xsend, r.xrecv, r.rsend, r.rrecv
    esend, erecv, s1send, s1recv, s2send, s2recv, wzsend, wzrecv = r.esend, r.erecv, r.s1send, r.s1recv, r.s2send, r.s2recv, r.wzsend, r.wzrecv
    fsend, frecv, vsend, vrecv = r.fsend, r.frecv, r.vsend, r.vrecv
    later = [
        pltpu.make_async_copy(src, dst, r.lsem.at[i])
        for i, (src, dst) in enumerate(
            ((r.x_hbm, x_ref), (r.hg_hbm, hg_ref), (r.wq_hbm, wq_ref), (r.wk_hbm, wk_ref), (r.wv_hbm, wv_ref))
        )
    ] if weights else []
    late_r = late_own if late_own is not None else (late_out if late_out is not None else late_in)
    rows, width = (mg_ref if attention else x_ref).shape
    size = width // HEADS
    lines = plane // 2
    length = rows * plane * PLANES
    half = rows // 2
    z, c = place(plane)
    column, core = c // 2, lax.rem(c, 2)
    group = lax.axis_index("grp")
    lw = width // groups

    def at_group(offset):
        return {"grp": lax.rem(group + offset, groups)}

    to_core = at_core(z, c, plane)
    greet(
        [at_z(z, c, plane, d) for d in range(1, PLANES)]
        + [at_x(z, c, plane, d) for d in range(1, lines)]
        + [to_core]
        + [at_group(d) for d in range(1, groups) if weights]
    )
    sent = []

    def start(copy):
        copy.start()
        sent.append(copy)

    for copy in later:
        copy.start()

    def dcopy(slot, d):
        return remote(
            dpack.at[lax.rem(z + d, PLANES), slot], drecv.at[slot, z],
            zsend.at[slot, d], zrecv.at[slot, d], at_z(z, c, plane, d),
        )

    def key_copy(slot):
        return pltpu.make_async_copy(all_ref.at[slot], keybuf.at[slot % 2], keysem.at[slot % 2])

    for slot in range(SLOTS if attention else 0):
        if slot < 2:
            key_copy(slot).start()
        for to in range(PLANES):
            cols = slice((to * SLOTS + slot) * size, (to * SLOTS + slot + 1) * size)
            dpack[to, slot] = jnp.concatenate([mg_ref[:half, cols], mg_ref[half:, cols]], axis=1)
        for d in (2, 1, 3):
            start(dcopy(slot, d))
        drecv[slot, z] = dpack[z, slot]

    def arrive(slot):
        for d in range(1, PLANES):
            dcopy(slot, d).wait_recv()

    exchange = {}

    def swap(index, src, dst):
        exchange[index] = remote(src, dst, esend.at[index], erecv.at[index], to_core)
        start(exchange[index])

    def arrived(*indices):
        for index in indices:
            copy = exchange.pop(index, None)
            if copy is not None:
                copy.wait_recv()

    if weights:
        swap(0, lt_a.at[:, :, 1 - core], ltp_a)
        swap(1, branch_ref, rp_branch)
        swap(2, lt_n2.at[:, :, 1 - core], ltp_n2)
        swap(3, ug_ref, rp_ug)
        swap(4, lt_act.at[:, :, 1 - core], ltp_act)
        swap(5, dout_ref, rp_dout)
        swap(6, lt_n.at[:, :, 1 - core], ltp_n)

    if attention:
        for k in range(PLANES):
            masks[k] = position_masks(spans_ref, plane, length, c, k, rows).astype(BF16)
        first, end = spans_ref[0, 0], length - spans_ref[0, 1]

    def vectors(value, result):
        stages = [
            (vbuf_y, group, groups, at_group, 2),
            (vbuf_c, core, 2, lambda e: to_core, 0),
            (vbuf_x, column, lines, lambda e: at_x(z, c, plane, e), 1),
            (vbuf_z, z, PLANES, lambda e: at_z(z, c, plane, e), 3),
        ]

        def copies(stage):
            buf, me, count, partner, axis = stages[stage]
            return [
                remote(
                    buf.at[me], buf.at[me],
                    vsend.at[axis, e], vrecv.at[axis, e], partner(e),
                )
                for e in range(1, count)
            ]

        def step(stage):
            if stage == 0:
                total = value()
            else:
                buf, me, count, partner, axis = stages[stage - 1]
                for copy in copies(stage - 1):
                    copy.wait_recv()
                total = buf[0]
                for i in range(1, count):
                    total = total + buf[i]
            if stage == len(stages):
                result[...] = total
                return
            buf, me = stages[stage][:2]
            buf[me] = total
            for copy in copies(stage):
                start(copy)

        return step

    def bufs(piece):
        if piece == VALUE:
            return 0, wbuf_v, gy_v, gx_v, sx_v, sy_v, zs_v, zg_v, fin_v
        return piece, wbuf, gy, gx, sx, sy, zs, zg, fin

    def make(piece):
        i, buf = bufs(piece)[:2]
        count = PLANES * lines * shard
        if piece == OUT:
            arrived(0, 1)
            mine, theirs = lt_a[:, :, core, 0], ltp_a[:, :, 0]
            right, other = branch_ref[...], rp_branch[...]
        elif piece < DOWN:
            arrived(2, 3)
            cols = slice((piece - UP) * width, (piece - UP + 1) * width)
            mine, theirs = lt_n2[:, :, core, 0], ltp_n2[:, :, 0]
            right, other = ug_ref[:, cols], rp_ug[:, cols]
        elif piece < QUERY:
            arrived(4, 5)
            mine, theirs = lt_act[:, :, core, piece - DOWN], ltp_act[:, :, piece - DOWN]
            right, other = dout_ref[...], rp_dout[...]
        else:
            arrived(6, 7)
            at = (piece - QUERY) * width
            cols = slice(at, at + (width // 2 if piece == VALUE else width))
            mine, theirs = lt_n[:, :, core, 0], ltp_n[:, :, 0]
            right, other = late_r[:, cols], rp_late[:, cols]
        grad = dot(mine.reshape(count, rows), right, NN) + dot(theirs.reshape(count, rows), other, NN)
        lanes = grad.shape[1] // groups
        for h in range(groups):
            for zz in range(PLANES):
                for xx in range(lines):
                    at = (zz * lines + xx) * shard
                    buf[i, h, xx, zz] = grad[at : at + shard, h * lanes : (h + 1) * lanes].astype(BF16)
        for copy in first_copies(piece):
            start(copy)

    def first_copies(piece):
        i, buf, gy_b, gx_b = bufs(piece)[:4]
        n = piece
        if piece in LINE_FIRST:
            return [
                remote(
                    buf.at[i, :, lax.rem(column + e, lines)], gx_b.at[i, e - 1],
                    s1send.at[n, e], s1recv.at[n, e], at_x(z, c, plane, e),
                )
                for e in range(1, lines)
            ]
        return [
            remote(
                buf.at[i, lax.rem(group + e, groups)], gy_b.at[i, e - 1],
                s1send.at[n, e], s1recv.at[n, e], at_group(e),
            )
            for e in range(1, groups)
        ]

    def second_copies(piece):
        i, buf, gy_b, gx_b, sx_b, sy_b = bufs(piece)[:6]
        n = piece
        if piece in LINE_FIRST:
            return [
                remote(
                    sy_b.at[i, e - 1], gy_b.at[i, e - 1, 0],
                    s2send.at[n, e], s2recv.at[n, e], at_group(e),
                )
                for e in range(1, groups)
            ]
        return [
            remote(
                sx_b.at[i, e - 1], gx_b.at[i, e - 1, 0],
                s2send.at[n, e], s2recv.at[n, e], at_x(z, c, plane, e),
            )
            for e in range(1, lines)
        ]

    def first_total(piece, at):
        i, buf, gy_b, gx_b = bufs(piece)[:4]
        if piece in LINE_FIRST:
            value = buf[i, at, column].astype(F32)
            for e in range(1, lines):
                value = value + gx_b[i, e - 1, at].astype(F32)
            return value
        value = buf[i, group, at].astype(F32)
        for e in range(1, groups):
            value = value + gy_b[i, e - 1, at].astype(F32)
        return value

    def second(piece):
        i, buf, gy_b, gx_b, sx_b, sy_b = bufs(piece)[:6]
        for copy in first_copies(piece):
            copy.wait_recv()
        if piece in LINE_FIRST:
            for e in range(1, groups):
                sy_b[i, e - 1] = first_total(piece, lax.rem(group + e, groups)).astype(BF16)
        else:
            for e in range(1, lines):
                sx_b[i, e - 1] = first_total(piece, lax.rem(column + e, lines)).astype(BF16)
        for copy in second_copies(piece):
            start(copy)

    def third_copies(piece):
        i = bufs(piece)[0]
        zs_b, zg_b = bufs(piece)[6:8]
        n = piece
        return [
            remote(
                zs_b.at[i, lax.rem(z + d, PLANES)], zg_b.at[i, d - 1],
                wzsend.at[n, d], wzrecv.at[n, d], at_z(z, c, plane, d),
            )
            for d in (2, 1, 3)
        ]

    def third(piece):
        i, buf, gy_b, gx_b, sx_b, sy_b, zs_b, zg_b, fin_b = bufs(piece)
        for copy in second_copies(piece):
            copy.wait_recv()
        value = first_total(piece, group if piece in LINE_FIRST else column)
        if piece in LINE_FIRST:
            for e in range(1, groups):
                value = value + gy_b[i, e - 1, 0].astype(F32)
        else:
            for e in range(1, lines):
                value = value + gx_b[i, e - 1, 0].astype(F32)
        zs_b[i] = value.astype(BF16)
        for copy in third_copies(piece):
            start(copy)

    def last_copies(piece):
        i = bufs(piece)[0]
        fin_b = bufs(piece)[8]
        n = piece
        return [
            remote(fin_b.at[i, group], fin_b.at[i, group], fsend.at[n, e], frecv.at[n, e], at_group(e))
            for e in range(1, groups)
        ]

    def fourth(piece):
        i, buf, gy_b, gx_b, sx_b, sy_b, zs_b, zg_b, fin_b = bufs(piece)
        for copy in third_copies(piece):
            copy.wait_recv()
        value = zs_b[i, z].astype(F32)
        for d in range(1, PLANES):
            value = value + zg_b[i, d - 1].astype(F32)
        fin_b[i, group] = value.astype(BF16)
        for copy in last_copies(piece):
            start(copy)

    def finish(piece):
        for copy in last_copies(piece):
            copy.wait_recv()

    span = min(plane, 4)

    def grads(slot, k):
        held = keybuf.at[slot % 2]
        query = query_rows(held[k, c, rows:, :], True)
        grad = query_rows(drecv[slot, k], False)
        both = jnp.concatenate([query, grad], axis=0)
        turned = jnp.transpose(drecv[slot, k].astype(F32))
        turned = jnp.concatenate([turned[:size], turned[size:]], axis=1)
        delta = jnp.sum(turned * o_ref[slot, k], axis=0, keepdims=True)
        lse = lse_ref[slot, k, 0:1, :]
        query_grad = jnp.zeros((2 * size, rows), F32)
        for k2 in range(k, -1, -1):
            level = lse
            if k2 < k and k == PLANES - 1:
                position = k * plane * rows + c * rows + lax.broadcasted_iota(jnp.int32, (1, rows), 1)
                level = jnp.where(position >= end, -NEG_FILL, lse)
            for at in range(0, plane, span):
                where = slice(at * rows, (at + span) * rows)
                keys = held[k2, at : at + span, :rows, :].reshape(span * rows, 2 * size)
                scores = dot(keys, query, NT)
                prob_grad = dot(keys, grad, NT)
                if k2 == k:
                    scores = scores + masks[k, where, :].astype(F32)
                elif k2 == 0 and at == 0:
                    index = lax.broadcasted_iota(jnp.int32, (span * rows, 1), 0)
                    scores = scores + jnp.where(index < first, NEG_FILL, 0.0)
                prob = jnp.exp(scores - level)
                score_grad = (prob * (prob_grad - delta)).astype(BF16)
                update = dot(jnp.concatenate([score_grad, prob.astype(BF16)], axis=1), both, NN)
                if k2 == k:
                    acc[slot % 2, k2, where] = update
                else:
                    acc[slot % 2, k2, where] += update
                query_grad = query_grad + dot(keys, score_grad, TN)
        packed = jnp.concatenate([query_grad[:size, :half], query_grad[:size, half:]], axis=0)
        ret[k, slot, rows:, :] = jnp.transpose(packed).astype(BF16)

    def mine(slot, k, col):
        return acc[slot % 2, k, pl.ds(pl.multiple_of(col * rows, rows), rows), :]

    def ccopy(slot, line):
        return remote(
            part.at[slot, line], cgot.at[slot, line],
            csend.at[slot, line], crecv.at[slot, line], to_core,
        )

    def xcopy(slot, e):
        return remote(
            xpart.at[slot, e - 1], xgot.at[slot, e - 1],
            xsend.at[slot, e], xrecv.at[slot, e], at_x(z, c, plane, e),
        )

    def rcopy(slot, d):
        return remote(
            ret.at[lax.rem(z + d, PLANES), slot], got.at[slot, z],
            rsend.at[slot, d], rrecv.at[slot, d], at_z(z, c, plane, d),
        )

    def reduce_core(slot):
        for line in range(lines):
            for k in range(PLANES):
                part[slot, line, k] = mine(slot, k, 2 * line + 1 - core).astype(BF16)
            start(ccopy(slot, line))

    def reduce_line(slot):
        for line in range(lines):
            ccopy(slot, line).wait_recv()
        for e in range(1, lines):
            line = lax.rem(column + e, lines)
            for k in range(PLANES):
                xpart[slot, e - 1, k] = (
                    mine(slot, k, 2 * line + core) + cgot[slot, line, k].astype(F32)
                ).astype(BF16)
            start(xcopy(slot, e))

    def reduce_end(slot):
        for e in range(1, lines):
            xcopy(slot, e).wait_recv()
        for k in range(PLANES):
            total = mine(slot, k, c) + cgot[slot, column, k].astype(F32)
            for e in range(1, lines):
                total = total + xgot[slot, e - 1, k].astype(F32)
            ret[k, slot, :rows, :] = total.astype(BF16)
        for d in (2, 1, 3):
            start(rcopy(slot, d))
        got[slot, z] = ret[z, slot]

    def late_factors():
        for slot in range(SLOTS):
            for d in range(1, PLANES):
                rcopy(slot, d).wait_recv()
        for pair in range(HEADS // 2):
            at = pair * 2 * size
            keys, values, queries = [], [], []
            for head in (2 * pair, 2 * pair + 1):
                src, slot = divmod(head, SLOTS)
                block = got[slot, src].astype(F32)
                keys.append(block[:rows, :size])
                values.append(block[:rows, size:])
                queries.append(jnp.concatenate([block[rows:, :size], block[rows:, size:]], axis=0))
            late_r[:, at : at + 2 * size] = (jnp.concatenate(queries, axis=1) * 0.125).astype(BF16)
            late_r[:, width + at : width + at + 2 * size] = jnp.concatenate(keys, axis=1).astype(BF16)
            if pair < HEADS // 4:
                at = 2 * width + at
                late_r[:, at : at + 2 * size] = jnp.concatenate(values, axis=1).astype(BF16)
            else:
                at = at - width // 2
                gfv_ref[:, at : at + 2 * size] = jnp.concatenate(values, axis=1).astype(BF16)
    def input_grad():
        for copy in later:
            copy.wait()
        normed_grad = (
            dot(late_r[:, :width], wq_ref[...], NT)
            + dot(late_r[:, width : 2 * width], wk_ref[...], NT)
            + dot(late_r[:, 2 * width :], wv_ref[...], NT)
        )
        values = x_ref[...].astype(F32)
        centred = values - jnp.mean(values, axis=-1, keepdims=True)
        scale = lax.rsqrt(jnp.mean(centred * centred, axis=-1, keepdims=True) + EPSILON)
        unit = centred * scale
        inner = normed_grad * g_ref[...].reshape(1, width)
        back = scale * (
            inner
            - jnp.mean(inner, axis=-1, keepdims=True)
            - unit * jnp.mean(inner * unit, axis=-1, keepdims=True)
        )
        gin_ref[...] = hg_ref[...] + back

        def sums(v):
            return jnp.sum(v.astype(F32), axis=0, keepdims=True)

        return jnp.concatenate(
            [
                sums(normed_grad * unit),
                sums(normed_grad),
                sums(late_r[:, :width]),
                jnp.concatenate([sums(late_r[:, 2 * width :]), jnp.zeros((1, width // 2), F32)], axis=1),
                jnp.zeros((4, width), F32),
            ],
            axis=0,
        )

    def do(*tasks):
        for stage, what in tasks if weights else ():
            (make, second, third, fourth, finish)[stage - 1](what)

    do(*BEFORE)
    if attention:
        for slot in range(SLOTS):
            key_copy(slot).wait()
            arrive(slot)
            for k in range(PLANES):
                grads(slot, k)
                if slot and k == 1:
                    reduce_line(slot - 1)
                do(*AT_POINTS.get((slot, k), ()))
            if slot == 0:
                key_copy(2).start()
            reduce_core(slot)
            if slot:
                reduce_end(slot - 1)
    else:
        for tasks in AT_POINTS.values():
            do(*tasks)
    do(*AFTER[0])
    if attention:
        reduce_line(SLOTS - 1)
    do(*AFTER[1])
    if attention:
        reduce_end(SLOTS - 1)
    do(*AFTER[2])
    if attention:
        late_factors()
    if weights:
        swap(7, late_r, rp_late)
        partial = input_grad()
        late_vectors = vectors(lambda: jnp.concatenate([vec_ref[...], partial], axis=0), vec1_ref)
        late_vectors(0)
        for stage, tasks in enumerate(AFTER[3:]):
            do(*tasks)
            if stage < 4:
                late_vectors(stage + 1)
    arrived(*range(8))
    for copy in sent:
        copy.wait_send()


BEFORE = ((1, OUT),)
AT_POINTS = {
    (0, 1): ((1, UP + 2), (1, DOWN)),
    (1, 0): ((2, OUT),),
    (1, 1): ((1, DOWN + 3), (2, UP + 2)),
    (1, 2): ((1, UP + 3), (3, OUT), (1, UP)),
    (2, 1): ((2, DOWN + 3), (2, DOWN)),
    (2, 2): ((3, UP + 2),),
}
AFTER = (
    (),
    ((2, UP), (1, UP + 1), (4, OUT), (1, DOWN + 2)),
    ((1, DOWN + 1), (2, UP + 1), (3, DOWN + 3), (2, DOWN + 1), (3, DOWN), (4, UP + 2)),
    ((3, UP + 1), (3, UP), (2, UP + 3), (1, QUERY)),
    ((1, KEY), (3, DOWN + 1)),
    ((4, DOWN), (2, DOWN + 2), (4, UP + 1), (1, VALUE)),
    ((2, QUERY), (3, DOWN + 2), (3, UP + 3)),
    (
        (4, DOWN + 1), (5, UP + 2), (4, DOWN + 3), (2, KEY), (2, VALUE), (3, QUERY), (3, KEY), (3, VALUE), (4, UP),
        (4, UP + 3), (4, DOWN + 2), (4, QUERY), (4, KEY), (4, VALUE), (5, OUT), (5, UP), (5, UP + 1), (5, UP + 3),
        (5, DOWN), (5, DOWN + 1), (5, DOWN + 2), (5, DOWN + 3), (5, QUERY), (5, KEY), (5, VALUE),
    ),
)


def backward_call(plane, groups, rows, width, hidden, attention, weights, arrays):
    blocks = plane * PLANES
    lines = plane // 2
    size = width // HEADS
    half = rows // 2
    shard = width // blocks
    tall = hidden // width
    lw = width // groups
    lv = width // 2 // groups
    late = 2 * width + width // 2
    count = PIECES
    dma = pltpu.SemaphoreType.DMA
    most = max(groups, lines)

    def vmem(*shape):
        return pltpu.VMEM(shape, BF16)

    def vmem32(*shape):
        return pltpu.VMEM(shape, F32)

    any_space = pl.BlockSpec(memory_space=pl.ANY)
    ins = {}
    outs = {}
    scratch = {}
    if attention:
        ins.update(mg_ref=VMEM, all_ref=any_space, o_ref=VMEM, lse_ref=VMEM, spans_ref=SMEM)
        outs.update(gfv_ref=((rows, width // 2), BF16))
        scratch.update(
            dpack=vmem(PLANES, SLOTS, half, 2 * size),
            drecv=vmem(SLOTS, PLANES, half, 2 * size),
            masks=vmem(PLANES, plane * rows, rows),
            acc=vmem32(2, PLANES, plane * rows, 2 * size),
            part=vmem(SLOTS, lines, PLANES, rows, 2 * size),
            cgot=vmem(SLOTS, lines, PLANES, rows, 2 * size),
            xpart=vmem(SLOTS, lines - 1, PLANES, rows, 2 * size),
            xgot=vmem(SLOTS, lines - 1, PLANES, rows, 2 * size),
            ret=vmem(PLANES, SLOTS, rows + half, 2 * size),
            got=vmem(SLOTS, PLANES, rows + half, 2 * size),
            keybuf=vmem(2, PLANES, plane, rows + half, 2 * size),
            keysem=dma((2,)),
            zsend=dma((SLOTS, PLANES)), zrecv=dma((SLOTS, PLANES)),
            csend=dma((SLOTS, lines)), crecv=dma((SLOTS, lines)),
            xsend=dma((SLOTS, lines)), xrecv=dma((SLOTS, lines)),
            rsend=dma((SLOTS, PLANES)), rrecv=dma((SLOTS, PLANES)),
        )
        if weights:
            scratch.update(late_own=vmem(rows, late))
        else:
            outs.update(late_out=((rows, late), BF16))
    if weights:
        ins.update(
            lt_a=VMEM, lt_n2=VMEM, lt_act=VMEM, lt_n=VMEM, branch_ref=VMEM, ug_ref=VMEM, dout_ref=VMEM, vec_ref=VMEM,
            g_ref=VMEM, x_hbm=any_space, hg_hbm=any_space, wq_hbm=any_space, wk_hbm=any_space, wv_hbm=any_space,
        )
        scratch.update(
            x_ref=vmem(rows, width), hg_ref=vmem32(rows, width), lsem=dma((5,)),
            wq_ref=vmem(width, width), wk_ref=vmem(width, width), wv_ref=vmem(width, width // 2),
        )
        if not attention:
            ins.update(late_in=VMEM)
        outs.update(
            gin_ref=((rows, width), F32), vec1_ref=((16, width), F32),
            fin=((count - 1, groups, shard, lw), BF16), fin_v=((1, groups, shard, lv), BF16),
        )
        scratch.update(
            ltp_a=vmem(PLANES, lines, 1, shard, rows),
            ltp_n2=vmem(PLANES, lines, 1, shard, rows),
            ltp_act=vmem(PLANES, lines, tall, shard, rows),
            ltp_n=vmem(PLANES, lines, 1, shard, rows),
            rp_branch=vmem(rows, width), rp_ug=vmem(rows, hidden), rp_dout=vmem(rows, width), rp_late=vmem(rows, late),
            vbuf_c=vmem32(2, 16, width), vbuf_x=vmem32(lines, 16, width),
            vbuf_y=vmem32(groups, 16, width), vbuf_z=vmem32(PLANES, 16, width),
            esend=dma((8,)), erecv=dma((8,)),
            s1send=dma((count, most)), s1recv=dma((count, most)),
            s2send=dma((count, most)), s2recv=dma((count, most)),
            wzsend=dma((count, PLANES)), wzrecv=dma((count, PLANES)),
            fsend=dma((count, groups)), frecv=dma((count, groups)),
            vsend=dma((4, max(most, PLANES))), vrecv=dma((4, max(most, PLANES))),
        )
        for tag, n, lanes in (("", count - 1, lw), ("_v", 1, lv)):
            scratch.update({
                "wbuf" + tag: vmem(n, groups, lines, PLANES, shard, lanes),
                "gy" + tag: vmem(n, groups - 1, lines, PLANES, shard, lanes),
                "gx" + tag: vmem(n, lines - 1, groups if LINE_FIRST else 1, PLANES, shard, lanes),
                "sx" + tag: vmem(n, lines - 1, PLANES, shard, lanes),
                "zs" + tag: vmem(n, PLANES, shard, lanes),
                "zg" + tag: vmem(n, PLANES - 1, shard, lanes),
            })
            if LINE_FIRST:
                scratch["sy" + tag] = vmem(n, groups - 1, PLANES, shard, lanes)
    names = tuple(ins) + tuple(outs) + tuple(scratch)
    result = pl.pallas_call(
        functools.partial(backward_kernel, plane, groups, shard, names, attention, weights),
        name="backward",
        out_shape=tuple(jax.ShapeDtypeStruct(*v) for v in outs.values()),
        in_specs=list(ins.values()),
        out_specs=(VMEM,) * len(outs),
        scratch_shapes=list(scratch.values()),
        compiler_params=pltpu.CompilerParams(
            collective_id=2 if attention else 3, has_side_effects=True, vmem_limit_bytes=61 << 20
        ),
    )(*[arrays[name] for name in ins])
    return dict(zip(outs, result))


def tail_kernel(
    gin_ref, gfv_ref, vec1_ref, fin_ref, finv_ref,
    o_gin, o_gfv, o_g1, o_s1, o_wq, o_bq, o_wk, o_wv, o_bv, o_wo, o_bo, o_g2, o_s2, o_wu, o_bu, o_wd, o_bd,
):
    groups, shard, lanes = fin_ref.shape[1:]
    width = groups * lanes
    tall = o_wd.shape[0] // shard
    o_gin[...] = gin_ref[...]
    o_gfv[...] = gfv_ref[...]

    def put(ref, rows, at, piece):
        for h in range(groups):
            ref[rows, at + h * lanes : at + (h + 1) * lanes] = fin_ref[piece, h].astype(F32)

    everything = slice(0, shard)
    put(o_wo, everything, 0, OUT)
    put(o_wq, everything, 0, QUERY)
    put(o_wk, everything, 0, KEY)
    for i in range(tall):
        put(o_wu, everything, i * width, UP + i)
        put(o_wd, slice(i * shard, (i + 1) * shard), 0, DOWN + i)
    for h in range(groups):
        o_wv[:, h * (lanes // 2) : (h + 1) * (lanes // 2)] = finv_ref[0, h].astype(F32)
    o_g2[...], o_s2[...], o_bo[...], o_bd[...] = vec1_ref[0], vec1_ref[1], vec1_ref[2], vec1_ref[3 + tall]
    for i in range(tall):
        o_bu[i * width : (i + 1) * width] = vec1_ref[3 + i]
    o_g1[...], o_s1[...], o_bq[...] = vec1_ref[8], vec1_ref[9], vec1_ref[10]
    o_bv[...] = vec1_ref[11, : width // 2]


def tail_part(rows, width, hidden, shard, got):
    def out(*shape):
        return jax.ShapeDtypeStruct(shape, F32)

    return pl.pallas_call(
        tail_kernel,
        name="tail",
        out_shape=(
            out(rows, width), jax.ShapeDtypeStruct((rows, width // 2), BF16), out(width), out(width),
            out(shard, width), out(width), out(shard, width), out(shard, width // 2), out(width // 2),
            out(shard, width), out(width), out(width), out(width),
            out(shard, hidden), out(hidden), out(hidden // width * shard, width), out(width),
        ),
        in_specs=[VMEM] * 5,
        out_specs=(VMEM,) * 17,
    )(*got)


def body(
    inputs,
    first_values,
    spans,
    ln1_gain,
    ln1_shift,
    w_query,
    b_query,
    w_key,
    w_value,
    b_value,
    w_out,
    b_out,
    ln2_gain,
    ln2_shift,
    w_up,
    b_up,
    w_down,
    b_down,
    out_grad,
):
    rows, width = inputs.shape
    hidden = w_up.shape[1]
    groups = lax.axis_size("grp")
    plane = lax.axis_size("blk") // PLANES
    attended, normed, all_blocks, mixed, lse = forward_part(
        inputs, first_values, spans, ln1_gain, ln1_shift, w_query, b_query, w_key, w_value, b_value
    )
    result, mixed_grad, hidden_grad, branch_grad, upper_grad, grad_down, vectors, lt_a, lt_n2, lt_act, lt_n = middle_part(
        plane, inputs, attended, normed, spans, out_grad, b_out, ln2_gain, ln2_shift, b_up, b_down, w_out, w_up, w_down
    )
    arrays = dict(
        mg_ref=mixed_grad, all_ref=all_blocks, o_ref=mixed, lse_ref=lse, spans_ref=spans,
        lt_a=lt_a, lt_n2=lt_n2, lt_act=lt_act, lt_n=lt_n,
        branch_ref=branch_grad, ug_ref=upper_grad, dout_ref=grad_down, vec_ref=vectors,
        x_hbm=inputs, g_ref=ln1_gain, hg_hbm=hidden_grad, wq_hbm=w_query, wk_hbm=w_key, wv_hbm=w_value,
    )
    call = functools.partial(backward_call, plane, groups, rows, width, hidden)
    if plane <= 4:
        got = Refs(call(True, True, arrays))
    else:
        got = Refs(call(True, False, arrays))
        arrays.update(late_in=got.late_out)
        got.update(call(False, True, arrays))
    return (result,) + tuple(
        tail_part(
            rows, width, hidden, width // (plane * PLANES),
            (got.gin_ref, got.gfv_ref, got.vec1_ref, got.fin, got.fin_v),
        )
    )


def solution(mesh):
    placed = (
        P(("grp", "blk"), None),
        P(("grp", "blk"), None),
        P("grp", None),
        P(),
        P(),
        P(),
        P(),
        P(),
        P(),
        P(),
        P(),
        P(),
        P(),
        P(),
        P(),
        P(),
        P(),
        P(),
        P(("grp", "blk"), None),
    )
    return jax.shard_map(
        body,
        mesh=mesh,
        in_specs=placed,
        out_specs=(
            P(("grp", "blk"), None),
            P(("grp", "blk"), None),
            P(("grp", "blk"), None),
            P(),
            P(),
            P("blk", None),
            P(),
            P("blk", None),
            P("blk", None),
            P(),
            P("blk", None),
            P(),
            P(),
            P(),
            P("blk", None),
            P(),
            P("blk", None),
            P(),
        ),
        check_vma=False,
    )
```

```python
import functools

import jax
import jax.numpy as jnp
from jax import lax
from jax.experimental import pallas as pl
from jax.experimental.pallas import tpu as pltpu
from jax.sharding import PartitionSpec as P

HEADS = 12
PLANES = 4
SLOTS = HEADS // PLANES
EPSILON = 1e-05
GELU_COEF = 0.7978845608028654
NEG_FILL = -1e30
BF16 = jnp.bfloat16
F32 = jnp.float32
MESH = pl.DeviceIdType.MESH
VMEM = pl.BlockSpec(memory_space=pltpu.VMEM)
SMEM = pl.BlockSpec(memory_space=pltpu.SMEM)


def dot(a, b, dims):
    return lax.dot_general(a, b, (dims, ((), ())), preferred_element_type=F32)


NN = ((1,), (0,))
NT = ((1,), (1,))
TN = ((0,), (0,))


def norm_rows(values, gain, shift):
    average = jnp.mean(values, axis=-1, keepdims=True)
    centred = values - average
    variance = jnp.mean(centred * centred, axis=-1, keepdims=True)
    return centred * lax.rsqrt(variance + EPSILON) * gain + shift


def place(plane):
    block = lax.axis_index("blk")
    return block // plane, lax.rem(block, plane)


def at_z(z, c, plane, offset):
    return {"blk": lax.rem(z + offset, PLANES) * plane + c}


def at_x(z, c, plane, offset):
    lines = plane // 2
    column, core = c // 2, lax.rem(c, 2)
    return {"blk": z * plane + lax.rem(column + offset, lines) * 2 + core}


def at_core(z, c, plane):
    return {"blk": z * plane + (c // 2) * 2 + 1 - lax.rem(c, 2)}


def greet(partners):
    barrier = pltpu.get_barrier_semaphore()
    for partner in partners:
        pl.semaphore_signal(barrier, inc=1, device_id=partner, device_id_type=MESH)
    pl.semaphore_wait(barrier, len(partners))


def remote(src, dst, send, recv, partner):
    return pltpu.make_async_remote_copy(
        src_ref=src, dst_ref=dst, send_sem=send, recv_sem=recv,
        device_id=partner, device_id_type=MESH,
    )


def query_rows(pack, first):
    half = pack.shape[1] // 2
    lanes = lax.broadcasted_iota(jnp.int32, pack.shape, 1)
    wide = pack.astype(F32)
    other = pltpu.roll(wide, half, 1)
    keep = lanes < half if first else lanes >= half
    top, bottom = (wide, other) if first else (other, wide)
    return jnp.concatenate(
        [jnp.where(keep, top, 0.0), jnp.where(keep, bottom, 0.0)], axis=0
    ).astype(BF16)


def position_masks(spans_ref, plane, length, c, k, rows):
    first, end = spans_ref[0, 0], length - spans_ref[0, 1]
    dead = end - spans_ref[0, 2]
    width = plane * rows
    key = k * width + lax.broadcasted_iota(jnp.int32, (width, rows), 0)
    query = k * width + c * rows + lax.broadcasted_iota(jnp.int32, (width, rows), 1)
    allowed = key <= query
    if k == 0:
        allowed &= ((key >= first) == (query >= first))
    if k == PLANES - 1:
        allowed &= ((key >= end) == (query >= end)) & ((key < dead) | (key >= end))
    return jnp.where(allowed, 0.0, NEG_FILL)


def forward_kernel(
    plane, x_ref, fv_ref, spans_ref, g_ref, s_ref, wq_hbm, bq_ref, wk_hbm, wv_hbm, bv_ref,
    att_ref, normed_ref, all_out, o_ref, lse_ref,
    wq_ref, wk_ref, wv_ref, wsem, all_ref, allsem, pack, opack, orecv, masks,
    zsend, zrecv, xsend, xrecv, csend, crecv, osend, orecv_sem,
):
    rows, width = x_ref.shape
    size = width // HEADS
    lines = plane // 2
    length = rows * plane * PLANES
    half = rows // 2
    weights = [
        pltpu.make_async_copy(src, dst, wsem.at[i])
        for i, (src, dst) in enumerate(((wq_hbm, wq_ref), (wk_hbm, wk_ref), (wv_hbm, wv_ref)))
    ]
    for copy in weights:
        copy.start()
    z, c = place(plane)
    core = lax.rem(c, 2)
    greet(
        [at_z(z, c, plane, d) for d in range(1, PLANES)]
        + [at_x(z, c, plane, d) for d in range(1, lines)]
        + [at_core(z, c, plane)]
    )
    normed = norm_rows(
        x_ref[...].astype(F32), g_ref[...].reshape(1, width), s_ref[...].reshape(1, width)
    ).astype(BF16)
    normed_ref[...] = normed
    for copy in weights:
        copy.wait()
    query = ((dot(normed, wq_ref[...], NN) + bq_ref[...].reshape(1, width)) * 0.125)
    key = dot(normed, wk_ref[...], NN)
    fresh = dot(normed, wv_ref[...], NN) + bv_ref[...].reshape(1, width // 2)
    value = jnp.concatenate([fresh, fv_ref[...].astype(F32)], axis=1)
    zcopies = {}
    for slot in range(SLOTS):
        for to in range(PLANES):
            head = to * SLOTS + slot
            cols = slice(head * size, (head + 1) * size)
            pack[to, slot, :rows, :] = jnp.concatenate(
                [key[:, cols], value[:, cols]], axis=1
            ).astype(BF16)
            pack[to, slot, rows:, :] = jnp.concatenate(
                [query[:half, cols], query[half:, cols]], axis=1
            ).astype(BF16)
        for d in (2, 1, 3):
            to = lax.rem(z + d, PLANES)
            copy = remote(
                pack.at[to, slot], all_ref.at[slot, z, c],
                zsend.at[slot, d], zrecv.at[slot, d], at_z(z, c, plane, d),
            )
            copy.start()
            zcopies[slot, d] = copy
        all_ref[slot, z, c] = pack[z, slot]

    started = []

    def hand_out(slot, d):
        block = all_ref.at[slot, lax.rem(z + PLANES - d, PLANES), c, pl.ds(0, rows)]
        for e in range(1, lines):
            copy = remote(
                block, block, xsend.at[slot, d, e], xrecv.at[slot, d, e], at_x(z, c, plane, e)
            )
            copy.start()
            started.append(copy)
        copy = remote(block, block, csend.at[slot, d, 0], crecv.at[slot, d, 0], at_core(z, c, plane))
        copy.start()
        started.append(copy)

    for slot in range(SLOTS):
        hand_out(slot, 0)
    for k in range(PLANES):
        masks[k] = position_masks(spans_ref, plane, length, c, k, rows)
    first, end = spans_ref[0, 0], length - spans_ref[0, 1]

    def spread(slot):
        for d in (1, 3, 2):
            zcopies[slot, d].wait_recv()
            hand_out(slot, d)

    def pass_on(slot):
        for d in (0, 1, 3, 2):
            src = lax.rem(z + PLANES - d, PLANES)
            for e in range(1, lines):
                column = lax.rem(c // 2 + lines - e, lines) * 2 + core
                block = all_ref.at[slot, src, column, pl.ds(0, rows)]
                remote(
                    block, block, xsend.at[slot, d, e], xrecv.at[slot, d, e], at_x(z, c, plane, e)
                ).wait_recv()
                copy = remote(
                    block, block, csend.at[slot, d, e], crecv.at[slot, d, e], at_core(z, c, plane)
                )
                copy.start()
                started.append(copy)

    def settle(slot):
        for d in range(PLANES):
            for e in range(lines):
                block = all_ref.at[slot, 0, c, pl.ds(0, rows)]
                remote(
                    block, block, csend.at[slot, d, e], crecv.at[slot, d, e], at_core(z, c, plane)
                ).wait_recv()

    def keys_of(slot, k):
        return all_ref[slot, k, :, :rows, :].reshape(plane * rows, 2 * size)

    def attend(slot, k):
        q = query_rows(all_ref[slot, k, c, rows:, :], True)

        def step(state, k2, bias):
            top, total, acc = state
            count = plane
            blocks = [all_ref[slot, k2, b, :rows, :] for b in range(count)]
            scores = [bias(dot(blocks[b], q, NT), b) for b in range(count)]
            new = top
            for part in scores:
                new = jnp.maximum(new, jnp.max(part, axis=0, keepdims=True))
            scale = jnp.exp(top - new)
            total, acc = total * scale, acc * scale
            for b in range(count):
                prob = jnp.exp(scores[b] - new)
                total = total + jnp.sum(prob, axis=0, keepdims=True)
                acc = acc + dot(blocks[b], prob.astype(BF16), TN)
            return new, total, acc

        state = (
            jnp.full((1, rows), NEG_FILL, F32),
            jnp.zeros((1, rows), F32),
            jnp.zeros((2 * size, rows), F32),
        )
        state = step(state, k, lambda t, b: t + masks[k, b * rows : (b + 1) * rows])
        diagonal = state
        for k2 in range(k):
            if k2 == 0:
                index = lax.broadcasted_iota(jnp.int32, (rows, 1), 0)
                shut = jnp.where(index < first, NEG_FILL, 0.0)
                state = step(state, k2, lambda t, b: t + shut if b == 0 else t)
            else:
                state = step(state, k2, lambda t, b: t)
        if k == PLANES - 1:
            position = k * plane * rows + c * rows + lax.broadcasted_iota(jnp.int32, (1, rows), 1)
            after = position >= end
            state = tuple(jnp.where(after, old, new) for old, new in zip(diagonal, state))
        top, total, acc = state
        mixed = acc[size:] / total
        o_ref[slot, k] = mixed
        lse_ref[slot, k] = jnp.broadcast_to(top + jnp.log(total), (8, rows))
        packed = jnp.concatenate([mixed[:, :half], mixed[:, half:]], axis=0)
        opack[slot, k] = jnp.transpose(packed).astype(BF16)

    def back(slot, k, src):
        return remote(
            opack.at[slot, k], orecv.at[slot, src],
            osend.at[slot, k], orecv_sem.at[slot, src], {"blk": k * plane + c},
        )

    def give_back(slot, k):
        @pl.when(z == k)
        def _():
            orecv[slot, k] = opack[slot, k]

        @pl.when(z != k)
        def _():
            back(slot, k, z).start()

    kept = []
    spread(0)
    pass_on(0)
    settle(0)
    spread(1)
    for slot in range(SLOTS):
        if slot:
            settle(slot)
        keep = pltpu.make_async_copy(all_ref.at[slot], all_out.at[slot], allsem.at[slot])
        keep.start()
        kept.append(keep)
        for k in (3, 2, 0, 1):
            attend(slot, k)
            give_back(slot, k)
        if slot + 2 < SLOTS:
            spread(slot + 2)
        if slot + 1 < SLOTS:
            pass_on(slot + 1)
    for slot in range(SLOTS):
        for k in range(PLANES):
            @pl.when(z != k)
            def _(slot=slot, k=k):
                back(slot, 0, k).wait_recv()
    for pair in range(HEADS // 2):
        parts = []
        for head in (2 * pair, 2 * pair + 1):
            src, slot = divmod(head, SLOTS)
            got = orecv[slot, src].astype(F32)
            parts.append(jnp.concatenate([got[:, :size], got[:, size:]], axis=0))
        att_ref[:, pair * 2 * size : (pair + 1) * 2 * size] = jnp.concatenate(parts, axis=1).astype(BF16)
    for slot in range(SLOTS):
        for k in range(PLANES):
            @pl.when(z != k)
            def _(slot=slot, k=k):
                back(slot, k, 0).wait_send()
    for keep in kept:
        keep.wait()
    for copy in list(zcopies.values()) + started:
        copy.wait_send()


def forward_part(inputs, first_values, spans, ln1_gain, ln1_shift, w_query, b_query, w_key, w_value, b_value):
    rows, width = inputs.shape
    plane = lax.axis_size("blk") // PLANES
    lines = plane // 2
    size = width // HEADS
    half = rows // 2
    dma = pltpu.SemaphoreType.DMA
    anywhere = pl.BlockSpec(memory_space=pl.ANY)
    return pl.pallas_call(
        functools.partial(forward_kernel, plane),
        name="forward",
        out_shape=(
            jax.ShapeDtypeStruct((rows, width), BF16),
            jax.ShapeDtypeStruct((rows, width), BF16),
            jax.ShapeDtypeStruct((SLOTS, PLANES, plane, rows + half, 2 * size), BF16),
            jax.ShapeDtypeStruct((SLOTS, PLANES, size, rows), F32),
            jax.ShapeDtypeStruct((SLOTS, PLANES, 8, rows), F32),
        ),
        in_specs=[VMEM, VMEM, SMEM, VMEM, VMEM, anywhere, VMEM, anywhere, anywhere, VMEM],
        out_specs=(VMEM, VMEM, anywhere, VMEM, VMEM),
        scratch_shapes=[
            pltpu.VMEM(w_query.shape, BF16), pltpu.VMEM(w_key.shape, BF16), pltpu.VMEM(w_value.shape, BF16),
            dma((3,)),
            pltpu.VMEM((SLOTS, PLANES, plane, rows + half, 2 * size), BF16),
            dma((SLOTS,)),
            pltpu.VMEM((PLANES, SLOTS, rows + half, 2 * size), BF16),
            pltpu.VMEM((SLOTS, PLANES, half, 2 * size), BF16),
            pltpu.VMEM((SLOTS, PLANES, half, 2 * size), BF16),
            pltpu.VMEM((PLANES, plane * rows, rows), F32),
            dma((SLOTS, PLANES)), dma((SLOTS, PLANES)),
            dma((SLOTS, PLANES, lines)), dma((SLOTS, PLANES, lines)),
            dma((SLOTS, PLANES, lines)), dma((SLOTS, PLANES, lines)),
            dma((SLOTS, PLANES)), dma((SLOTS, PLANES)),
        ],
        compiler_params=pltpu.CompilerParams(
            collective_id=1, has_side_effects=True, vmem_limit_bytes=56 << 20
        ),
    )(
        inputs, first_values, spans, ln1_gain, ln1_shift, w_query, b_query, w_key, w_value, b_value,
    )


def middle_kernel(
    x_ref, att_ref, normed_ref, spans_ref, og_ref, bo_ref, g_ref, s_ref, bu_ref, bd_ref,
    wo_hbm, wu_hbm, wd_hbm,
    result_ref, mg_ref, hg_ref, branch_ref, ug_ref, dout_ref, vec_ref, lt_a, lt_n2, lt_act, lt_n,
    wo_ref, wu_ref, wd_ref, sem,
):
    rows, width = x_ref.shape
    tall = bu_ref.shape[0] // width
    shard = lt_a.shape[4]
    copies = [pltpu.make_async_copy(wo_hbm, wo_ref, sem.at[0])]
    for i in range(tall):
        part = pl.ds(i * width, width)
        copies.append(pltpu.make_async_copy(wu_hbm.at[:, part], wu_ref.at[:, part], sem.at[1 + 2 * i]))
        copies.append(pltpu.make_async_copy(wd_hbm.at[part], wd_ref.at[part], sem.at[2 + 2 * i]))
    for copy in copies:
        copy.start()

    def turn(value, dst, piece):
        turned = jnp.transpose(value)
        at = 0
        span = width // (dst.shape[0] * dst.shape[1] * 2)
        if dst.shape[3] == 1:
            for zz in range(dst.shape[0]):
                for xx in range(dst.shape[1]):
                    for cc in range(2):
                        dst[zz, xx, cc, 0] = turned[at : at + span]
                        at += span
            return
        per = dst.shape[3]
        for unit in range(width // span):
            index = piece * (width // span) + unit
            owner, part = divmod(index, per)
            chip, cc = divmod(owner, 2)
            zz, xx = divmod(chip, dst.shape[1])
            dst[zz, xx, cc, part] = turned[unit * span : (unit + 1) * span]

    def sums(value):
        return jnp.sum(value.astype(F32), axis=0, keepdims=True)

    block = lax.axis_index("blk")
    length = rows * lax.axis_size("blk")
    end = length - spans_ref[0, 1]
    position = block * rows + lax.broadcasted_iota(jnp.int32, (rows, 1), 0)
    alive = (position < end - spans_ref[0, 2]) | (position >= end)
    dout = jnp.where(alive, og_ref[...].astype(F32), 0.0)
    dout_low = dout.astype(BF16)
    dout_ref[...] = dout_low
    vec_ref[3 + tall : 4 + tall, :] = sums(dout)
    attended = att_ref[...]
    turn(normed_ref[...], lt_n, 0)
    turn(attended, lt_a, 0)
    copies[0].wait()
    hidden = x_ref[...].astype(F32) + dot(attended, wo_ref[...], NN) + bo_ref[...].reshape(1, width)
    average = jnp.mean(hidden, axis=-1, keepdims=True)
    centred = hidden - average
    scale = lax.rsqrt(jnp.mean(centred * centred, axis=-1, keepdims=True) + EPSILON)
    unit = centred * scale
    gain = g_ref[...].reshape(1, width)
    normed2 = (unit * gain + s_ref[...].reshape(1, width)).astype(BF16)
    turn(normed2, lt_n2, 0)
    result = hidden + bd_ref[...].reshape(1, width)
    normed2_grad = jnp.zeros((rows, width), F32)
    for i in range(tall):
        cols = slice(i * width, (i + 1) * width)
        copies[1 + 2 * i].wait()
        copies[2 + 2 * i].wait()
        upper = dot(normed2, wu_ref[:, cols], NN) + bu_ref[cols].reshape(1, width)
        square = upper * upper
        curve = jnp.tanh(GELU_COEF * (upper + 0.044715 * upper * square))
        half = 0.5 * (1.0 + curve)
        active = (upper * half).astype(BF16)
        slope = half + 0.5 * upper * (1.0 - curve * curve) * (GELU_COEF * (1.0 + 3.0 * 0.044715 * square))
        turn(active, lt_act, i)
        result = result + dot(active, wd_ref[cols, :], NN)
        upper_grad = (dot(dout_low, wd_ref[cols, :], NT) * slope).astype(BF16)
        ug_ref[:, cols] = upper_grad
        vec_ref[3 + i : 4 + i, :] = sums(upper_grad)
        normed2_grad = normed2_grad + dot(upper_grad, wu_ref[:, cols], NT)
    result_ref[...] = result
    vec_ref[0:1, :] = sums(normed2_grad * unit)
    vec_ref[1:2, :] = sums(normed2_grad)
    inner = normed2_grad * gain
    back = scale * (
        inner - jnp.mean(inner, axis=-1, keepdims=True) - unit * jnp.mean(inner * unit, axis=-1, keepdims=True)
    )
    hidden_grad = dout + back
    hg_ref[...] = hidden_grad
    branch = hidden_grad.astype(BF16)
    branch_ref[...] = branch
    vec_ref[2:3, :] = sums(branch)
    mg_ref[...] = dot(branch, wo_ref[...], NT).astype(BF16)


def middle_part(plane, inputs, attended, normed, spans, out_grad, b_out, gain, shift, b_up, b_down, w_out, w_up, w_down):
    rows, width = inputs.shape
    hidden = w_up.shape[1]
    tall = hidden // width
    lines = plane // 2
    shard = width // (plane * PLANES)

    def low(*shape):
        return jax.ShapeDtypeStruct(shape, BF16)

    any_space = pl.BlockSpec(memory_space=pl.ANY)
    return pl.pallas_call(
        middle_kernel,
        name="middle",
        out_shape=(
            jax.ShapeDtypeStruct((rows, width), F32), low(rows, width), jax.ShapeDtypeStruct((rows, width), F32),
            low(rows, width), low(rows, hidden), low(rows, width), jax.ShapeDtypeStruct((4 + tall, width), F32),
            low(PLANES, lines, 2, 1, shard, rows), low(PLANES, lines, 2, 1, shard, rows),
            low(PLANES, lines, 2, tall, shard, rows), low(PLANES, lines, 2, 1, shard, rows),
        ),
        in_specs=[VMEM, VMEM, VMEM, SMEM] + [VMEM] * 6 + [any_space] * 3,
        out_specs=(VMEM,) * 11,
        scratch_shapes=[
            pltpu.VMEM((width, width), BF16), pltpu.VMEM((width, hidden), BF16), pltpu.VMEM((hidden, width), BF16),
            pltpu.SemaphoreType.DMA((1 + 2 * tall,)),
        ],
        compiler_params=pltpu.CompilerParams(vmem_limit_bytes=56 << 20),
    )(inputs, attended, normed, spans, out_grad, b_out, gain, shift, b_up, b_down, w_out, w_up, w_down)


OUT, UP, DOWN, QUERY, KEY, VALUE = 0, 1, 5, 9, 10, 11
PIECES = 12
LINE_FIRST = frozenset((OUT, DOWN, DOWN + 1, VALUE))


class Refs(dict):
    __getattr__ = dict.get


def backward_kernel(plane, groups, shard, names, attention, weights, *refs):
    r = Refs(zip(names, refs, strict=True))
    mg_ref, all_ref, o_ref, lse_ref, spans_ref, lt_a, lt_n2, lt_act = r.mg_ref, r.all_ref, r.o_ref, r.lse_ref, r.spans_ref, r.lt_a, r.lt_n2, r.lt_act
    lt_n, branch_ref, ug_ref, dout_ref, vec_ref, x_ref, g_ref, hg_ref = r.lt_n, r.branch_ref, r.ug_ref, r.dout_ref, r.vec_ref, r.x_ref, r.g_ref, r.hg_ref
    wq_ref, wk_ref, wv_ref, late_in, gin_ref, gfv_ref, vec1_ref = r.wq_ref, r.wk_ref, r.wv_ref, r.late_in, r.gin_ref, r.gfv_ref, r.vec1_ref
    late_out, dpack = r.late_out, r.dpack
    drecv, masks, acc, part, cgot, xpart, xgot, ret = r.drecv, r.masks, r.acc, r.part, r.cgot, r.xpart, r.xgot, r.ret
    got, keybuf, keysem, ltp_a, ltp_n2, ltp_act, ltp_n, rp_branch = r.got, r.keybuf, r.keysem, r.ltp_a, r.ltp_n2, r.ltp_act, r.ltp_n, r.rp_branch
    rp_ug, rp_dout, late_own, rp_late, wbuf, gy, gx, sx = r.rp_ug, r.rp_dout, r.late_own, r.rp_late, r.wbuf, r.gy, r.gx, r.sx
    sy, zs, zg, fin, wbuf_v, gy_v, gx_v, sx_v = r.sy, r.zs, r.zg, r.fin, r.wbuf_v, r.gy_v, r.gx_v, r.sx_v
    sy_v, zs_v, zg_v, fin_v, vbuf_c, vbuf_x, vbuf_y, vbuf_z = r.sy_v, r.zs_v, r.zg_v, r.fin_v, r.vbuf_c, r.vbuf_x, r.vbuf_y, r.vbuf_z
    zsend, zrecv, csend, crecv, xsend, xrecv, rsend, rrecv = r.zsend, r.zrecv, r.csend, r.crecv, r.xsend, r.xrecv, r.rsend, r.rrecv
    esend, erecv, s1send, s1recv, s2send, s2recv, wzsend, wzrecv = r.esend, r.erecv, r.s1send, r.s1recv, r.s2send, r.s2recv, r.wzsend, r.wzrecv
    fsend, frecv, vsend, vrecv = r.fsend, r.frecv, r.vsend, r.vrecv
    later = [
        pltpu.make_async_copy(src, dst, r.lsem.at[i])
        for i, (src, dst) in enumerate(
            ((r.x_hbm, x_ref), (r.hg_hbm, hg_ref), (r.wq_hbm, wq_ref), (r.wk_hbm, wk_ref), (r.wv_hbm, wv_ref))
        )
    ] if weights else []
    late_r = late_own if late_own is not None else (late_out if late_out is not None else late_in)
    rows, width = (mg_ref if attention else x_ref).shape
    size = width // HEADS
    lines = plane // 2
    length = rows * plane * PLANES
    half = rows // 2
    z, c = place(plane)
    column, core = c // 2, lax.rem(c, 2)
    group = lax.axis_index("grp")
    lw = width // groups

    def at_group(offset):
        return {"grp": lax.rem(group + offset, groups)}

    to_core = at_core(z, c, plane)
    greet(
        [at_z(z, c, plane, d) for d in range(1, PLANES)]
        + [at_x(z, c, plane, d) for d in range(1, lines)]
        + [to_core]
        + [at_group(d) for d in range(1, groups) if weights]
    )
    sent = []

    def start(copy):
        copy.start()
        sent.append(copy)

    for copy in later:
        copy.start()

    def dcopy(slot, d):
        return remote(
            dpack.at[lax.rem(z + d, PLANES), slot], drecv.at[slot, z],
            zsend.at[slot, d], zrecv.at[slot, d], at_z(z, c, plane, d),
        )

    def key_copy(slot):
        return pltpu.make_async_copy(all_ref.at[slot], keybuf.at[slot % 2], keysem.at[slot % 2])

    for slot in range(SLOTS if attention else 0):
        if slot < 2:
            key_copy(slot).start()
        for to in range(PLANES):
            cols = slice((to * SLOTS + slot) * size, (to * SLOTS + slot + 1) * size)
            dpack[to, slot] = jnp.concatenate([mg_ref[:half, cols], mg_ref[half:, cols]], axis=1)
        for d in (2, 1, 3):
            start(dcopy(slot, d))
        drecv[slot, z] = dpack[z, slot]

    def arrive(slot):
        for d in range(1, PLANES):
            dcopy(slot, d).wait_recv()

    exchange = {}

    def swap(index, src, dst):
        exchange[index] = remote(src, dst, esend.at[index], erecv.at[index], to_core)
        start(exchange[index])

    def arrived(*indices):
        for index in indices:
            copy = exchange.pop(index, None)
            if copy is not None:
                copy.wait_recv()

    if weights:
        swap(0, lt_a.at[:, :, 1 - core], ltp_a)
        swap(1, branch_ref, rp_branch)
        swap(2, lt_n2.at[:, :, 1 - core], ltp_n2)
        swap(3, ug_ref, rp_ug)
        swap(4, lt_act.at[:, :, 1 - core], ltp_act)
        swap(5, dout_ref, rp_dout)
        swap(6, lt_n.at[:, :, 1 - core], ltp_n)

    if attention:
        for k in range(PLANES):
            masks[k] = position_masks(spans_ref, plane, length, c, k, rows).astype(BF16)
        first, end = spans_ref[0, 0], length - spans_ref[0, 1]

    def vectors(value, result):
        stages = [
            (vbuf_y, group, groups, at_group, 2),
            (vbuf_c, core, 2, lambda e: to_core, 0),
            (vbuf_x, column, lines, lambda e: at_x(z, c, plane, e), 1),
            (vbuf_z, z, PLANES, lambda e: at_z(z, c, plane, e), 3),
        ]

        def copies(stage):
            buf, me, count, partner, axis = stages[stage]
            return [
                remote(
                    buf.at[me], buf.at[me],
                    vsend.at[axis, e], vrecv.at[axis, e], partner(e),
                )
                for e in range(1, count)
            ]

        def step(stage):
            if stage == 0:
                total = value()
            else:
                buf, me, count, partner, axis = stages[stage - 1]
                for copy in copies(stage - 1):
                    copy.wait_recv()
                total = buf[0]
                for i in range(1, count):
                    total = total + buf[i]
            if stage == len(stages):
                result[...] = total
                return
            buf, me = stages[stage][:2]
            buf[me] = total
            for copy in copies(stage):
                start(copy)

        return step

    def bufs(piece):
        if piece == VALUE:
            return 0, wbuf_v, gy_v, gx_v, sx_v, sy_v, zs_v, zg_v, fin_v
        return piece, wbuf, gy, gx, sx, sy, zs, zg, fin

    def make(piece):
        i, buf = bufs(piece)[:2]
        count = PLANES * lines * shard
        if piece == OUT:
            arrived(0, 1)
            mine, theirs = lt_a[:, :, core, 0], ltp_a[:, :, 0]
            right, other = branch_ref[...], rp_branch[...]
        elif piece < DOWN:
            arrived(2, 3)
            cols = slice((piece - UP) * width, (piece - UP + 1) * width)
            mine, theirs = lt_n2[:, :, core, 0], ltp_n2[:, :, 0]
            right, other = ug_ref[:, cols], rp_ug[:, cols]
        elif piece < QUERY:
            arrived(4, 5)
            mine, theirs = lt_act[:, :, core, piece - DOWN], ltp_act[:, :, piece - DOWN]
            right, other = dout_ref[...], rp_dout[...]
        else:
            arrived(6, 7)
            at = (piece - QUERY) * width
            cols = slice(at, at + (width // 2 if piece == VALUE else width))
            mine, theirs = lt_n[:, :, core, 0], ltp_n[:, :, 0]
            right, other = late_r[:, cols], rp_late[:, cols]
        grad = dot(mine.reshape(count, rows), right, NN) + dot(theirs.reshape(count, rows), other, NN)
        lanes = grad.shape[1] // groups
        for h in range(groups):
            for zz in range(PLANES):
                for xx in range(lines):
                    at = (zz * lines + xx) * shard
                    buf[i, h, xx, zz] = grad[at : at + shard, h * lanes : (h + 1) * lanes].astype(BF16)
        for copy in first_copies(piece):
            start(copy)

    def first_copies(piece):
        i, buf, gy_b, gx_b = bufs(piece)[:4]
        n = piece
        if piece in LINE_FIRST:
            return [
                remote(
                    buf.at[i, :, lax.rem(column + e, lines)], gx_b.at[i, e - 1],
                    s1send.at[n, e], s1recv.at[n, e], at_x(z, c, plane, e),
                )
                for e in range(1, lines)
            ]
        return [
            remote(
                buf.at[i, lax.rem(group + e, groups)], gy_b.at[i, e - 1],
                s1send.at[n, e], s1recv.at[n, e], at_group(e),
            )
            for e in range(1, groups)
        ]

    def second_copies(piece):
        i, buf, gy_b, gx_b, sx_b, sy_b = bufs(piece)[:6]
        n = piece
        if piece in LINE_FIRST:
            return [
                remote(
                    sy_b.at[i, e - 1], gy_b.at[i, e - 1, 0],
                    s2send.at[n, e], s2recv.at[n, e], at_group(e),
                )
                for e in range(1, groups)
            ]
        return [
            remote(
                sx_b.at[i, e - 1], gx_b.at[i, e - 1, 0],
                s2send.at[n, e], s2recv.at[n, e], at_x(z, c, plane, e),
            )
            for e in range(1, lines)
        ]

    def first_total(piece, at):
        i, buf, gy_b, gx_b = bufs(piece)[:4]
        if piece in LINE_FIRST:
            value = buf[i, at, column].astype(F32)
            for e in range(1, lines):
                value = value + gx_b[i, e - 1, at].astype(F32)
            return value
        value = buf[i, group, at].astype(F32)
        for e in range(1, groups):
            value = value + gy_b[i, e - 1, at].astype(F32)
        return value

    def second(piece):
        i, buf, gy_b, gx_b, sx_b, sy_b = bufs(piece)[:6]
        for copy in first_copies(piece):
            copy.wait_recv()
        if piece in LINE_FIRST:
            for e in range(1, groups):
                sy_b[i, e - 1] = first_total(piece, lax.rem(group + e, groups)).astype(BF16)
        else:
            for e in range(1, lines):
                sx_b[i, e - 1] = first_total(piece, lax.rem(column + e, lines)).astype(BF16)
        for copy in second_copies(piece):
            start(copy)

    def third_copies(piece):
        i = bufs(piece)[0]
        zs_b, zg_b = bufs(piece)[6:8]
        n = piece
        return [
            remote(
                zs_b.at[i, lax.rem(z + d, PLANES)], zg_b.at[i, d - 1],
                wzsend.at[n, d], wzrecv.at[n, d], at_z(z, c, plane, d),
            )
            for d in (2, 1, 3)
        ]

    def third(piece):
        i, buf, gy_b, gx_b, sx_b, sy_b, zs_b, zg_b, fin_b = bufs(piece)
        for copy in second_copies(piece):
            copy.wait_recv()
        value = first_total(piece, group if piece in LINE_FIRST else column)
        if piece in LINE_FIRST:
            for e in range(1, groups):
                value = value + gy_b[i, e - 1, 0].astype(F32)
        else:
            for e in range(1, lines):
                value = value + gx_b[i, e - 1, 0].astype(F32)
        zs_b[i] = value.astype(BF16)
        for copy in third_copies(piece):
            start(copy)

    def last_copies(piece):
        i = bufs(piece)[0]
        fin_b = bufs(piece)[8]
        n = piece
        return [
            remote(fin_b.at[i, group], fin_b.at[i, group], fsend.at[n, e], frecv.at[n, e], at_group(e))
            for e in range(1, groups)
        ]

    def fourth(piece):
        i, buf, gy_b, gx_b, sx_b, sy_b, zs_b, zg_b, fin_b = bufs(piece)
        for copy in third_copies(piece):
            copy.wait_recv()
        value = zs_b[i, z].astype(F32)
        for d in range(1, PLANES):
            value = value + zg_b[i, d - 1].astype(F32)
        fin_b[i, group] = value.astype(BF16)
        for copy in last_copies(piece):
            start(copy)

    def finish(piece):
        for copy in last_copies(piece):
            copy.wait_recv()

    span = min(plane, 4)

    def grads(slot, k):
        held = keybuf.at[slot % 2]
        query = query_rows(held[k, c, rows:, :], True)
        grad = query_rows(drecv[slot, k], False)
        both = jnp.concatenate([query, grad], axis=0)
        turned = jnp.transpose(drecv[slot, k].astype(F32))
        turned = jnp.concatenate([turned[:size], turned[size:]], axis=1)
        delta = jnp.sum(turned * o_ref[slot, k], axis=0, keepdims=True)
        lse = lse_ref[slot, k, 0:1, :]
        query_grad = jnp.zeros((2 * size, rows), F32)
        for k2 in range(k, -1, -1):
            level = lse
            if k2 < k and k == PLANES - 1:
                position = k * plane * rows + c * rows + lax.broadcasted_iota(jnp.int32, (1, rows), 1)
                level = jnp.where(position >= end, -NEG_FILL, lse)
            for at in range(0, plane, span):
                where = slice(at * rows, (at + span) * rows)
                keys = held[k2, at : at + span, :rows, :].reshape(span * rows, 2 * size)
                scores = dot(keys, query, NT)
                prob_grad = dot(keys, grad, NT)
                if k2 == k:
                    scores = scores + masks[k, where, :].astype(F32)
                elif k2 == 0 and at == 0:
                    index = lax.broadcasted_iota(jnp.int32, (span * rows, 1), 0)
                    scores = scores + jnp.where(index < first, NEG_FILL, 0.0)
                prob = jnp.exp(scores - level)
                score_grad = (prob * (prob_grad - delta)).astype(BF16)
                update = dot(jnp.concatenate([score_grad, prob.astype(BF16)], axis=1), both, NN)
                if k2 == k:
                    acc[slot % 2, k2, where] = update
                else:
                    acc[slot % 2, k2, where] += update
                query_grad = query_grad + dot(keys, score_grad, TN)
        packed = jnp.concatenate([query_grad[:size, :half], query_grad[:size, half:]], axis=0)
        ret[k, slot, rows:, :] = jnp.transpose(packed).astype(BF16)

    def mine(slot, k, col):
        return acc[slot % 2, k, pl.ds(pl.multiple_of(col * rows, rows), rows), :]

    def ccopy(slot, line):
        return remote(
            part.at[slot, line], cgot.at[slot, line],
            csend.at[slot, line], crecv.at[slot, line], to_core,
        )

    def xcopy(slot, e):
        return remote(
            xpart.at[slot, e - 1], xgot.at[slot, e - 1],
            xsend.at[slot, e], xrecv.at[slot, e], at_x(z, c, plane, e),
        )

    def rcopy(slot, d):
        return remote(
            ret.at[lax.rem(z + d, PLANES), slot], got.at[slot, z],
            rsend.at[slot, d], rrecv.at[slot, d], at_z(z, c, plane, d),
        )

    def reduce_core(slot):
        for line in range(lines):
            for k in range(PLANES):
                part[slot, line, k] = mine(slot, k, 2 * line + 1 - core).astype(BF16)
            start(ccopy(slot, line))

    def reduce_line(slot):
        for line in range(lines):
            ccopy(slot, line).wait_recv()
        for e in range(1, lines):
            line = lax.rem(column + e, lines)
            for k in range(PLANES):
                xpart[slot, e - 1, k] = (
                    mine(slot, k, 2 * line + core) + cgot[slot, line, k].astype(F32)
                ).astype(BF16)
            start(xcopy(slot, e))

    def reduce_end(slot):
        for e in range(1, lines):
            xcopy(slot, e).wait_recv()
        for k in range(PLANES):
            total = mine(slot, k, c) + cgot[slot, column, k].astype(F32)
            for e in range(1, lines):
                total = total + xgot[slot, e - 1, k].astype(F32)
            ret[k, slot, :rows, :] = total.astype(BF16)
        for d in (2, 1, 3):
            start(rcopy(slot, d))
        got[slot, z] = ret[z, slot]

    def late_factors():
        for slot in range(SLOTS):
            for d in range(1, PLANES):
                rcopy(slot, d).wait_recv()
        for pair in range(HEADS // 2):
            at = pair * 2 * size
            keys, values, queries = [], [], []
            for head in (2 * pair, 2 * pair + 1):
                src, slot = divmod(head, SLOTS)
                block = got[slot, src].astype(F32)
                keys.append(block[:rows, :size])
                values.append(block[:rows, size:])
                queries.append(jnp.concatenate([block[rows:, :size], block[rows:, size:]], axis=0))
            late_r[:, at : at + 2 * size] = (jnp.concatenate(queries, axis=1) * 0.125).astype(BF16)
            late_r[:, width + at : width + at + 2 * size] = jnp.concatenate(keys, axis=1).astype(BF16)
            if pair < HEADS // 4:
                at = 2 * width + at
                late_r[:, at : at + 2 * size] = jnp.concatenate(values, axis=1).astype(BF16)
            else:
                at = at - width // 2
                gfv_ref[:, at : at + 2 * size] = jnp.concatenate(values, axis=1).astype(BF16)
    def input_grad():
        for copy in later:
            copy.wait()
        normed_grad = (
            dot(late_r[:, :width], wq_ref[...], NT)
            + dot(late_r[:, width : 2 * width], wk_ref[...], NT)
            + dot(late_r[:, 2 * width :], wv_ref[...], NT)
        )
        values = x_ref[...].astype(F32)
        centred = values - jnp.mean(values, axis=-1, keepdims=True)
        scale = lax.rsqrt(jnp.mean(centred * centred, axis=-1, keepdims=True) + EPSILON)
        unit = centred * scale
        inner = normed_grad * g_ref[...].reshape(1, width)
        back = scale * (
            inner
            - jnp.mean(inner, axis=-1, keepdims=True)
            - unit * jnp.mean(inner * unit, axis=-1, keepdims=True)
        )
        gin_ref[...] = hg_ref[...] + back

        def sums(v):
            return jnp.sum(v.astype(F32), axis=0, keepdims=True)

        return jnp.concatenate(
            [
                sums(normed_grad * unit),
                sums(normed_grad),
                sums(late_r[:, :width]),
                jnp.concatenate([sums(late_r[:, 2 * width :]), jnp.zeros((1, width // 2), F32)], axis=1),
                jnp.zeros((4, width), F32),
            ],
            axis=0,
        )

    def do(*tasks):
        for stage, what in tasks if weights else ():
            (make, second, third, fourth, finish)[stage - 1](what)

    do(*BEFORE)
    if attention:
        for slot in range(SLOTS):
            key_copy(slot).wait()
            arrive(slot)
            for k in range(PLANES):
                grads(slot, k)
                if slot and k == 1:
                    reduce_line(slot - 1)
                do(*AT_POINTS.get((slot, k), ()))
            if slot == 0:
                key_copy(2).start()
            reduce_core(slot)
            if slot:
                reduce_end(slot - 1)
    else:
        for tasks in AT_POINTS.values():
            do(*tasks)
    do(*AFTER[0])
    if attention:
        reduce_line(SLOTS - 1)
    do(*AFTER[1])
    if attention:
        reduce_end(SLOTS - 1)
    do(*AFTER[2])
    if attention:
        late_factors()
    if weights:
        swap(7, late_r, rp_late)
        partial = input_grad()
        late_vectors = vectors(lambda: jnp.concatenate([vec_ref[...], partial], axis=0), vec1_ref)
        late_vectors(0)
        for stage, tasks in enumerate(AFTER[3:]):
            do(*tasks)
            if stage < 4:
                late_vectors(stage + 1)
    arrived(*range(8))
    for copy in sent:
        copy.wait_send()


BEFORE = ((1, OUT),)
AT_POINTS = {
    (0, 1): ((1, UP + 2), (1, DOWN)),
    (1, 0): ((2, OUT),),
    (1, 1): ((1, DOWN + 3), (2, UP + 2)),
    (1, 2): ((1, UP + 3), (3, OUT), (1, UP)),
    (2, 1): ((2, DOWN + 3), (2, DOWN)),
    (2, 2): ((3, UP + 2),),
}
AFTER = (
    (),
    ((2, UP), (1, UP + 1), (4, OUT), (1, DOWN + 2)),
    ((1, DOWN + 1), (2, UP + 1), (3, DOWN + 3), (2, DOWN + 1), (3, DOWN), (4, UP + 2)),
    ((3, UP + 1), (3, UP), (2, UP + 3), (1, QUERY)),
    ((1, KEY), (3, DOWN + 1)),
    ((4, DOWN), (2, DOWN + 2), (4, UP + 1), (1, VALUE)),
    ((2, QUERY), (3, DOWN + 2), (3, UP + 3)),
    (
        (4, DOWN + 1), (5, UP + 2), (4, DOWN + 3), (2, KEY), (2, VALUE), (3, QUERY), (3, KEY), (3, VALUE), (4, UP),
        (4, UP + 3), (4, DOWN + 2), (4, QUERY), (4, KEY), (4, VALUE), (5, OUT), (5, UP), (5, UP + 1), (5, UP + 3),
        (5, DOWN), (5, DOWN + 1), (5, DOWN + 2), (5, DOWN + 3), (5, QUERY), (5, KEY), (5, VALUE),
    ),
)


def backward_call(plane, groups, rows, width, hidden, attention, weights, arrays):
    blocks = plane * PLANES
    lines = plane // 2
    size = width // HEADS
    half = rows // 2
    shard = width // blocks
    tall = hidden // width
    lw = width // groups
    lv = width // 2 // groups
    late = 2 * width + width // 2
    count = PIECES
    dma = pltpu.SemaphoreType.DMA
    most = max(groups, lines)

    def vmem(*shape):
        return pltpu.VMEM(shape, BF16)

    def vmem32(*shape):
        return pltpu.VMEM(shape, F32)

    any_space = pl.BlockSpec(memory_space=pl.ANY)
    ins = {}
    outs = {}
    scratch = {}
    if attention:
        ins.update(mg_ref=VMEM, all_ref=any_space, o_ref=VMEM, lse_ref=VMEM, spans_ref=SMEM)
        outs.update(gfv_ref=((rows, width // 2), BF16))
        scratch.update(
            dpack=vmem(PLANES, SLOTS, half, 2 * size),
            drecv=vmem(SLOTS, PLANES, half, 2 * size),
            masks=vmem(PLANES, plane * rows, rows),
            acc=vmem32(2, PLANES, plane * rows, 2 * size),
            part=vmem(SLOTS, lines, PLANES, rows, 2 * size),
            cgot=vmem(SLOTS, lines, PLANES, rows, 2 * size),
            xpart=vmem(SLOTS, lines - 1, PLANES, rows, 2 * size),
            xgot=vmem(SLOTS, lines - 1, PLANES, rows, 2 * size),
            ret=vmem(PLANES, SLOTS, rows + half, 2 * size),
            got=vmem(SLOTS, PLANES, rows + half, 2 * size),
            keybuf=vmem(2, PLANES, plane, rows + half, 2 * size),
            keysem=dma((2,)),
            zsend=dma((SLOTS, PLANES)), zrecv=dma((SLOTS, PLANES)),
            csend=dma((SLOTS, lines)), crecv=dma((SLOTS, lines)),
            xsend=dma((SLOTS, lines)), xrecv=dma((SLOTS, lines)),
            rsend=dma((SLOTS, PLANES)), rrecv=dma((SLOTS, PLANES)),
        )
        if weights:
            scratch.update(late_own=vmem(rows, late))
        else:
            outs.update(late_out=((rows, late), BF16))
    if weights:
        ins.update(
            lt_a=VMEM, lt_n2=VMEM, lt_act=VMEM, lt_n=VMEM, branch_ref=VMEM, ug_ref=VMEM, dout_ref=VMEM, vec_ref=VMEM,
            g_ref=VMEM, x_hbm=any_space, hg_hbm=any_space, wq_hbm=any_space, wk_hbm=any_space, wv_hbm=any_space,
        )
        scratch.update(
            x_ref=vmem(rows, width), hg_ref=vmem32(rows, width), lsem=dma((5,)),
            wq_ref=vmem(width, width), wk_ref=vmem(width, width), wv_ref=vmem(width, width // 2),
        )
        if not attention:
            ins.update(late_in=VMEM)
        outs.update(
            gin_ref=((rows, width), F32), vec1_ref=((16, width), F32),
            fin=((count - 1, groups, shard, lw), BF16), fin_v=((1, groups, shard, lv), BF16),
        )
        scratch.update(
            ltp_a=vmem(PLANES, lines, 1, shard, rows),
            ltp_n2=vmem(PLANES, lines, 1, shard, rows),
            ltp_act=vmem(PLANES, lines, tall, shard, rows),
            ltp_n=vmem(PLANES, lines, 1, shard, rows),
            rp_branch=vmem(rows, width), rp_ug=vmem(rows, hidden), rp_dout=vmem(rows, width), rp_late=vmem(rows, late),
            vbuf_c=vmem32(2, 16, width), vbuf_x=vmem32(lines, 16, width),
            vbuf_y=vmem32(groups, 16, width), vbuf_z=vmem32(PLANES, 16, width),
            esend=dma((8,)), erecv=dma((8,)),
            s1send=dma((count, most)), s1recv=dma((count, most)),
            s2send=dma((count, most)), s2recv=dma((count, most)),
            wzsend=dma((count, PLANES)), wzrecv=dma((count, PLANES)),
            fsend=dma((count, groups)), frecv=dma((count, groups)),
            vsend=dma((4, max(most, PLANES))), vrecv=dma((4, max(most, PLANES))),
        )
        for tag, n, lanes in (("", count - 1, lw), ("_v", 1, lv)):
            scratch.update({
                "wbuf" + tag: vmem(n, groups, lines, PLANES, shard, lanes),
                "gy" + tag: vmem(n, groups - 1, lines, PLANES, shard, lanes),
                "gx" + tag: vmem(n, lines - 1, groups if LINE_FIRST else 1, PLANES, shard, lanes),
                "sx" + tag: vmem(n, lines - 1, PLANES, shard, lanes),
                "zs" + tag: vmem(n, PLANES, shard, lanes),
                "zg" + tag: vmem(n, PLANES - 1, shard, lanes),
            })
            if LINE_FIRST:
                scratch["sy" + tag] = vmem(n, groups - 1, PLANES, shard, lanes)
    names = tuple(ins) + tuple(outs) + tuple(scratch)
    result = pl.pallas_call(
        functools.partial(backward_kernel, plane, groups, shard, names, attention, weights),
        name="backward",
        out_shape=tuple(jax.ShapeDtypeStruct(*v) for v in outs.values()),
        in_specs=list(ins.values()),
        out_specs=(VMEM,) * len(outs),
        scratch_shapes=list(scratch.values()),
        compiler_params=pltpu.CompilerParams(
            collective_id=2 if attention else 3, has_side_effects=True, vmem_limit_bytes=61 << 20
        ),
    )(*[arrays[name] for name in ins])
    return dict(zip(outs, result))


def tail_kernel(
    gin_ref, gfv_ref, vec1_ref, fin_ref, finv_ref,
    o_gin, o_gfv, o_g1, o_s1, o_wq, o_bq, o_wk, o_wv, o_bv, o_wo, o_bo, o_g2, o_s2, o_wu, o_bu, o_wd, o_bd,
):
    groups, shard, lanes = fin_ref.shape[1:]
    width = groups * lanes
    tall = o_wd.shape[0] // shard
    o_gin[...] = gin_ref[...]
    o_gfv[...] = gfv_ref[...]

    def put(ref, rows, at, piece):
        for h in range(groups):
            ref[rows, at + h * lanes : at + (h + 1) * lanes] = fin_ref[piece, h].astype(F32)

    everything = slice(0, shard)
    put(o_wo, everything, 0, OUT)
    put(o_wq, everything, 0, QUERY)
    put(o_wk, everything, 0, KEY)
    for i in range(tall):
        put(o_wu, everything, i * width, UP + i)
        put(o_wd, slice(i * shard, (i + 1) * shard), 0, DOWN + i)
    for h in range(groups):
        o_wv[:, h * (lanes // 2) : (h + 1) * (lanes // 2)] = finv_ref[0, h].astype(F32)
    o_g2[...], o_s2[...], o_bo[...], o_bd[...] = vec1_ref[0], vec1_ref[1], vec1_ref[2], vec1_ref[3 + tall]
    for i in range(tall):
        o_bu[i * width : (i + 1) * width] = vec1_ref[3 + i]
    o_g1[...], o_s1[...], o_bq[...] = vec1_ref[8], vec1_ref[9], vec1_ref[10]
    o_bv[...] = vec1_ref[11, : width // 2]


def tail_part(rows, width, hidden, shard, got):
    def out(*shape):
        return jax.ShapeDtypeStruct(shape, F32)

    return pl.pallas_call(
        tail_kernel,
        name="tail",
        out_shape=(
            out(rows, width), jax.ShapeDtypeStruct((rows, width // 2), BF16), out(width), out(width),
            out(shard, width), out(width), out(shard, width), out(shard, width // 2), out(width // 2),
            out(shard, width), out(width), out(width), out(width),
            out(shard, hidden), out(hidden), out(hidden // width * shard, width), out(width),
        ),
        in_specs=[VMEM] * 5,
        out_specs=(VMEM,) * 17,
    )(*got)


def body(
    inputs,
    first_values,
    spans,
    ln1_gain,
    ln1_shift,
    w_query,
    b_query,
    w_key,
    w_value,
    b_value,
    w_out,
    b_out,
    ln2_gain,
    ln2_shift,
    w_up,
    b_up,
    w_down,
    b_down,
    out_grad,
):
    rows, width = inputs.shape
    hidden = w_up.shape[1]
    groups = lax.axis_size("grp")
    plane = lax.axis_size("blk") // PLANES
    attended, normed, all_blocks, mixed, lse = forward_part(
        inputs, first_values, spans, ln1_gain, ln1_shift, w_query, b_query, w_key, w_value, b_value
    )
    result, mixed_grad, hidden_grad, branch_grad, upper_grad, grad_down, vectors, lt_a, lt_n2, lt_act, lt_n = middle_part(
        plane, inputs, attended, normed, spans, out_grad, b_out, ln2_gain, ln2_shift, b_up, b_down, w_out, w_up, w_down
    )
    arrays = dict(
        mg_ref=mixed_grad, all_ref=all_blocks, o_ref=mixed, lse_ref=lse, spans_ref=spans,
        lt_a=lt_a, lt_n2=lt_n2, lt_act=lt_act, lt_n=lt_n,
        branch_ref=branch_grad, ug_ref=upper_grad, dout_ref=grad_down, vec_ref=vectors,
        x_hbm=inputs, g_ref=ln1_gain, hg_hbm=hidden_grad, wq_hbm=w_query, wk_hbm=w_key, wv_hbm=w_value,
    )
    call = functools.partial(backward_call, plane, groups, rows, width, hidden)
    if plane <= 4:
        got = Refs(call(True, True, arrays))
    else:
        got = Refs(call(True, False, arrays))
        arrays.update(late_in=got.late_out)
        got.update(call(False, True, arrays))
    return (result,) + tuple(
        tail_part(
            rows, width, hidden, width // (plane * PLANES),
            (got.gin_ref, got.gfv_ref, got.vec1_ref, got.fin, got.fin_v),
        )
    )


def solution(mesh):
    placed = (
        P(("grp", "blk"), None),
        P(("grp", "blk"), None),
        P("grp", None),
        P(),
        P(),
        P(),
        P(),
        P(),
        P(),
        P(),
        P(),
        P(),
        P(),
        P(),
        P(),
        P(),
        P(),
        P(),
        P(("grp", "blk"), None),
    )
    return jax.shard_map(
        body,
        mesh=mesh,
        in_specs=placed,
        out_specs=(
            P(("grp", "blk"), None),
            P(("grp", "blk"), None),
            P(("grp", "blk"), None),
            P(),
            P(),
            P("blk", None),
            P(),
            P("blk", None),
            P("blk", None),
            P(),
            P("blk", None),
            P(),
            P(),
            P(),
            P("blk", None),
            P(),
            P("blk", None),
            P(),
        ),
        check_vma=False,
    )
```
